128 devices in a mesh: seq: 16 (over z, y), head: 8 (over x, core).
Axes of the slice: x: 4, y: 4, z: 4, core: 2. Of those that a mesh axis runs over, the one named last changes fastest.
Arguments:
- hidden_in: bfloat16 [8192, 768], P('seq'), may hold values from -6 to 6
- cotangent: bfloat16 [8192, 768], P('seq'), may hold values from -6 to 6
- doc_starts: int32 [8192], P('seq'), may hold values from 0 to 1, as said below
- proj_weight: float32 [768, 24, 128], P('seq', 'head'), may hold values from -0.21875 to 0.21875
- step_weight: float32 [768, 24], P('seq', 'head'), may hold values from -0.109375 to 0.109375
- out_weight: float32 [24, 64, 768], P('head', None, 'seq'), may hold values from -0.15625 to 0.15625
- shared_weight: float32 [768, 256], P(('seq', 'head')), may hold values from -0.21875 to 0.21875
- pre_gain: float32 [768], P(('seq', 'head')), may hold values from 0.5 to 1.5
- channel_params: float32 [6, 24, 64], P(None, 'head'), may hold values from -0.5 to 1.5
- head_params: float32 [3, 24], P(None, 'head'), may hold values from -7 to 1.5
- shared_conv: float32 [256, 5], P(('seq', 'head')), may hold values from -0.5 to 0.5
- proj_first: float32 [768, 24, 128], P('seq', 'head'), may hold values from -28 to 28
- proj_second: float32 [768, 24, 128], P('seq', 'head'), may hold values from 1.6384 to 32.768
- step_first: float32 [768, 24], P('seq', 'head'), may hold values from -28 to 28
- step_second: float32 [768, 24], P('seq', 'head'), may hold values from 1.6384 to 32.768
- out_first: float32 [24, 64, 768], P('head', None, 'seq'), may hold values from -28 to 28
- out_second: float32 [24, 64, 768], P('head', None, 'seq'), may hold values from 1.6384 to 32.768
- shared_first: float32 [768, 256], P(('seq', 'head')), may hold values from -28 to 28
- shared_second: float32 [768, 256], P(('seq', 'head')), may hold values from 1.6384 to 32.768
- gain_first: float32 [768], P(('seq', 'head')), may hold values from -28 to 28
- gain_second: float32 [768], P(('seq', 'head')), may hold values from 1.6384 to 32.768
- channel_first: float32 [6, 24, 64], P(None, 'head'), may hold values from -28 to 28
- channel_second: float32 [6, 24, 64], P(None, 'head'), may hold values from 1.6384 to 32.768
- head_first: float32 [3, 24], P(None, 'head'), may hold values from -28 to 28
- head_second: float32 [3, 24], P(None, 'head'), may hold values from 1.6384 to 32.768
- conv_first: float32 [256, 5], P(('seq', 'head')), may hold values from -28 to 28
- conv_second: float32 [256, 5], P(('seq', 'head')), may hold values from 1.6384 to 32.768
Outputs:
- block_out: bfloat16 [8192, 768], P('seq')
- input_grad: float32 [8192, 768], P('seq')
- proj_first_new: float32 [768, 24, 128], P('seq', 'head')
- proj_second_new: float32 [768, 24, 128], P('seq', 'head')
- proj_weight_new: float32 [768, 24, 128], P('seq', 'head')
- step_first_new: float32 [768, 24], P('seq', 'head')
- step_second_new: float32 [768, 24], P('seq', 'head')
- step_weight_new: float32 [768, 24], P('seq', 'head')
- out_first_new: float32 [24, 64, 768], P('head', None, 'seq')
- out_second_new: float32 [24, 64, 768], P('head', None, 'seq')
- out_weight_new: float32 [24, 64, 768], P('head', None, 'seq')
- shared_first_new: float32 [768, 256], P(('seq', 'head'))
- shared_second_new: float32 [768, 256], P(('seq', 'head'))
- shared_weight_new: float32 [768, 256], P(('seq', 'head'))
- gain_first_new: float32 [768], P(('seq', 'head'))
- gain_second_new: float32 [768], P(('seq', 'head'))
- pre_gain_new: float32 [768], P(('seq', 'head'))
- channel_first_new: float32 [6, 24, 64], P(None, 'head')
- channel_second_new: float32 [6, 24, 64], P(None, 'head')
- channel_params_new: float32 [6, 24, 64], P(None, 'head')
- head_first_new: float32 [3, 24], P(None, 'head')
- head_second_new: float32 [3, 24], P(None, 'head')
- head_params_new: float32 [3, 24], P(None, 'head')
- conv_first_new: float32 [256, 5], P(('seq', 'head'))
- conv_second_new: float32 [256, 5], P(('seq', 'head'))
- shared_conv_new: float32 [256, 5], P(('seq', 'head'))
The draws below stay inside these ranges and needn't reach their ends.
Inputs may be any that keep to these rules, and one draw needn't show every extreme that they name: `doc_starts`: 1 marks a document's first position; position 0 starts one, and documents start only at positions that are multiples of 4.
All inputs are finite; a program needn't handle non-finite values.
Results may differ from the reference program's by a relative error of at most 0.012.
Values may be sent and summed in bfloat16 or wider, within the bound.
No kernel may reach another device: no remote copies, remote signals or barrier semaphores. Data moves between devices by JAX's collectives and lax.ppermute only.
A program may use at most 128 MiB of HBM per device.

```python
import math
from functools import partial
import jax
import jax.numpy as jnp
from jax import lax

D = 768
NHEADS = 24
P_SIZE = 64
N = 128
DI = 1536
CONV = 4
Q = 256
STEP = 10
TOK_DEV = 512
SEQLEN = 8192
N_SEQ = 16


def draw_doc_starts(key, part):
    key = jax.random.fold_in(key, 11)
    key_list = jax.random.split(key, 7)
    blocks_dev = TOK_DEV // CONV
    device_count = SEQLEN // TOK_DEV
    half_count = device_count // 2
    first_cut = CONV * jax.random.randint(key_list[0], (), 1, blocks_dev)
    lower_device = jax.random.randint(key_list[1], (), 1, half_count)
    upper_device = jax.random.randint(key_list[2], (), half_count, device_count - 1)
    lower_cut = lower_device * TOK_DEV + CONV * jax.random.randint(key_list[3], (), 1, blocks_dev)
    upper_cut = upper_device * TOK_DEV + CONV * jax.random.randint(key_list[4], (), 1, blocks_dev)
    last_base = SEQLEN - TOK_DEV
    second_cut = last_base + CONV * jax.random.randint(key_list[5], (), 1, blocks_dev)
    third_cut = last_base + CONV * jax.random.randint(key_list[6], (), 1, blocks_dev)
    position = jnp.arange(SEQLEN)
    marked = (position == 0) | (position == first_cut) | (position == lower_cut) | (position == upper_cut)
    marked = marked | (position == second_cut) | (position == third_cut)
    return marked.astype(jnp.int32)


def draw_channel_params(key, part):
    key = jax.random.fold_in(key, 12)
    raw_vals = jax.random.uniform(key, (CONV + 2, NHEADS, P_SIZE), jnp.float32, -0.5, 0.5)
    row_index = jnp.arange(CONV + 2)[:, None, None]
    scale_rows = jnp.where(row_index == CONV, 0.6, 1.0)
    shift_rows = jnp.where(row_index == CONV + 1, 1.0, 0.0)
    return raw_vals * scale_rows + shift_rows


def draw_head_params(key, part):
    key = jax.random.fold_in(key, 13)
    unit_vals = jax.random.uniform(key, (3, NHEADS), jnp.float32, 0.0, 1.0)
    widths_row = jnp.array([3.5, 2.5, 1.0], jnp.float32)[:, None]
    lowest_row = jnp.array([-7.0, -1.0, 0.5], jnp.float32)[:, None]
    return lowest_row + widths_row * unit_vals


def draw_shared_conv(key, part):
    key = jax.random.fold_in(key, 14)
    raw_vals = jax.random.uniform(key, (2 * N, CONV + 1), jnp.float32, -0.5, 0.5)
    column_index = jnp.arange(CONV + 1)[None, :]
    return raw_vals * jnp.where(column_index == CONV, 0.6, 1.0)


def steps_of(rng, extent, cuts, least, top_value):
    gain = 1.0
    for dim, blocks in cuts:
        draws = jax.random.uniform(jax.random.fold_in(jax.random.fold_in(rng, 6), dim), (blocks,), jnp.float32, least / len(cuts), top_value / len(cuts))
        gain = gain * jnp.repeat(jnp.exp(draws), extent[dim] // blocks).reshape((-1,) + (1,) * (len(extent) - 1 - dim))
    return gain


def normal_values(stream_key, shape, deviation, bound, cuts=(), held_as=jnp.bfloat16):
    factor_of = steps_of(stream_key, shape, cuts, -0.22, 0.18) if cuts else 1.0
    result = jax.random.normal(stream_key, shape, jnp.float32) * deviation * factor_of
    return jnp.minimum(jnp.maximum(result, -bound), bound).astype(held_as)


def setup_inputs(seed: int = 0) -> dict:
    streams_of = jax.random.split(jax.random.key(seed), 28)
    return {
        "hidden_in": normal_values(streams_of[0], (SEQLEN, D), 1.0, 6.0, ((0, 16),)),
        "cotangent": normal_values(streams_of[1], (SEQLEN, D), 1.0, 6.0, ((0, 16),)),
        "doc_starts": draw_doc_starts(jax.random.fold_in(streams_of[27], 71), 0),
        "proj_weight": normal_values(streams_of[3], (D, NHEADS, 2 * P_SIZE), D ** -0.5, 0.21875, ((0, 16), (1, 8)), jnp.float32),
        "step_weight": normal_values(streams_of[4], (D, NHEADS), (4 * D) ** -0.5, 0.109375, ((0, 16), (1, 8)), jnp.float32),
        "out_weight": normal_values(streams_of[5], (NHEADS, P_SIZE, D), DI ** -0.5, 0.15625, ((0, 8), (2, 16)), jnp.float32),
        "shared_weight": normal_values(streams_of[6], (D, 2 * N), D ** -0.5, 0.21875, ((0, 128),), jnp.float32),
        "pre_gain": jnp.clip(1.0 + 0.1 * jax.random.normal(streams_of[7], (D,), jnp.float32), 0.5, 1.5),
        "channel_params": draw_channel_params(jax.random.fold_in(streams_of[27], 71), 0),
        "head_params": draw_head_params(jax.random.fold_in(streams_of[27], 71), 0),
        "shared_conv": draw_shared_conv(jax.random.fold_in(streams_of[27], 71), 0),
        "proj_first": normal_values(streams_of[11], (D, NHEADS, 2 * P_SIZE), (0.05 * (TOK_DEV * N_SEQ) ** 0.5), 28.0, ((0, 16), (1, 8)), jnp.float32),
        "proj_second": jnp.clip(jnp.exp(math.log(32.768) - 2.9957323 * jax.random.uniform(streams_of[12], (D, NHEADS, 2 * P_SIZE), jnp.float32) ** steps_of(streams_of[12], (D, NHEADS, 2 * P_SIZE), ((0, 16), (1, 8)), -0.2, 0.2)), 1.6384, 32.768),
        "step_first": normal_values(streams_of[13], (D, NHEADS), (0.05 * (TOK_DEV * N_SEQ) ** 0.5), 28.0, ((0, 16), (1, 8)), jnp.float32),
        "step_second": jnp.clip(jnp.exp(math.log(32.768) - 2.9957323 * jax.random.uniform(streams_of[14], (D, NHEADS), jnp.float32) ** steps_of(streams_of[14], (D, NHEADS), ((0, 16), (1, 8)), -0.2, 0.2)), 1.6384, 32.768),
        "out_first": normal_values(streams_of[15], (NHEADS, P_SIZE, D), (0.05 * (TOK_DEV * N_SEQ) ** 0.5), 28.0, ((0, 8), (2, 16)), jnp.float32),
        "out_second": jnp.clip(jnp.exp(math.log(32.768) - 2.9957323 * jax.random.uniform(streams_of[16], (NHEADS, P_SIZE, D), jnp.float32) ** steps_of(streams_of[16], (NHEADS, P_SIZE, D), ((0, 8), (2, 16)), -0.2, 0.2)), 1.6384, 32.768),
        "shared_first": normal_values(streams_of[17], (D, 2 * N), (0.05 * (TOK_DEV * N_SEQ) ** 0.5), 28.0, ((0, 128),), jnp.float32),
        "shared_second": jnp.clip(jnp.exp(math.log(32.768) - 2.9957323 * jax.random.uniform(streams_of[18], (D, 2 * N), jnp.float32) ** steps_of(streams_of[18], (D, 2 * N), ((0, 128),), -0.2, 0.2)), 1.6384, 32.768),
        "gain_first": normal_values(streams_of[19], (D,), (0.05 * (TOK_DEV * N_SEQ) ** 0.5), 28.0, ((0, 128),), jnp.float32),
        "gain_second": jnp.clip(jnp.exp(math.log(32.768) - 2.9957323 * jax.random.uniform(streams_of[20], (D,), jnp.float32) ** steps_of(streams_of[20], (D,), ((0, 128),), -0.2, 0.2)), 1.6384, 32.768),
        "channel_first": normal_values(streams_of[21], (CONV + 2, NHEADS, P_SIZE), (0.05 * (TOK_DEV * N_SEQ) ** 0.5), 28.0, ((1, 8),), jnp.float32),
        "channel_second": jnp.clip(jnp.exp(math.log(32.768) - 2.9957323 * jax.random.uniform(streams_of[22], (CONV + 2, NHEADS, P_SIZE), jnp.float32) ** steps_of(streams_of[22], (CONV + 2, NHEADS, P_SIZE), ((1, 8),), -0.2, 0.2)), 1.6384, 32.768),
        "head_first": normal_values(streams_of[23], (3, NHEADS), (0.05 * (TOK_DEV * N_SEQ) ** 0.5), 28.0, ((1, 8),), jnp.float32),
        "head_second": jnp.clip(jnp.exp(math.log(32.768) - 2.9957323 * jax.random.uniform(streams_of[24], (3, NHEADS), jnp.float32) ** steps_of(streams_of[24], (3, NHEADS), ((1, 8),), -0.2, 0.2)), 1.6384, 32.768),
        "conv_first": normal_values(streams_of[25], (2 * N, CONV + 1), (0.05 * (TOK_DEV * N_SEQ) ** 0.5), 28.0, ((0, 128),), jnp.float32),
        "conv_second": jnp.clip(jnp.exp(math.log(32.768) - 2.9957323 * jax.random.uniform(streams_of[26], (2 * N, CONV + 1), jnp.float32) ** steps_of(streams_of[26], (2 * N, CONV + 1), ((0, 128),), -0.2, 0.2)), 1.6384, 32.768),
    }


@jax.custom_vjp
def low(v):
    return lax.optimization_barrier(v.astype(jnp.bfloat16)).astype(jnp.float32)

@jax.custom_vjp
def low_back(v):
    return v

def low_keep(v):
    return (low(v), None)

def low_pass(kept, grad):
    return (grad,)

def back_keep(v):
    return (v, None)

def back_low(kept, grad):
    return (low(grad),)
low.defvjp(low_keep, low_pass)
low_back.defvjp(back_keep, back_low)
highest = lax.Precision.HIGHEST
norm_eps = 1e-05
beta_one = 0.9
beta_two = 0.999
adam_eps = 1e-08
decay_rate = 0.01

def conv_masks(starts, conv_width):
    length_all = starts.shape[0]
    phase = jnp.arange(length_all) % conv_width
    first_mark = jnp.repeat(starts.reshape(length_all // conv_width, conv_width)[:, 0], conv_width).astype(jnp.float32)
    return [1.0 - first_mark * (phase < lagging).astype(jnp.float32) for lagging in range(conv_width)]

def group_step(state_now, pieces):
    x_conv, b_mat, c_mat, delta, log_decay, marks = pieces
    segment = jnp.cumsum(marks)
    cum_log = jnp.cumsum(log_decay, axis=0)
    size_q = marks.shape[0]
    lower_tri = jnp.arange(size_q)[:, None] >= jnp.arange(size_q)[None, :]
    joined_mask = (lower_tri & (segment[:, None] == segment[None, :]))[:, :, None]
    differ = cum_log[:, None, :] - cum_log[None, :, :]
    decay_mat = jnp.where(joined_mask, jnp.exp(jnp.where(joined_mask, differ, 0.0)), 0.0)
    scores = jnp.dot(c_mat, b_mat.T, precision=highest)
    mixing = decay_mat * scores[:, :, None] * delta[None, :, :]
    output = jnp.einsum('ijh,jhp->ihp', mixing, x_conv, precision=highest)
    keeper = jnp.exp(cum_log) * (segment == 0).astype(jnp.float32)[:, None]
    output = output + keeper[:, :, None] * jnp.einsum('in,hpn->ihp', c_mat, state_now, precision=highest)
    last_log = cum_log[-1]
    ending = jnp.exp(last_log[None, :] - cum_log) * (segment == segment[-1]).astype(jnp.float32)[:, None]
    summed = jnp.einsum('jh,jhp,jn->hpn', ending * delta, x_conv, b_mat, precision=highest)
    through = jnp.exp(last_log) * (segment[-1] == 0).astype(jnp.float32)
    return (through[:, None, None] * state_now + summed, output)

def forward(hidden, proj_weight, step_weight, out_weight, shared_weight, pre_gain, channel_params, head_params, shared_conv, doc_starts):
    length_all = hidden.shape[0]
    inv_rms = lax.rsqrt(lax.optimization_barrier(jnp.mean(hidden * hidden, axis=1)) + norm_eps)
    normed_low = low(hidden * inv_rms[:, None] * pre_gain[None, :])
    zx_out = low_back(jnp.einsum('td,dhk->thk', normed_low, low(proj_weight), precision=highest))
    delta_raw = low_back(jnp.dot(normed_low, low(step_weight), precision=highest))
    shared_raw = jnp.dot(normed_low, low(shared_weight), precision=highest)
    gate_raw = zx_out[:, :, :P_SIZE]
    x_raw = zx_out[:, :, P_SIZE:]
    values = jnp.concatenate([x_raw.reshape(length_all, DI), shared_raw], axis=1)
    padded = jnp.concatenate([jnp.zeros((CONV - 1, DI + 2 * N), jnp.float32), values], axis=0)
    conv_taps = jnp.concatenate([channel_params[:CONV].reshape(CONV, DI), shared_conv[:, :CONV].T], axis=1)
    biases = jnp.concatenate([channel_params[CONV].reshape(DI), shared_conv[:, CONV]])
    tap_masks = conv_masks(doc_starts, CONV)
    conv_out = biases[None, :] + conv_taps[CONV - 1][None, :] * values
    for lagging in range(1, CONV):
        begin = CONV - 1 - lagging
        conv_out = conv_out + conv_taps[begin][None, :] * padded[begin:begin + length_all] * tap_masks[lagging][:, None]
    active = jax.nn.silu(conv_out)
    x_conv = active[:, :DI].reshape(length_all, NHEADS, P_SIZE)
    b_mat = active[:, DI:DI + N]
    c_mat = active[:, DI + N:]
    delta = jax.nn.softplus(delta_raw + head_params[0][None, :])
    log_decay = -jnp.exp(head_params[1])[None, :] * delta
    blocks = length_all // Q

    def to_blocks(array_in):
        return array_in.reshape((blocks, Q) + array_in.shape[1:])
    pieces = (to_blocks(x_conv), to_blocks(b_mat), to_blocks(c_mat), to_blocks(delta), to_blocks(log_decay), to_blocks(doc_starts))
    state_end, outputs = lax.scan(jax.checkpoint(group_step), jnp.zeros((NHEADS, P_SIZE, N), jnp.float32), pieces)
    y_full = outputs.reshape(length_all, NHEADS, P_SIZE) + head_params[2][None, :, None] * x_conv
    gated = y_full * jax.nn.silu(gate_raw)
    gate_rms = lax.rsqrt(lax.optimization_barrier(jnp.sum(gated * gated, axis=(1, 2))) / DI + norm_eps)
    normed_out = low(gated * gate_rms[:, None, None] * channel_params[CONV + 1][None])
    return hidden + jnp.einsum('thp,hpd->td', normed_out, low(out_weight), precision=highest)

def adam_step(weight, grad_sum, first, second, rate):
    first_new = beta_one * first + (1.0 - beta_one) * grad_sum
    second_new = beta_two * second + (1.0 - beta_two) * grad_sum * grad_sum
    first_hat = first_new / (1.0 - beta_one ** STEP)
    second_hat = second_new / (1.0 - beta_two ** STEP)
    weight_new = weight - rate * (first_hat / (jnp.sqrt(second_hat) + adam_eps) + decay_rate * weight)
    return (first_new, second_new, weight_new)

def reference(hidden_in, cotangent, doc_starts, proj_weight, step_weight, out_weight, shared_weight, pre_gain, channel_params, head_params, shared_conv, proj_first, proj_second, step_first, step_second, out_first, out_second, shared_first, shared_second, gain_first, gain_second, channel_first, channel_second, head_first, head_second, conv_first, conv_second):
    forward_fixed = partial(forward, doc_starts=doc_starts)
    block, pullback = jax.vjp(forward_fixed, hidden_in.astype(jnp.float32), proj_weight, step_weight, out_weight, shared_weight, pre_gain, channel_params, head_params, shared_conv)
    grads = pullback(cotangent.astype(jnp.float32))
    matrix_rate = 1.4 * D ** (-0.5)
    proj_new = adam_step(proj_weight, grads[1], proj_first, proj_second, matrix_rate)
    step_new = adam_step(step_weight, grads[2], step_first, step_second, matrix_rate)
    out_new = adam_step(out_weight, grads[3], out_first, out_second, 1.4 * DI ** (-0.5))
    shared_new = adam_step(shared_weight, grads[4], shared_first, shared_second, matrix_rate)
    gain_new = adam_step(pre_gain, grads[5], gain_first, gain_second, 0.5)
    channel_new = adam_step(channel_params, grads[6], channel_first, channel_second, 0.5)
    head_new = adam_step(head_params, grads[7], head_first, head_second, 1.0)
    conv_new = adam_step(shared_conv, grads[8], conv_first, conv_second, 0.5)
    return (block.astype(jnp.bfloat16), grads[0], proj_new[0], proj_new[1], proj_new[2], step_new[0], step_new[1], step_new[2], out_new[0], out_new[1], out_new[2], shared_new[0], shared_new[1], shared_new[2], gain_new[0], gain_new[1], gain_new[2], channel_new[0], channel_new[1], channel_new[2], head_new[0], head_new[1], head_new[2], conv_new[0], conv_new[1], conv_new[2])
```

```python
import functools

import jax
import jax.numpy as jnp
from jax import lax
from jax.experimental import pallas as pl
from jax.experimental.pallas import tpu as pltpu
from jax.sharding import Mesh
from jax.sharding import PartitionSpec as P

D = 768
DI = 1536
STEP = 10
SEQ = ("seq_0", "seq_1")
HEAD = ("head_0", "head_1")
SEQ_HEAD = SEQ + HEAD
N_SEQ = 16
N_HEAD = 8

T = 512
HALO = 16
NV = 640
NW = 896
MISC = 64
SROWS = 208

f32 = jnp.float32
bf16 = jnp.bfloat16
norm_eps = 1e-05
beta_one = 0.9
beta_two = 0.999
adam_eps = 1e-08
decay_rate = 0.01
LOW = -1e30

PARAMS = pltpu.CompilerParams(vmem_limit_bytes=56 * 1024 * 1024)
VM = pl.BlockSpec(memory_space=pltpu.VMEM)
SM = pl.BlockSpec(memory_space=pltpu.SMEM)


def call(kernel, outs, *args, smem=(), scratch=(), name=None):
    return pl.pallas_call(
        kernel,
        out_shape=[jax.ShapeDtypeStruct(s, d) for s, d in outs],
        in_specs=[SM if i in smem else VM for i in range(len(args))],
        out_specs=[VM] * len(outs),
        scratch_shapes=list(scratch),
        compiler_params=PARAMS,
        name=name,
    )(*args)


def dot(a, b, ca=1, cb=0):
    return lax.dot_general(a, b, (((ca,), (cb,)), ((), ())), preferred_element_type=f32)


def lanes(rows):
    return lax.broadcasted_iota(jnp.int32, (rows, 128), 1)


def half(v):
    return pltpu.roll(v, 64, 1)


def rolled(v, by):
    return pltpu.roll(v, by % 128, 1)


def sig(v):
    return 1.0 / (1.0 + jnp.exp(-v))


def silu(v):
    return v * sig(v)


def dsilu(v):
    s = sig(v)
    return s * (1.0 + v * (1.0 - s))


def gate_pair(t0, t1, t2):
    lo = lanes(t0.shape[0]) < 64
    return jnp.where(lo, t0, half(t1)), jnp.where(lo, t2, 0.0)


def x_pair(t0, t1, t2):
    lo = lanes(t0.shape[0]) < 64
    return jnp.where(lo, half(t0), t1), jnp.where(lo, half(t2), 0.0)


def head_tiles(gate, x):
    lo = lanes(gate[0].shape[0]) < 64
    return (
        jnp.where(lo, gate[0], half(x[0])),
        jnp.where(lo, half(gate[0]), x[0]),
        jnp.where(lo, gate[1], half(x[1])),
    )


def spread(a, at):
    lo = lanes(a.shape[0]) < 64
    return (
        jnp.where(lo, a[:, at : at + 1], a[:, at + 1 : at + 2]),
        jnp.where(lo, a[:, at + 2 : at + 3], 0.0),
    )


def head_sums(pair):
    a, b = pair
    lane = lanes(a.shape[0])
    s0 = jnp.sum(jnp.where(lane < 64, a, 0.0), axis=1, keepdims=True)
    s1 = jnp.sum(jnp.where(lane < 64, 0.0, a), axis=1, keepdims=True)
    s2 = jnp.sum(b, axis=1, keepdims=True)
    return jnp.where(lane == 0, s0, jnp.where(lane == 1, s1, jnp.where(lane == 2, s2, 0.0)))


def pair_of(ref):
    return ref[:, 0:128], ref[:, 128:256]


def head_row(hp_ref, k, rows=1):
    lane = lanes(rows)
    return jnp.where(
        lane == 0,
        hp_ref[k, 0],
        jnp.where(lane == 1, hp_ref[k, 1], jnp.where(lane == 2, hp_ref[k, 2], 0.0)),
    )


def skip_pair(hp_ref):
    lane = lanes(1)
    return (
        jnp.where(lane < 64, hp_ref[2, 0], hp_ref[2, 1]),
        jnp.where(lane < 64, hp_ref[2, 2], 0.0),
    )


def three_parts(v):
    hi = v.astype(bf16).astype(f32)
    rest = v - hi
    mid = rest.astype(bf16).astype(f32)
    return hi + rolled(mid, 3) + rolled(rest - mid, 6)


def joined(v):
    total = v + rolled(v, -3) + rolled(v, -6)
    return jnp.where(lanes(v.shape[0]) < 3, total, 0.0)


def aux_parts(aux):
    return aux


def act_tiles(c_ref):
    return [silu(c_ref[:, 128 * k : 128 * (k + 1)]) for k in range(5)]


def valid_masks(starts_col):
    row = lax.broadcasted_iota(jnp.int32, starts_col.shape, 0)
    one = jnp.where(row < 1, 0.0, pltpu.roll(starts_col, 1, 0))
    two = jnp.where(row < 2, 0.0, pltpu.roll(starts_col, 2, 0))
    first = 1.0 - starts_col
    return first, first - one, first - one - two


def column_of(row_ref):
    return jnp.broadcast_to(row_ref[0:1, :], (128, T)).T


def selector():
    r = lax.broadcasted_iota(jnp.int32, (D, 256), 0)
    k = lax.broadcasted_iota(jnp.int32, (D, 256), 1)
    return jnp.where(r == k + 32 * jnp.right_shift(k, 4), 1.0, 0.0).astype(bf16)


def first_kernel(
    hid_ref, halo_ref, st_ref, w_ref, tap_ref, hp_ref,
    normed_ref, v_ref, c_ref, aux_ref, send_ref, row_ref,
):
    misc_t = w_ref[:, 512:640].astype(f32).T
    gain = misc_t[MISC + 3 : MISC + 4] + misc_t[MISC + 4 : MISC + 5]
    conv_t = dot(misc_t.astype(bf16), selector())
    conv_taps = conv_t[MISC + 5 : MISC + 10] + conv_t[MISC + 10 : MISC + 15]
    row_ref[0:1, :] = gain
    row_ref[1:8, :] = jnp.zeros((7, D), f32)
    for src, at, rows in ((halo_ref, 0, HALO), (hid_ref, HALO, T)):
        h = src[...].astype(f32)
        inv = lax.rsqrt(jnp.mean(h * h, axis=1, keepdims=True) + norm_eps)
        normed_ref[at : at + rows, :] = (h * inv * gain).astype(bf16)
    normed = normed_ref[...]
    v_ref[:, 0:384] = dot(normed, w_ref[:, 0:384])
    v_ref[:, 384:640] = dot(normed, w_ref[:, 640:896])
    raw = half(dot(normed[HALO:], w_ref[:, 512:640]))

    lane = lanes(T)
    pre = raw + head_row(hp_ref, 0)
    delta = jnp.where(
        lane < 3, jnp.maximum(pre, 0.0) + jnp.log1p(jnp.exp(-jnp.abs(pre))), 0.0
    )
    slope = jnp.where(lane < 3, sig(pre), 0.0)
    log_decay = -jnp.exp(head_row(hp_ref, 1)) * delta
    starts = column_of(st_ref)
    parts = three_parts(log_decay) + jnp.where(lane == 9, starts, 0.0)
    ri = lax.broadcasted_iota(jnp.int32, (T, T), 0)
    ci = lax.broadcasted_iota(jnp.int32, (T, T), 1)
    summed = dot(jnp.where(ri >= ci, 1.0, 0.0).astype(bf16), parts.astype(bf16))
    cum = joined(summed)
    segment = summed[:, 9:10]
    last = cum[T - 1 : T, :]
    last_segment = segment[T - 1 : T, :]
    keeper = jnp.where((lane < 3) & (segment == 0.0), jnp.exp(cum), 0.0)
    ending = jnp.where((lane < 3) & (segment == last_segment), jnp.exp(last - cum), 0.0)
    aux_ref[...] = (
        cum
        + rolled(delta, 3)
        + rolled(slope, 6)
        + jnp.where(lane == 9, segment, 0.0)
        + rolled(keeper, 10)
        + rolled(ending, 13)
    )

    valid = valid_masks(starts)
    for k in range(5):
        at = slice(128 * k, 128 * (k + 1))
        if k < 3:
            taps = tap_ref[0:5, at]
        else:
            taps = conv_taps[:, 128 * (k - 3) : 128 * (k - 2)]
        total = taps[4:5] + taps[3:4] * v_ref[HALO:, at]
        for lag in (1, 2, 3):
            total = total + taps[3 - lag : 4 - lag] * (
                v_ref[pl.ds(HALO - lag, T), at] * valid[lag - 1]
            )
        c_ref[:, at] = total

    act = act_tiles(c_ref)
    x = x_pair(*act[:3])
    weight = spread(ending * delta, 0)
    ended = jnp.concatenate([x[0] * weight[0], x[1] * weight[1]], axis=1).astype(bf16)
    state = dot(ended, act[3].astype(bf16), 0, 0)
    through = jnp.where(last_segment == 0.0, jnp.exp(last), 0.0)
    high = through.astype(bf16).astype(f32)
    lower = through - high
    sub = lax.broadcasted_iota(jnp.int32, (16, 128), 0)
    tail = jnp.zeros((16, 128), f32)
    for h in range(3):
        tail = jnp.where(sub == h, high[:, h : h + 1], tail)
        tail = jnp.where(sub == 3 + h, lower[:, h : h + 1], tail)
    body = state[0:192].astype(bf16)
    tail = tail.astype(bf16)
    for q in range(N_SEQ):
        send_ref[q, 0:192, :] = body
        send_ref[q, 192:SROWS, :] = tail


def own_kernel(c_ref, aux_ref, cot_ref, w_ref, hp_ref, y_ref, dn_ref, m_ref, mg_ref):
    act = act_tiles(c_ref)
    x = x_pair(*act[:3])
    aux = aux_ref[...]
    aux_t = aux.T
    scores = dot(act[4].astype(bf16), act[3].astype(bf16), 1, 1)
    ri = lax.broadcasted_iota(jnp.int32, (T, T), 0)
    ci = lax.broadcasted_iota(jnp.int32, (T, T), 1)
    allowed = (ri >= ci) & (aux[:, 9:10] == aux_t[9:10, :])
    mask = jnp.where(allowed, 0.0, LOW)
    delta = spread(aux, 3)
    fed = x[0] * delta[0], x[1] * delta[1]
    lo = lanes(T) < 64
    fed_h = (
        jnp.where(lo, fed[0], 0.0).astype(bf16),
        jnp.where(lo, 0.0, fed[0]).astype(bf16),
        fed[1].astype(bf16),
    )
    skip = skip_pair(hp_ref)
    y = [x[0] * skip[0], x[1] * skip[1]]
    for h in range(3):
        decay = jnp.exp(aux[:, h : h + 1] - aux_t[h : h + 1, :] + mask)
        m_ref[h] = decay.astype(bf16)
        mixing = (decay * scores).astype(bf16)
        mg_ref[h] = mixing
        y[h // 2] = y[h // 2] + dot(mixing, fed_h[h])
    y_ref[:, 0:128] = y[0]
    y_ref[:, 128:256] = y[1]
    back = dot(cot_ref[...], w_ref[:, 384:640])
    dn_ref[:, 0:128] = back[:, 0:128]
    dn_ref[:, 128:256] = jnp.where(lo, back[:, 128:256], 0.0)


def decay_rows(tail, shape=(192, 128)):
    both = tail[0:3] + tail[3:6]
    return jnp.concatenate(
        [jnp.broadcast_to(both[h : h + 1], (64, 128)) for h in range(3)], axis=0
    )


def enter_kernel(
    at_ref, got_ref, y0_ref, dn_ref, c_ref, aux_ref, tap_ref, y_ref, state_ref, stat_ref
):
    here = at_ref[0]
    state = jnp.zeros((192, 128), f32)
    for q in range(N_SEQ - 1):
        through = decay_rows(got_ref[q, 192:SROWS, :].astype(f32))
        merged = through * state + got_ref[q, 0:192, :].astype(f32)
        state = jnp.where(q < here, merged, state)
    state_ref[0:192] = state
    state_ref[192:256] = jnp.zeros((64, 128), f32)
    c_mat = silu(c_ref[:, 512:640]).astype(bf16)
    carried = dot(c_mat, state_ref[...].astype(bf16), 1, 1)
    aux = aux_ref[...]
    keeper = spread(aux, 10)
    gate = gate_pair(*[silu(c_ref[:, 128 * k : 128 * (k + 1)]) for k in range(3)])
    squares = jnp.zeros((T, 1), f32)
    inner = jnp.zeros((T, 1), f32)
    for k in range(2):
        at = slice(128 * k, 128 * (k + 1))
        y = y0_ref[:, at] + keeper[k] * carried[:, at]
        y_ref[:, at] = y
        gated = y * gate[k]
        squares = squares + jnp.sum(gated * gated, axis=1, keepdims=True)
        inner = inner + jnp.sum(
            gated * dn_ref[:, at] * tap_ref[0:1, 384 + 128 * k : 512 + 128 * k],
            axis=1, keepdims=True,
        )
    lane = lanes(T)
    both = jnp.where(lane == 0, squares, jnp.where(lane == 1, inner, 0.0)).T
    for q in range(N_HEAD):
        stat_ref[q] = both[0:8]


def gated_kernel(
    got_ref, y_ref, dn_ref, c_ref, aux_ref, tap_ref,
    dy_ref, dgate_ref, nout_ref, send_ref, rows_ref,
):
    total = got_ref[0]
    for q in range(1, N_HEAD):
        total = total + got_ref[q]
    total = jnp.concatenate([total, jnp.zeros((120, T), f32)], axis=0).T
    rms = lax.rsqrt(total[:, 0:1] / DI + norm_eps)
    coef = rms * rms * rms * total[:, 1:2] / DI
    aux = aux_ref[...]
    keeper = spread(aux, 10)
    raw = gate_pair(*[c_ref[:, 128 * k : 128 * (k + 1)] for k in range(3)])
    x = x_pair(*[silu(c_ref[:, 128 * k : 128 * (k + 1)]) for k in range(3)])
    kept = []
    rows_ref[...] = jnp.zeros_like(rows_ref)
    for k in range(2):
        at = slice(128 * k, 128 * (k + 1))
        gain = tap_ref[0:1, 384 + 128 * k : 512 + 128 * k]
        s = sig(raw[k])
        gate = raw[k] * s
        y = y_ref[:, at]
        gated = y * gate
        dn = dn_ref[:, at]
        scaled = gated * rms
        nout_ref[:, at] = (scaled * gain).astype(bf16)
        d_gated = rms * gain * dn - gated * coef
        dy = d_gated * gate
        dy_ref[:, at] = dy
        dgate_ref[:, at] = d_gated * y * s * (1.0 + raw[k] * (1.0 - s))
        kept.append((dy * keeper[k]).astype(bf16))
        rows_ref[0:1, at] = jnp.sum(dn * scaled, axis=0, keepdims=True)
        rows_ref[1:2, at] = jnp.sum(dy * x[k], axis=0, keepdims=True)
    c_mat = silu(c_ref[:, 512:640]).astype(bf16)
    adj = dot(jnp.concatenate(kept, axis=1), c_mat, 0, 0)[0:192].astype(bf16)
    for q in range(N_SEQ):
        send_ref[q] = adj


def out_kernel(nout_ref, w_ref, out_ref):
    lo = lanes(T) < 64
    a = nout_ref[...]
    del lo
    res = dot(a, w_ref[:, 384:640], 1, 1)
    out_ref[...] = res.astype(bf16)


def own_back_kernel(
    dy_ref, y_ref, y0_ref, c_ref, aux_ref, m_ref, mg_ref, state_ref,
    dx_ref, db_ref, dc_ref, dcum_ref,
):
    aux = aux_ref[...]
    aux_t = aux.T
    act = act_tiles(c_ref)
    x = x_pair(*act[:3])
    b_low, c_low = act[3].astype(bf16), act[4].astype(bf16)
    dy = pair_of(dy_ref)
    lo = lanes(T) < 64
    dy_h = (
        jnp.where(lo, dy[0], 0.0).astype(bf16),
        jnp.where(lo, 0.0, dy[0]).astype(bf16),
        dy[1].astype(bf16),
    )
    x_low = x[0].astype(bf16), x[1].astype(bf16)
    lane = lanes(T)
    dx = [jnp.zeros((T, 128), f32), jnp.zeros((T, 128), f32)]
    spread_sum = jnp.zeros((T, T), f32)
    rows = jnp.zeros((T, 128), f32)
    cols = jnp.zeros((128, T), f32)
    sub = lax.broadcasted_iota(jnp.int32, (128, T), 0)
    for h in range(3):
        pairs = dot(dy_h[h], x_low[h // 2], 1, 1) * aux_t[3 + h : 4 + h, :]
        mixing = mg_ref[h]
        spread_sum = spread_sum + pairs * m_ref[h].astype(f32)
        weights = pairs * mixing.astype(f32)
        rows = jnp.where(lane == h, jnp.sum(weights, axis=1, keepdims=True), rows)
        cols = jnp.where(sub == h, jnp.sum(weights, axis=0, keepdims=True), cols)
        dx[h // 2] = dx[h // 2] + dot(mixing, dy_h[h], 0, 0)
    low = spread_sum.astype(bf16)
    keeper = spread(aux, 10)
    kept = jnp.concatenate([dy[0] * keeper[0], dy[1] * keeper[1]], axis=1).astype(bf16)
    dc_ref[...] = dot(low, b_low) + dot(kept, state_ref[...].astype(bf16))
    db_ref[...] = dot(low, c_low, 0, 0)
    dx_ref[:, 0:128] = dx[0]
    dx_ref[:, 128:256] = dx[1]
    carried = [
        dy[k] * (y_ref[:, 128 * k : 128 * (k + 1)] - y0_ref[:, 128 * k : 128 * (k + 1)])
        for k in range(2)
    ]
    dcum_ref[...] = rows - cols.T + head_sums(carried)


def back_kernel(
    at_ref, got_ref, fwd_ref, state_ref, dx_ref, db_ref, dc_ref, dcum_ref, c_ref, aux_ref,
    v_ref, tap_ref, hp_ref, st_ref, dy_ref, dgate_ref, w_ref, rows_ref, hid_ref, halo_ref,
    dv_ref, dstep_ref, dnorm_ref, edge_ref, chan_ref, conv_ref, gain_ref,
    pad_ref, big_ref,
):
    here = at_ref[0]
    adj = jnp.zeros((192, 128), f32)
    for q in range(N_SEQ - 1, 0, -1):
        through = decay_rows(fwd_ref[q, 192:SROWS, :].astype(f32))
        merged = through * adj + got_ref[q].astype(f32)
        adj = jnp.where(q > here, merged, adj)
    aux = aux_ref[...]
    lane = lanes(T)
    conv = [c_ref[:, 128 * k : 128 * (k + 1)] for k in range(5)]
    sigs = [sig(v) for v in conv]
    x = x_pair(*[conv[k] * sigs[k] for k in range(3)])
    b_low = (conv[3] * sigs[3]).astype(bf16)
    delta, ending = spread(aux, 3), spread(aux, 13)
    adj_low = jnp.concatenate([adj, jnp.zeros((64, 128), f32)], axis=0).astype(bf16)
    through_b = dot(b_low, adj_low, 1, 1)
    skip = skip_pair(hp_ref)
    dy = pair_of(dy_ref)
    ended, extra, full, d_x = [], [], [], []
    for k in range(2):
        at = slice(128 * k, 128 * (k + 1))
        late = ending[k] * through_b[:, at]
        total = dx_ref[:, at] + late
        d_x.append(delta[k] * total + skip[k] * dy[k])
        full.append(x[k] * total)
        extra.append(x[k] * late)
        ended.append(x[k] * delta[k] * ending[k])
    d_b = db_ref[...] + dot(jnp.concatenate(ended, axis=1).astype(bf16), adj_low)
    d_delta = head_sums(full)
    tail = head_sums(extra) * rolled(aux, -3)
    tail = jnp.where(lane < 3, tail, 0.0)
    d_cum = dcum_ref[...] - tail
    ri = lax.broadcasted_iota(jnp.int32, (T, T), 0)
    ci = lax.broadcasted_iota(jnp.int32, (T, T), 1)
    upper = jnp.where(ci >= ri, 1.0, 0.0).astype(bf16)
    d_log = joined(dot(upper, three_parts(d_cum).astype(bf16)))
    own = decay_rows(fwd_ref[here, 192:SROWS, :].astype(f32))
    met = own * adj * state_ref[0:192]
    lane1 = lanes(1)
    meets = jnp.zeros((1, 128), f32)
    for h in range(3):
        meets = jnp.where(lane1 == h, jnp.sum(met[64 * h : 64 * h + 64]), meets)
    d_log = d_log + jnp.sum(tail, axis=0, keepdims=True) + meets
    d_log = jnp.where(lane < 3, d_log, 0.0)
    rate = jnp.exp(head_row(hp_ref, 1))
    d_raw = (d_delta - rate * d_log) * rolled(aux, -6)
    d_raw = jnp.where(lane < 3, d_raw, 0.0)
    delta_cols = jnp.where(lane < 3, rolled(aux, -3), 0.0)
    step_low = half(d_raw).astype(bf16)
    dstep_ref[...] = step_low

    d_gate = pair_of(dgate_ref)
    x_tiles = head_tiles((jnp.zeros_like(d_x[0]),) * 2, d_x)
    gate_tiles = head_tiles(d_gate, (jnp.zeros_like(d_x[0]),) * 2)
    lo = lane < 64
    conv_t = dot(w_ref[:, 512:640].astype(f32).T.astype(bf16), selector())
    conv_taps = conv_t[MISC + 5 : MISC + 10] + conv_t[MISC + 10 : MISC + 15]
    starts = column_of(st_ref)
    valid = valid_masks(starts)
    pad_ref[0:HALO] = jnp.zeros((HALO, 128), f32)
    pad_ref[HALO + T :] = jnp.zeros((HALO, 128), f32)
    tap_rows = []
    for k in range(5):
        at = slice(128 * k, 128 * (k + 1))
        slope = sigs[k] * (1.0 + conv[k] * (1.0 - sigs[k]))
        if k < 3:
            d_conv = jnp.where(lo, gate_tiles[k], x_tiles[k] * slope)
            taps = tap_ref[0:5, at]
        else:
            d_conv = (d_b if k == 3 else dc_ref[...]) * slope
            taps = conv_taps[:, 128 * (k - 3) : 128 * (k - 2)]
        sums = [None, None, None, None, jnp.sum(d_conv, axis=0, keepdims=True)]
        sums[3] = jnp.sum(d_conv * v_ref[HALO:, at], axis=0, keepdims=True)
        pad_ref[HALO : HALO + T] = taps[3:4] * d_conv
        acc = pad_ref[0 : HALO + T]
        for lag in (1, 2, 3):
            masked = d_conv * valid[lag - 1]
            sums[3 - lag] = jnp.sum(
                masked * v_ref[pl.ds(HALO - lag, T), at], axis=0, keepdims=True
            )
            pad_ref[HALO : HALO + T] = taps[3 - lag : 4 - lag] * masked
            acc = acc + pad_ref[pl.ds(lag, HALO + T)]
        dv_ref[:, at] = acc.astype(bf16)
        tap_rows.append(sums)

    chan_ref_rows = []
    for j in range(5):
        pair = x_pair(*[tap_rows[k][j] for k in range(3)])
        chan_ref_rows.append(jnp.concatenate(pair, axis=1))
    chan_ref_rows.append(rows_ref[0:1, :])
    h0 = jnp.sum(d_raw, axis=0, keepdims=True)
    h1 = jnp.sum(d_log * (-rate) * delta_cols, axis=0, keepdims=True)
    h2 = head_sums((rows_ref[1:2, 0:128], rows_ref[1:2, 128:256]))
    zero = jnp.zeros((1, 128), f32)
    for r in (h0, h1, h2):
        chan_ref_rows.append(jnp.concatenate([r, zero], axis=1))
    for j, r in enumerate(chan_ref_rows):
        big_ref[j : j + 1, :] = r
    big_ref[9:16, :] = jnp.zeros((7, 256), f32)
    for q in range(N_SEQ):
        chan_ref[q] = big_ref[...]
    for j in range(5):
        conv_ref[j : j + 1, :] = jnp.concatenate([tap_rows[3][j], tap_rows[4][j]], axis=1)
    conv_ref[5:8, :] = jnp.zeros((3, 256), f32)

    d_norm = dot(dv_ref[:, 0:384], w_ref[:, 0:384], 1, 1)
    d_norm = d_norm + dot(dv_ref[:, 384:640], w_ref[:, 640:896], 1, 1)
    main = d_norm[HALO:] + dot(step_low, w_ref[:, 512:640], 1, 1)
    dnorm_ref[...] = main.astype(bf16)
    edge_ref[...] = d_norm[0:HALO].astype(bf16)
    total = jnp.zeros((1, D), f32)
    for src, val in ((halo_ref, d_norm[0:HALO]), (hid_ref, main)):
        h = src[...].astype(f32)
        inv = lax.rsqrt(jnp.mean(h * h, axis=1, keepdims=True) + norm_eps)
        total = total + jnp.sum(val * (h * inv), axis=0, keepdims=True)
    gain_ref[0:1] = total
    gain_ref[1:8] = jnp.zeros((7, D), f32)


def grad_kernel(normed_ref, dv_ref, dstep_ref, nout_ref, cot_ref, conv_ref, gain_ref, out_ref):
    normed = normed_ref[...]
    out_ref[:, 0:384] = dot(normed, dv_ref[:, 0:384], 0, 0).astype(bf16)
    out_ref[:, 640:896] = dot(normed, dv_ref[:, 384:640], 0, 0).astype(bf16)
    outs = dot(cot_ref[...], nout_ref[...], 0, 0)
    out_ref[:, 384:512] = outs[:, 0:128].astype(bf16)
    tile = outs[:, 128:256] + dot(normed_ref[HALO:, :], dstep_ref[...], 0, 0)
    grads = jnp.concatenate([jnp.zeros((MISC + 5, 256), f32), conv_ref[0:5, :]], axis=0)
    grads = jnp.concatenate([grads, jnp.zeros((128 - MISC - 10, 256), f32)], axis=0)
    high = grads.astype(bf16)
    lower = (grads - high.astype(f32)).astype(bf16)
    sel = selector()
    tile = tile + dot(sel, high, 1, 1) + pltpu.roll(dot(sel, lower, 1, 1), 5, 1)
    gain = gain_ref[0:1]
    gain_high = gain.astype(bf16).astype(f32)
    sub = lax.broadcasted_iota(jnp.int32, (128, D), 0)
    column = jnp.where(
        sub == MISC + 3, gain_high, jnp.where(sub == MISC + 4, gain - gain_high, 0.0)
    ).T
    out_ref[:, 512:640] = (tile + column).astype(bf16)


def sum_kernel(got_ref, out_ref):
    total = got_ref[0].astype(f32)
    for q in range(1, N_HEAD):
        total = total + got_ref[q].astype(f32)
    total = total.astype(bf16)
    for q in range(N_HEAD):
        out_ref[q] = total


def block_sum_kernel(at_ref, got_ref, hid_ref, out_ref):
    start = pl.multiple_of(at_ref[1] * (T // N_HEAD), T // N_HEAD)
    total = hid_ref[pl.ds(start, T // N_HEAD), :].astype(f32)
    for q in range(N_HEAD):
        total = total + got_ref[q].astype(f32)
    total = total.astype(bf16)
    for q in range(N_HEAD):
        out_ref[q] = total


def input_kernel(sum_ref, hid_ref, cot_ref, row_ref, out_ref):
    h = hid_ref[...].astype(f32)
    inv = lax.rsqrt(jnp.mean(h * h, axis=1, keepdims=True) + norm_eps)
    d_scaled = sum_ref[...].astype(f32) * row_ref[0:1, :]
    inner = jnp.sum(d_scaled * h, axis=1, keepdims=True)
    out_ref[...] = (
        cot_ref[...].astype(f32) + inv * d_scaled - h * (inv * inv * inv * inner / D)
    )


def adam(weight, grad, first, second, rate):
    first_new = beta_one * first + (1.0 - beta_one) * grad
    second_new = beta_two * second + (1.0 - beta_two) * grad * grad
    first_hat = first_new / (1.0 - beta_one**STEP)
    second_hat = second_new / (1.0 - beta_two**STEP)
    weight_new = weight - rate * (
        first_hat / (jnp.sqrt(second_hat) + adam_eps) + decay_rate * weight
    )
    return first_new, second_new, weight_new


RATE_D = 1.4 * D ** (-0.5)
RATE_I = 1.4 * DI ** (-0.5)


def put(refs, at, values):
    for ref, value in zip(refs, values):
        ref[at] = value


def update_kernel(*refs):
    (grad_ref, chan_ref), refs = refs[:2], refs[2:]
    proj, step, out, chan, head = (refs[3 * k : 3 * k + 3] for k in range(5))
    outs = refs[15:]
    proj_o, step_o, out_o, chan_o, head_o = (outs[3 * k : 3 * k + 3] for k in range(5))
    rest_ref = outs[15]
    total = grad_ref[0].astype(f32)
    for q in range(1, N_SEQ):
        total = total + grad_ref[q].astype(f32)
    misc = total[:, 512:640]
    rest_ref[...] = jnp.zeros_like(rest_ref)
    for h in range(N_HEAD):
        rest_ref[h, 0:6, 0:256] = total[6 * h : 6 * h + 6, 640:896]
        rest_ref[h, 0:6, 256:384] = misc[6 * h : 6 * h + 6]
        rest_ref[h, 0:2, 384:512] = misc[2 * h : 2 * h + 2]
    for h in range(3):
        at = (slice(None), h, slice(None))
        w, m, v = (r[at] for r in proj)
        put(proj_o, at, adam(w, total[:, 128 * h : 128 * (h + 1)], m, v, RATE_D))
    at = (slice(None), slice(None))
    w, m, v = (r[at] for r in step)
    put(step_o, at, adam(w, half(misc)[:, 0:3], m, v, RATE_D))
    filled = jnp.concatenate([total[:, 384:640], jnp.zeros((80, 256), f32)], axis=0).T
    for h in range(3):
        w, m, v = (r[h] for r in out)
        put(out_o, h, adam(w, filled[64 * h : 64 * h + 64, 0:48], m, v, RATE_I))
    sums = chan_ref[0]
    for q in range(1, N_SEQ):
        sums = sums + chan_ref[q]
    for h in range(3):
        piece = sums[0:6, 128 * (h // 2) : 128 * (h // 2) + 128]
        if h == 1:
            piece = half(piece)
        at = (slice(None), h, slice(None))
        w, m, v = (r[at] for r in chan)
        put(chan_o, at, adam(w, piece[:, 0:64], m, v, 0.5))
    at = (slice(None), slice(None))
    w, m, v = (r[at] for r in head)
    put(head_o, at, adam(w, sums[6:9, 0:3], m, v, 1.0))


def rest_kernel(*refs):
    got_ref, refs = refs[0], refs[1:]
    shared, gain, conv = (refs[3 * k : 3 * k + 3] for k in range(3))
    outs = refs[9:]
    shared_o, gain_o, conv_o = (outs[3 * k : 3 * k + 3] for k in range(3))
    total = got_ref[0]
    for q in range(1, N_HEAD):
        total = total + got_ref[q]
    at = (slice(None), slice(None))
    w, m, v = (r[at] for r in shared)
    put(shared_o, at, adam(w, total[0:6, 0:256], m, v, RATE_D))
    column = total[:, 256 + MISC + 3 : 256 + MISC + 4] + total[:, 256 + MISC + 4 : 256 + MISC + 5]
    sub = lax.broadcasted_iota(jnp.int32, (8, 128), 0)
    row = jnp.sum(jnp.where(sub == lanes(8), column, 0.0), axis=0, keepdims=True)
    w, m, v = (r[at] for r in gain)
    put(gain_o, at, adam(w, row[:, 0:6], m, v, 0.5))
    tile = total[0:2, 384:512]
    both = rolled(tile, -(MISC + 5)) + rolled(tile, -(MISC + 10))
    w, m, v = (r[at] for r in conv)
    put(conv_o, at, adam(w, both[:, 0:5], m, v, 0.5))


def two_parts(a):
    high = lax.reduce_precision(a, 8, 7)
    return high.astype(bf16), (a - high).astype(bf16)


def exchange(blocks, axis):
    return lax.all_to_all(blocks, axis, 0, 0, tiled=True)


def shifted(a, by):
    pairs = [(i, i + by) for i in range(N_SEQ) if 0 <= i + by < N_SEQ]
    return lax.ppermute(a, SEQ, pairs)


def body(
    hidden_in, cotangent, doc_starts, proj_weight, step_weight, out_weight, shared_weight,
    pre_gain, channel_params, head_params, shared_conv, proj_first, proj_second, step_first,
    step_second, out_first, out_second, shared_first, shared_second, gain_first, gain_second,
    channel_first, channel_second, head_first, head_second, conv_first, conv_second,
):
    where = jnp.stack([lax.axis_index(SEQ), lax.axis_index(HEAD)]).astype(jnp.int32)
    halo = shifted(hidden_in[T - HALO :], 1)

    small = jnp.concatenate(
        [*two_parts(pre_gain), *(p.reshape(10) for p in two_parts(shared_conv))]
    )
    small = jnp.concatenate(
        [shared_weight.astype(bf16), jnp.pad(small, (0, 224))[None], jnp.zeros((1, 256), bf16)]
    )
    got = exchange(jnp.broadcast_to(small, (N_HEAD, 8, 256)), HEAD)
    line = got[:, 6]
    gain_cols = [line[:, 0:6].reshape(48, 1), line[:, 6:12].reshape(48, 1)]
    conv_cols = jnp.concatenate(
        [line[:, 12:22].reshape(16, 5), line[:, 22:32].reshape(16, 5)], axis=1
    )
    misc = jnp.concatenate(
        [step_weight.astype(bf16), *gain_cols, jnp.pad(conv_cols, ((0, 32), (0, 0)))], axis=1
    )
    pack = jnp.concatenate(
        [
            proj_weight.astype(bf16).reshape(48, 384),
            out_weight.astype(bf16).reshape(192, 48).T,
            jnp.pad(misc, ((0, 0), (0, 49))),
            got[:, 0:6].reshape(48, 256),
        ],
        axis=1,
    )
    weights = exchange(jnp.broadcast_to(pack, (N_SEQ, 48, NW)), SEQ).reshape(D, NW)

    marks = doc_starts.astype(f32).reshape(1, T)
    fixed = jnp.broadcast_to(
        (jnp.arange(6) == 3).astype(f32)[:, None, None], channel_params.shape
    )
    taps = jnp.concatenate([fixed, channel_params], axis=2).reshape(6, 384)
    gains = jnp.pad(channel_params[5].reshape(1, 192), ((0, 5), (0, 64)))
    taps = jnp.pad(jnp.concatenate([taps, gains], axis=1), ((0, 2), (0, 0)))

    normed, values, conv, aux, sent, row = call(
        first_kernel,
        [
            ((HALO + T, D), bf16), ((HALO + T, NV), f32), ((T, NV), f32), ((T, 128), f32),
            ((N_SEQ, SROWS, 128), bf16), ((8, D), f32),
        ],
        hidden_in, halo, marks, weights, taps, head_params, smem=(5,), name="first",
    )
    states = exchange(sent, SEQ)
    y_own, d_normed, decays, mixing = call(
        own_kernel,
        [((T, 256), f32), ((T, 256), f32), ((3, T, T), bf16), ((3, T, T), bf16)],
        conv, aux, cotangent, weights, head_params, smem=(4,), name="own",
    )
    y_full, state, stat = call(
        enter_kernel,
        [((T, 256), f32), ((256, 128), f32), ((N_HEAD, 8, T), f32)],
        where, states, y_own, d_normed, conv, aux, taps, smem=(0,), name="enter",
    )
    stats = exchange(stat, HEAD)
    d_y, d_gate, normed_out, sent_adj, rows = call(
        gated_kernel,
        [
            ((T, 256), f32), ((T, 256), f32), ((T, 256), bf16),
            ((N_SEQ, 192, 128), bf16), ((8, 256), f32),
        ],
        stats, y_full, d_normed, conv, aux, taps, name="gated",
    )
    adjoints = exchange(sent_adj, SEQ)
    (partial_out,) = call(out_kernel, [((T, D), bf16)], normed_out, weights, name="out")
    own_out = exchange(partial_out.reshape(N_HEAD, T // N_HEAD, D), HEAD)
    d_x, d_b, d_c, d_cum = call(
        own_back_kernel,
        [((T, 256), f32), ((T, 128), f32), ((T, 128), f32), ((T, 128), f32)],
        d_y, y_full, y_own, conv, aux, decays, mixing, state, name="own_back",
    )
    (sums,) = call(
        block_sum_kernel, [((N_HEAD, T // N_HEAD, D), bf16)],
        where, own_out, hidden_in, smem=(0,), name="block_sum",
    )
    block_out = exchange(sums, HEAD).reshape(T, D)
    d_values, d_step, d_norm, edge, chan, d_conv, d_gain = call(
        back_kernel,
        [
            ((HALO + T, NV), bf16), ((T, 128), bf16), ((T, D), bf16), ((HALO, D), bf16),
            ((N_SEQ, 16, 256), f32), ((8, 256), f32), ((8, D), f32),
        ],
        where, adjoints, states, state, d_x, d_b, d_c, d_cum, conv, aux,
        values, taps, head_params, marks, d_y, d_gate, weights, rows, hidden_in, halo,
        smem=(0, 12),
        scratch=[pltpu.VMEM((T + 2 * HALO, 128), f32), pltpu.VMEM((16, 256), f32)],
        name="back",
    )
    edge = shifted(edge, -1)
    chans = exchange(chan, SEQ)
    (grads,) = call(
        grad_kernel, [((D, NW), bf16)],
        normed, d_values, d_step, normed_out, cotangent, d_conv, d_gain, name="grad",
    )
    grads = exchange(grads.reshape(N_SEQ, 48, NW), SEQ)
    d_norm = jnp.concatenate([d_norm[: T - HALO], d_norm[T - HALO :] + edge], axis=0)
    d_norm = exchange(d_norm.reshape(N_HEAD, T // N_HEAD, D), HEAD)
    (sums,) = call(sum_kernel, [((N_HEAD, T // N_HEAD, D), bf16)], d_norm, name="sum")
    d_norm = exchange(sums, HEAD).reshape(T, D)

    proj, step, out = (48, 3, 128), (48, 3), (3, 64, 48)
    shapes = [proj] * 3 + [step] * 3 + [out] * 3 + [(6, 3, 64)] * 3 + [(3, 3)] * 3
    updated = call(
        update_kernel,
        [(s, f32) for s in shapes] + [((N_HEAD, 8, 512), f32)],
        grads, chans, proj_weight, proj_first, proj_second, step_weight, step_first,
        step_second, out_weight, out_first, out_second, channel_params, channel_first,
        channel_second, head_params, head_first, head_second, name="update",
    )
    rest = exchange(updated[15], HEAD)
    (input_grad,) = call(
        input_kernel, [((T, D), f32)], d_norm, hidden_in, cotangent, row, name="input",
    )
    shared = call(
        rest_kernel,
        [(s, f32) for s in [(6, 256)] * 3 + [(1, 6)] * 3 + [(2, 5)] * 3],
        rest, shared_weight, shared_first, shared_second, pre_gain.reshape(1, 6),
        gain_first.reshape(1, 6), gain_second.reshape(1, 6), shared_conv, conv_first,
        conv_second, name="rest",
    )
    gain_new = [g.reshape(6) for g in shared[3:6]]
    return (
        block_out, input_grad, *updated[0:9], *shared[0:3], *gain_new, *updated[9:15],
        *shared[6:9],
    )


def solution(mesh):
    finer = Mesh(mesh.devices.reshape(4, 4, 4, 2), SEQ_HEAD)
    matrix = P(SEQ, HEAD, None)
    step = P(SEQ, HEAD)
    out = P(HEAD, None, SEQ)
    both = P(SEQ_HEAD, None)
    gain = P(SEQ_HEAD)
    channel = P(None, HEAD, None)
    head = P(None, HEAD)
    tokens = P(SEQ, None)
    return jax.shard_map(
        body,
        mesh=finer,
        in_specs=(
            tokens, tokens, P(SEQ), matrix, step, out, both, gain, channel, head, both,
            matrix, matrix, step, step, out, out, both, both, gain, gain, channel, channel,
            head, head, both, both,
        ),
        out_specs=(
            (tokens, tokens)
            + (matrix,) * 3 + (step,) * 3 + (out,) * 3 + (both,) * 3 + (gain,) * 3
            + (channel,) * 3 + (head,) * 3 + (both,) * 3
        ),
        check_vma=False,
    )
```

```python
import functools

import jax
import jax.numpy as jnp
from jax import lax
from jax.experimental import pallas as pl
from jax.experimental.pallas import tpu as pltpu
from jax.sharding import Mesh
from jax.sharding import PartitionSpec as P

D = 768
DI = 1536
STEP = 10
SEQ = ("seq_0", "seq_1")
HEAD = ("head_0", "head_1")
SEQ_HEAD = SEQ + HEAD
N_SEQ = 16
N_HEAD = 8

T = 512
HALO = 16
NV = 640
NW = 896
MISC = 64
SROWS = 208

f32 = jnp.float32
bf16 = jnp.bfloat16
norm_eps = 1e-05
beta_one = 0.9
beta_two = 0.999
adam_eps = 1e-08
decay_rate = 0.01
LOW = -1e30

PARAMS = pltpu.CompilerParams(vmem_limit_bytes=56 * 1024 * 1024)
VM = pl.BlockSpec(memory_space=pltpu.VMEM)
SM = pl.BlockSpec(memory_space=pltpu.SMEM)


def call(kernel, outs, *args, smem=(), scratch=(), name=None):
    return pl.pallas_call(
        kernel,
        out_shape=[jax.ShapeDtypeStruct(s, d) for s, d in outs],
        in_specs=[SM if i in smem else VM for i in range(len(args))],
        out_specs=[VM] * len(outs),
        scratch_shapes=list(scratch),
        compiler_params=PARAMS,
        name=name,
    )(*args)


def dot(a, b, ca=1, cb=0):
    return lax.dot_general(a, b, (((ca,), (cb,)), ((), ())), preferred_element_type=f32)


def lanes(rows):
    return lax.broadcasted_iota(jnp.int32, (rows, 128), 1)


def half(v):
    return pltpu.roll(v, 64, 1)


def rolled(v, by):
    return pltpu.roll(v, by % 128, 1)


def sig(v):
    return 1.0 / (1.0 + jnp.exp(-v))


def silu(v):
    return v * sig(v)


def dsilu(v):
    s = sig(v)
    return s * (1.0 + v * (1.0 - s))


def gate_pair(t0, t1, t2):
    lo = lanes(t0.shape[0]) < 64
    return jnp.where(lo, t0, half(t1)), jnp.where(lo, t2, 0.0)


def x_pair(t0, t1, t2):
    lo = lanes(t0.shape[0]) < 64
    return jnp.where(lo, half(t0), t1), jnp.where(lo, half(t2), 0.0)


def head_tiles(gate, x):
    lo = lanes(gate[0].shape[0]) < 64
    return (
        jnp.where(lo, gate[0], half(x[0])),
        jnp.where(lo, half(gate[0]), x[0]),
        jnp.where(lo, gate[1], half(x[1])),
    )


def spread(a, at):
    lo = lanes(a.shape[0]) < 64
    return (
        jnp.where(lo, a[:, at : at + 1], a[:, at + 1 : at + 2]),
        jnp.where(lo, a[:, at + 2 : at + 3], 0.0),
    )


def head_sums(pair):
    a, b = pair
    lane = lanes(a.shape[0])
    s0 = jnp.sum(jnp.where(lane < 64, a, 0.0), axis=1, keepdims=True)
    s1 = jnp.sum(jnp.where(lane < 64, 0.0, a), axis=1, keepdims=True)
    s2 = jnp.sum(b, axis=1, keepdims=True)
    return jnp.where(lane == 0, s0, jnp.where(lane == 1, s1, jnp.where(lane == 2, s2, 0.0)))


def pair_of(ref):
    return ref[:, 0:128], ref[:, 128:256]


def head_row(hp_ref, k, rows=1):
    lane = lanes(rows)
    return jnp.where(
        lane == 0,
        hp_ref[k, 0],
        jnp.where(lane == 1, hp_ref[k, 1], jnp.where(lane == 2, hp_ref[k, 2], 0.0)),
    )


def skip_pair(hp_ref):
    lane = lanes(1)
    return (
        jnp.where(lane < 64, hp_ref[2, 0], hp_ref[2, 1]),
        jnp.where(lane < 64, hp_ref[2, 2], 0.0),
    )


def three_parts(v):
    hi = v.astype(bf16).astype(f32)
    rest = v - hi
    mid = rest.astype(bf16).astype(f32)
    return hi + rolled(mid, 3) + rolled(rest - mid, 6)


def joined(v):
    total = v + rolled(v, -3) + rolled(v, -6)
    return jnp.where(lanes(v.shape[0]) < 3, total, 0.0)


def aux_parts(aux):
    return aux


def act_tiles(c_ref):
    return [silu(c_ref[:, 128 * k : 128 * (k + 1)]) for k in range(5)]


def valid_masks(starts_col):
    row = lax.broadcasted_iota(jnp.int32, starts_col.shape, 0)
    one = jnp.where(row < 1, 0.0, pltpu.roll(starts_col, 1, 0))
    two = jnp.where(row < 2, 0.0, pltpu.roll(starts_col, 2, 0))
    first = 1.0 - starts_col
    return first, first - one, first - one - two


def column_of(row_ref):
    return jnp.broadcast_to(row_ref[0:1, :], (128, T)).T


def selector():
    r = lax.broadcasted_iota(jnp.int32, (D, 256), 0)
    k = lax.broadcasted_iota(jnp.int32, (D, 256), 1)
    return jnp.where(r == k + 32 * jnp.right_shift(k, 4), 1.0, 0.0).astype(bf16)


def small_kernel(shared_ref, gain_ref, conv_ref, out_ref, rows_ref):
    rows_ref[...] = jnp.zeros_like(rows_ref)
    rows_ref[0:6, :] = shared_ref[...]
    gain = gain_ref[...]
    high = gain.astype(bf16).astype(f32)
    rows_ref[6:7, 0:6] = high
    rows_ref[6:7, 128:134] = gain - high
    conv = conv_ref[...]
    high = conv.astype(bf16).astype(f32)
    rows_ref[8:10, MISC + 5 : MISC + 10] = high
    rows_ref[8:10, MISC + 10 : MISC + 15] = conv - high
    low = rows_ref[...].astype(bf16)
    for q in range(N_HEAD):
        out_ref[q] = low


def pack_kernel(
    got_ref, proj_ref, outw_ref, step_ref, pack_ref, shared_ref, misc_ref, wide_ref
):
    misc_ref[...] = jnp.zeros_like(misc_ref)
    misc_ref[0:3, 0:48] = step_ref[...]
    misc = half(misc_ref[...].T)[0:48]
    misc_ref[0:48, :] = misc
    sub = lax.broadcasted_iota(jnp.int32, (6, 128), 0)
    lane = lanes(6)
    for q in range(N_HEAD):
        rows = got_ref[q].astype(f32)
        shared_ref[6 * q : 6 * q + 6, :] = rows[0:6]
        part = jnp.zeros((6, 128), f32)
        for k in range(2):
            line = rows[6:7, 128 * k : 128 * (k + 1)]
            column = jnp.sum(jnp.where(sub == lane, line, 0.0), axis=1, keepdims=True)
            part = part + jnp.where(lane == MISC + 3 + k, column, 0.0)
        misc_ref[6 * q : 6 * q + 6, :] += part
        misc_ref[2 * q : 2 * q + 2, :] += rows[8:10, 0:128]
    misc = misc_ref[0:48, :]
    lo = lanes(48) < 64
    tiles = [proj_ref[h] for h in range(3)]
    wide = []
    for h in range(3):
        wide_ref[:, 0:64] = outw_ref[h]
        wide.append(wide_ref[...])
    tiles += [jnp.where(lo, wide[0], half(wide[1])), jnp.where(lo, wide[2], misc)]
    tiles += [shared_ref[:, 0:128], shared_ref[:, 128:256]]
    for k, tile in enumerate(tiles):
        low = tile.astype(bf16)
        for q in range(N_SEQ):
            pack_ref[q, :, 128 * k : 128 * (k + 1)] = low


def first_kernel(
    hid_ref, halo_ref, st_ref, w_ref, tap_ref, hp_ref,
    normed_ref, v_ref, c_ref, aux_ref, send_ref, row_ref,
):
    misc_t = w_ref[:, 512:640].astype(f32).T
    gain = misc_t[MISC + 3 : MISC + 4] + misc_t[MISC + 4 : MISC + 5]
    conv_t = dot(misc_t.astype(bf16), selector())
    conv_taps = conv_t[MISC + 5 : MISC + 10] + conv_t[MISC + 10 : MISC + 15]
    row_ref[0:1, :] = gain
    row_ref[1:8, :] = jnp.zeros((7, D), f32)
    for src, at, rows in ((halo_ref, 0, HALO), (hid_ref, HALO, T)):
        h = src[...].astype(f32)
        inv = lax.rsqrt(jnp.mean(h * h, axis=1, keepdims=True) + norm_eps)
        normed_ref[at : at + rows, :] = (h * inv * gain).astype(bf16)
    normed = normed_ref[...]
    v_ref[:, 0:384] = dot(normed, w_ref[:, 0:384])
    v_ref[:, 384:640] = dot(normed, w_ref[:, 640:896])
    raw = half(dot(normed[HALO:], w_ref[:, 512:640]))

    lane = lanes(T)
    pre = raw + head_row(hp_ref, 0)
    delta = jnp.where(
        lane < 3, jnp.maximum(pre, 0.0) + jnp.log1p(jnp.exp(-jnp.abs(pre))), 0.0
    )
    slope = jnp.where(lane < 3, sig(pre), 0.0)
    log_decay = -jnp.exp(head_row(hp_ref, 1)) * delta
    starts = column_of(st_ref)
    parts = three_parts(log_decay) + jnp.where(lane == 9, starts, 0.0)
    ri = lax.broadcasted_iota(jnp.int32, (T, T), 0)
    ci = lax.broadcasted_iota(jnp.int32, (T, T), 1)
    summed = dot(jnp.where(ri >= ci, 1.0, 0.0).astype(bf16), parts.astype(bf16))
    cum = joined(summed)
    segment = summed[:, 9:10]
    last = cum[T - 1 : T, :]
    last_segment = segment[T - 1 : T, :]
    keeper = jnp.where((lane < 3) & (segment == 0.0), jnp.exp(cum), 0.0)
    ending = jnp.where((lane < 3) & (segment == last_segment), jnp.exp(last - cum), 0.0)
    aux_ref[...] = (
        cum
        + rolled(delta, 3)
        + rolled(slope, 6)
        + jnp.where(lane == 9, segment, 0.0)
        + rolled(keeper, 10)
        + rolled(ending, 13)
    )

    valid = valid_masks(starts)
    for k in range(5):
        at = slice(128 * k, 128 * (k + 1))
        if k < 3:
            taps = tap_ref[0:5, at]
        else:
            taps = conv_taps[:, 128 * (k - 3) : 128 * (k - 2)]
        total = taps[4:5] + taps[3:4] * v_ref[HALO:, at]
        for lag in (1, 2, 3):
            total = total + taps[3 - lag : 4 - lag] * (
                v_ref[pl.ds(HALO - lag, T), at] * valid[lag - 1]
            )
        c_ref[:, at] = total

    act = act_tiles(c_ref)
    x = x_pair(*act[:3])
    weight = spread(ending * delta, 0)
    ended = jnp.concatenate([x[0] * weight[0], x[1] * weight[1]], axis=1).astype(bf16)
    state = dot(ended, act[3].astype(bf16), 0, 0)
    through = jnp.where(last_segment == 0.0, jnp.exp(last), 0.0)
    high = through.astype(bf16).astype(f32)
    lower = through - high
    sub = lax.broadcasted_iota(jnp.int32, (16, 128), 0)
    tail = jnp.zeros((16, 128), f32)
    for h in range(3):
        tail = jnp.where(sub == h, high[:, h : h + 1], tail)
        tail = jnp.where(sub == 3 + h, lower[:, h : h + 1], tail)
    body = state[0:192].astype(bf16)
    tail = tail.astype(bf16)
    for q in range(N_SEQ):
        send_ref[q, 0:192, :] = body
        send_ref[q, 192:SROWS, :] = tail


def own_kernel(c_ref, aux_ref, cot_ref, w_ref, hp_ref, y_ref, dn_ref, m_ref, mg_ref):
    act = act_tiles(c_ref)
    x = x_pair(*act[:3])
    aux = aux_ref[...]
    aux_t = aux.T
    scores = dot(act[4].astype(bf16), act[3].astype(bf16), 1, 1)
    ri = lax.broadcasted_iota(jnp.int32, (T, T), 0)
    ci = lax.broadcasted_iota(jnp.int32, (T, T), 1)
    allowed = (ri >= ci) & (aux[:, 9:10] == aux_t[9:10, :])
    mask = jnp.where(allowed, 0.0, LOW)
    delta = spread(aux, 3)
    fed = x[0] * delta[0], x[1] * delta[1]
    lo = lanes(T) < 64
    fed_h = (
        jnp.where(lo, fed[0], 0.0).astype(bf16),
        jnp.where(lo, 0.0, fed[0]).astype(bf16),
        fed[1].astype(bf16),
    )
    skip = skip_pair(hp_ref)
    y = [x[0] * skip[0], x[1] * skip[1]]
    for h in range(3):
        decay = jnp.exp(aux[:, h : h + 1] - aux_t[h : h + 1, :] + mask)
        m_ref[h] = decay.astype(bf16)
        mixing = (decay * scores).astype(bf16)
        mg_ref[h] = mixing
        y[h // 2] = y[h // 2] + dot(mixing, fed_h[h])
    y_ref[:, 0:128] = y[0]
    y_ref[:, 128:256] = y[1]
    back = dot(cot_ref[...], w_ref[:, 384:640])
    dn_ref[:, 0:128] = back[:, 0:128]
    dn_ref[:, 128:256] = jnp.where(lo, back[:, 128:256], 0.0)


def decay_rows(tail, shape=(192, 128)):
    both = tail[0:3] + tail[3:6]
    return jnp.concatenate(
        [jnp.broadcast_to(both[h : h + 1], (64, 128)) for h in range(3)], axis=0
    )


def enter_kernel(
    at_ref, got_ref, y0_ref, dn_ref, c_ref, aux_ref, tap_ref,
    y_ref, state_ref, stat_ref, fed_ref,
):
    here = at_ref[0]
    state = jnp.zeros((192, 128), f32)
    for q in range(N_SEQ - 1):
        through = decay_rows(got_ref[q, 192:SROWS, :].astype(f32))
        merged = through * state + got_ref[q, 0:192, :].astype(f32)
        state = jnp.where(q < here, merged, state)
    state_ref[0:192] = state
    state_ref[192:256] = jnp.zeros((64, 128), f32)
    c_mat = silu(c_ref[:, 512:640]).astype(bf16)
    carried = dot(c_mat, state_ref[...].astype(bf16), 1, 1)
    aux = aux_ref[...]
    keeper = spread(aux, 10)
    gate = gate_pair(*[silu(c_ref[:, 128 * k : 128 * (k + 1)]) for k in range(3)])
    squares = jnp.zeros((T, 1), f32)
    inner = jnp.zeros((T, 1), f32)
    for k in range(2):
        at = slice(128 * k, 128 * (k + 1))
        y = y0_ref[:, at] + keeper[k] * carried[:, at]
        y_ref[:, at] = y
        gated = y * gate[k]
        fed = gated * tap_ref[0:1, 384 + 128 * k : 512 + 128 * k]
        fed_ref[:, at] = fed.astype(bf16)
        squares = squares + jnp.sum(gated * gated, axis=1, keepdims=True)
        inner = inner + jnp.sum(fed * dn_ref[:, at], axis=1, keepdims=True)
    lane = lanes(T)
    both = jnp.where(lane == 0, squares, jnp.where(lane == 1, inner, 0.0)).T
    for q in range(N_HEAD):
        stat_ref[q] = both[0:8]


def gated_kernel(
    got_ref, y_ref, dn_ref, c_ref, aux_ref, tap_ref,
    dy_ref, dgate_ref, nout_ref, send_ref, rows_ref, rms_ref,
):
    total = got_ref[0]
    for q in range(1, N_HEAD):
        total = total + got_ref[q]
    total = jnp.concatenate([total, jnp.zeros((120, T), f32)], axis=0).T
    rms = lax.rsqrt(total[:, 0:1] / DI + norm_eps)
    coef = rms * rms * rms * total[:, 1:2] / DI
    rms_ref[...] = jnp.broadcast_to(rms, (T, 128))
    aux = aux_ref[...]
    keeper = spread(aux, 10)
    raw = gate_pair(*[c_ref[:, 128 * k : 128 * (k + 1)] for k in range(3)])
    x = x_pair(*[silu(c_ref[:, 128 * k : 128 * (k + 1)]) for k in range(3)])
    kept = []
    rows_ref[...] = jnp.zeros_like(rows_ref)
    for k in range(2):
        at = slice(128 * k, 128 * (k + 1))
        gain = tap_ref[0:1, 384 + 128 * k : 512 + 128 * k]
        s = sig(raw[k])
        gate = raw[k] * s
        y = y_ref[:, at]
        gated = y * gate
        dn = dn_ref[:, at]
        scaled = gated * rms
        nout_ref[:, at] = (scaled * gain).astype(bf16)
        d_gated = rms * gain * dn - gated * coef
        dy = d_gated * gate
        dy_ref[:, at] = dy
        dgate_ref[:, at] = d_gated * y * s * (1.0 + raw[k] * (1.0 - s))
        kept.append((dy * keeper[k]).astype(bf16))
        rows_ref[0:1, at] = jnp.sum(dn * scaled, axis=0, keepdims=True)
        rows_ref[1:2, at] = jnp.sum(dy * x[k], axis=0, keepdims=True)
    c_mat = silu(c_ref[:, 512:640]).astype(bf16)
    adj = dot(jnp.concatenate(kept, axis=1), c_mat, 0, 0)[0:192].astype(bf16)
    for q in range(N_SEQ):
        send_ref[q] = adj


def out_kernel(fed_ref, w_ref, out_ref):
    out_ref[...] = dot(fed_ref[...], w_ref[:, 384:640], 1, 1).astype(bf16)


def block_kernel(sum_ref, rms_ref, hid_ref, out_ref):
    rms = rms_ref[:, 0:1]
    out_ref[...] = (hid_ref[...].astype(f32) + rms * sum_ref[...].astype(f32)).astype(bf16)


def own_back_kernel(
    dy_ref, y_ref, y0_ref, c_ref, aux_ref, m_ref, mg_ref, state_ref,
    dx_ref, db_ref, dc_ref, dcum_ref,
):
    aux = aux_ref[...]
    aux_t = aux.T
    act = act_tiles(c_ref)
    x = x_pair(*act[:3])
    b_low, c_low = act[3].astype(bf16), act[4].astype(bf16)
    dy = pair_of(dy_ref)
    lo = lanes(T) < 64
    dy_h = (
        jnp.where(lo, dy[0], 0.0).astype(bf16),
        jnp.where(lo, 0.0, dy[0]).astype(bf16),
        dy[1].astype(bf16),
    )
    x_low = x[0].astype(bf16), x[1].astype(bf16)
    lane = lanes(T)
    dx = [jnp.zeros((T, 128), f32), jnp.zeros((T, 128), f32)]
    spread_sum = jnp.zeros((T, T), f32)
    rows = jnp.zeros((T, 128), f32)
    cols = jnp.zeros((128, T), f32)
    sub = lax.broadcasted_iota(jnp.int32, (128, T), 0)
    for h in range(3):
        pairs = dot(dy_h[h], x_low[h // 2], 1, 1) * aux_t[3 + h : 4 + h, :]
        mixing = mg_ref[h]
        spread_sum = spread_sum + pairs * m_ref[h].astype(f32)
        weights = pairs * mixing.astype(f32)
        rows = jnp.where(lane == h, jnp.sum(weights, axis=1, keepdims=True), rows)
        cols = jnp.where(sub == h, jnp.sum(weights, axis=0, keepdims=True), cols)
        dx[h // 2] = dx[h // 2] + dot(mixing, dy_h[h], 0, 0)
    low = spread_sum.astype(bf16)
    keeper = spread(aux, 10)
    kept = jnp.concatenate([dy[0] * keeper[0], dy[1] * keeper[1]], axis=1).astype(bf16)
    dc_ref[...] = dot(low, b_low) + dot(kept, state_ref[...].astype(bf16))
    db_ref[...] = dot(low, c_low, 0, 0)
    dx_ref[:, 0:128] = dx[0]
    dx_ref[:, 128:256] = dx[1]
    carried = [
        dy[k] * (y_ref[:, 128 * k : 128 * (k + 1)] - y0_ref[:, 128 * k : 128 * (k + 1)])
        for k in range(2)
    ]
    dcum_ref[...] = rows - cols.T + head_sums(carried)


def back_kernel(
    at_ref, got_ref, fwd_ref, state_ref, dx_ref, db_ref, dc_ref, dcum_ref, c_ref, aux_ref,
    v_ref, tap_ref, hp_ref, st_ref, dy_ref, dgate_ref, w_ref, rows_ref, hid_ref, halo_ref,
    dv_ref, dstep_ref, keep_ref, give_ref, edge_ref, chan_ref, conv_ref, gain_ref,
    pad_ref, norm_ref,
):
    here = at_ref[0]
    adj = jnp.zeros((192, 128), f32)
    for q in range(N_SEQ - 1, 0, -1):
        through = decay_rows(fwd_ref[q, 192:SROWS, :].astype(f32))
        merged = through * adj + got_ref[q].astype(f32)
        adj = jnp.where(q > here, merged, adj)
    aux = aux_ref[...]
    lane = lanes(T)
    conv = [c_ref[:, 128 * k : 128 * (k + 1)] for k in range(5)]
    sigs = [sig(v) for v in conv]
    x = x_pair(*[conv[k] * sigs[k] for k in range(3)])
    b_low = (conv[3] * sigs[3]).astype(bf16)
    delta, ending = spread(aux, 3), spread(aux, 13)
    adj_low = jnp.concatenate([adj, jnp.zeros((64, 128), f32)], axis=0).astype(bf16)
    through_b = dot(b_low, adj_low, 1, 1)
    skip = skip_pair(hp_ref)
    dy = pair_of(dy_ref)
    ended, extra, full, d_x = [], [], [], []
    for k in range(2):
        at = slice(128 * k, 128 * (k + 1))
        late = ending[k] * through_b[:, at]
        total = dx_ref[:, at] + late
        d_x.append(delta[k] * total + skip[k] * dy[k])
        full.append(x[k] * total)
        extra.append(x[k] * late)
        ended.append(x[k] * delta[k] * ending[k])
    d_b = db_ref[...] + dot(jnp.concatenate(ended, axis=1).astype(bf16), adj_low)
    d_delta = head_sums(full)
    tail = head_sums(extra) * rolled(aux, -3)
    tail = jnp.where(lane < 3, tail, 0.0)
    d_cum = dcum_ref[...] - tail
    ri = lax.broadcasted_iota(jnp.int32, (T, T), 0)
    ci = lax.broadcasted_iota(jnp.int32, (T, T), 1)
    upper = jnp.where(ci >= ri, 1.0, 0.0).astype(bf16)
    d_log = joined(dot(upper, three_parts(d_cum).astype(bf16)))
    own = decay_rows(fwd_ref[here, 192:SROWS, :].astype(f32))
    met = own * adj * state_ref[0:192]
    lane1 = lanes(1)
    meets = jnp.zeros((1, 128), f32)
    for h in range(3):
        meets = jnp.where(lane1 == h, jnp.sum(met[64 * h : 64 * h + 64]), meets)
    d_log = d_log + jnp.sum(tail, axis=0, keepdims=True) + meets
    d_log = jnp.where(lane < 3, d_log, 0.0)
    rate = jnp.exp(head_row(hp_ref, 1))
    d_raw = (d_delta - rate * d_log) * rolled(aux, -6)
    d_raw = jnp.where(lane < 3, d_raw, 0.0)
    delta_cols = jnp.where(lane < 3, rolled(aux, -3), 0.0)
    step_low = half(d_raw).astype(bf16)
    dstep_ref[...] = step_low

    d_gate = pair_of(dgate_ref)
    x_tiles = head_tiles((jnp.zeros_like(d_x[0]),) * 2, d_x)
    gate_tiles = head_tiles(d_gate, (jnp.zeros_like(d_x[0]),) * 2)
    lo = lane < 64
    conv_t = dot(w_ref[:, 512:640].astype(f32).T.astype(bf16), selector())
    conv_taps = conv_t[MISC + 5 : MISC + 10] + conv_t[MISC + 10 : MISC + 15]
    starts = column_of(st_ref)
    valid = valid_masks(starts)
    pad_ref[0:HALO] = jnp.zeros((HALO, 128), f32)
    pad_ref[HALO + T :] = jnp.zeros((HALO, 128), f32)
    tap_rows = []
    for k in range(5):
        at = slice(128 * k, 128 * (k + 1))
        slope = sigs[k] * (1.0 + conv[k] * (1.0 - sigs[k]))
        if k < 3:
            d_conv = jnp.where(lo, gate_tiles[k], x_tiles[k] * slope)
            taps = tap_ref[0:5, at]
        else:
            d_conv = (d_b if k == 3 else dc_ref[...]) * slope
            taps = conv_taps[:, 128 * (k - 3) : 128 * (k - 2)]
        sums = [None, None, None, None, jnp.sum(d_conv, axis=0, keepdims=True)]
        sums[3] = jnp.sum(d_conv * v_ref[HALO:, at], axis=0, keepdims=True)
        pad_ref[HALO : HALO + T] = taps[3:4] * d_conv
        acc = pad_ref[0 : HALO + T]
        for lag in (1, 2, 3):
            masked = d_conv * valid[lag - 1]
            sums[3 - lag] = jnp.sum(
                masked * v_ref[pl.ds(HALO - lag, T), at], axis=0, keepdims=True
            )
            pad_ref[HALO : HALO + T] = taps[3 - lag : 4 - lag] * masked
            acc = acc + pad_ref[pl.ds(lag, HALO + T)]
        dv_ref[:, at] = acc.astype(bf16)
        tap_rows.append(sums)

    chan_ref_rows = []
    for j in range(5):
        pair = x_pair(*[tap_rows[k][j] for k in range(3)])
        chan_ref_rows.append(jnp.concatenate(pair, axis=1))
    chan_ref_rows.append(rows_ref[0:1, :])
    h0 = jnp.sum(d_raw, axis=0, keepdims=True)
    h1 = jnp.sum(d_log * (-rate) * delta_cols, axis=0, keepdims=True)
    h2 = head_sums((rows_ref[1:2, 0:128], rows_ref[1:2, 128:256]))
    zero = jnp.zeros((1, 128), f32)
    for r in (h0, h1, h2):
        chan_ref_rows.append(jnp.concatenate([r, zero], axis=1))
    for j, r in enumerate(chan_ref_rows):
        chan_ref[j : j + 1, :] = r
    chan_ref[9:16, :] = jnp.zeros((7, 256), f32)
    for j in range(5):
        conv_ref[j : j + 1, :] = jnp.concatenate([tap_rows[3][j], tap_rows[4][j]], axis=1)
    conv_ref[5:8, :] = jnp.zeros((3, 256), f32)

    d_norm = dot(dv_ref[:, 0:384], w_ref[:, 0:384], 1, 1)
    d_norm = d_norm + dot(dv_ref[:, 384:640], w_ref[:, 640:896], 1, 1)
    main = d_norm[HALO:] + dot(step_low, w_ref[:, 512:640], 1, 1)
    norm_ref[...] = main
    core = at_ref[2]
    keep_ref[...] = norm_ref[pl.ds(pl.multiple_of(core * 256, 256), 256), :].astype(bf16)
    give_ref[...] = norm_ref[pl.ds(pl.multiple_of(256 - core * 256, 256), 256), :].astype(bf16)
    edge_ref[...] = d_norm[0:HALO].astype(bf16)
    total = jnp.zeros((1, D), f32)
    for src, val in ((halo_ref, d_norm[0:HALO]), (hid_ref, main)):
        h = src[...].astype(f32)
        inv = lax.rsqrt(jnp.mean(h * h, axis=1, keepdims=True) + norm_eps)
        total = total + jnp.sum(val * (h * inv), axis=0, keepdims=True)
    gain_ref[0:1] = total
    gain_ref[1:8] = jnp.zeros((7, D), f32)


def grad_kernel(
    normed_ref, dv_ref, dstep_ref, nout_ref, cot_ref, conv_ref, gain_ref, chan_ref, out_ref
):
    normed = normed_ref[...]
    out_ref[:, 0:384] = dot(normed, dv_ref[:, 0:384], 0, 0).astype(bf16)
    out_ref[:, 640:896] = dot(normed, dv_ref[:, 384:640], 0, 0).astype(bf16)
    outs = dot(cot_ref[...], nout_ref[...], 0, 0)
    out_ref[:, 384:512] = outs[:, 0:128].astype(bf16)
    tile = outs[:, 128:256] + dot(normed_ref[HALO:, :], dstep_ref[...], 0, 0)
    grads = jnp.concatenate([jnp.zeros((MISC + 5, 256), f32), conv_ref[0:5, :]], axis=0)
    grads = jnp.concatenate([grads, jnp.zeros((128 - MISC - 10, 256), f32)], axis=0)
    high = grads.astype(bf16)
    lower = (grads - high.astype(f32)).astype(bf16)
    sel = selector()
    tile = tile + dot(sel, high, 1, 1) + pltpu.roll(dot(sel, lower, 1, 1), 5, 1)
    gain = gain_ref[0:1]
    gain_high = gain.astype(bf16).astype(f32)
    sub = lax.broadcasted_iota(jnp.int32, (128, D), 0)
    column = jnp.where(
        sub == MISC + 3, gain_high, jnp.where(sub == MISC + 4, gain - gain_high, 0.0)
    ).T
    turned = jnp.concatenate([chan_ref[...], jnp.zeros((112, 256), f32)], axis=0).T
    turned = jnp.where(lanes(256) < 9, turned, 0.0)
    shared = jnp.zeros((48, 128), f32)
    for g in range(4):
        shared = shared + rolled(turned[48 * g : 48 * g + 48], MISC + 16 + 9 * g)
    tile = tile + column + jnp.concatenate([shared] * N_SEQ, axis=0)
    out_ref[:, 512:640] = tile.astype(bf16)


def pair_kernel(at_ref, keep_ref, got_ref, edge0_ref, edge1_ref, own_ref, s1, s2, s3, sum_ref):
    sum_ref[...] = keep_ref[...].astype(f32) + got_ref[...].astype(f32)
    sum_ref[256 - HALO :, :] += edge0_ref[...].astype(f32) + edge1_ref[...].astype(f32)
    for by, ref in enumerate((own_ref, s1, s2, s3)):
        start = pl.multiple_of(lax.rem(at_ref[1] + by, 4) * 64, 64)
        ref[...] = sum_ref[pl.ds(start, 64), :].astype(bf16)


def four_kernel(a_ref, b_ref, c_ref, d_ref, out_ref):
    total = a_ref[...].astype(f32) + b_ref[...].astype(f32)
    out_ref[...] = (total + c_ref[...].astype(f32) + d_ref[...].astype(f32)).astype(bf16)


def input_kernel(*refs):
    at_ref, refs = refs[0], refs[1:]
    hid_ref, cot_ref, row_ref, out_ref = refs[8:]
    for side in range(2):
        core = at_ref[2] if side == 0 else 1 - at_ref[2]
        for by in range(4):
            block = core * 4 + lax.rem(at_ref[1] + 4 - by, 4)
            rows = pl.ds(pl.multiple_of(block * 64, 64), 64)
            h = hid_ref[rows, :].astype(f32)
            inv = lax.rsqrt(jnp.mean(h * h, axis=1, keepdims=True) + norm_eps)
            d_scaled = refs[4 * side + by][...].astype(f32) * row_ref[0:1, :]
            inner = jnp.sum(d_scaled * h, axis=1, keepdims=True)
            out_ref[rows, :] = (
                cot_ref[rows, :].astype(f32)
                + inv * d_scaled
                - h * (inv * inv * inv * inner / D)
            )


def adam(weight, grad, first, second, rate):
    first_new = beta_one * first + (1.0 - beta_one) * grad
    second_new = beta_two * second + (1.0 - beta_two) * grad * grad
    first_hat = first_new / (1.0 - beta_one**STEP)
    second_hat = second_new / (1.0 - beta_two**STEP)
    weight_new = weight - rate * (
        first_hat / (jnp.sqrt(second_hat) + adam_eps) + decay_rate * weight
    )
    return first_new, second_new, weight_new


RATE_D = 1.4 * D ** (-0.5)
RATE_I = 1.4 * DI ** (-0.5)


def put(refs, at, values):
    for ref, value in zip(refs, values):
        ref[at] = value


def update_kernel(*refs):
    grad_ref, refs = refs[0], refs[1:]
    proj, step, out, chan, head = (refs[3 * k : 3 * k + 3] for k in range(5))
    outs = refs[15:]
    proj_o, step_o, out_o, chan_o, head_o = (outs[3 * k : 3 * k + 3] for k in range(5))
    rest_ref = outs[15]
    total = grad_ref[0].astype(f32)
    for q in range(1, N_SEQ):
        total = total + grad_ref[q].astype(f32)
    misc = total[:, 512:640]
    rest_ref[...] = jnp.zeros_like(rest_ref)
    for h in range(N_HEAD):
        rest_ref[h, 0:6, 0:256] = total[6 * h : 6 * h + 6, 640:896]
        rest_ref[h, 0:6, 256:384] = misc[6 * h : 6 * h + 6]
        rest_ref[h, 0:2, 384:512] = misc[2 * h : 2 * h + 2]
    for h in range(3):
        w, m, v = (r[h] for r in proj)
        put(proj_o, h, adam(w, total[:, 128 * h : 128 * (h + 1)], m, v, RATE_D))
        tile = total[:, 384 + 128 * (h // 2) : 512 + 128 * (h // 2)]
        tile = half(tile) if h == 1 else tile
        w, m, v = (r[h] for r in out)
        put(out_o, h, adam(w, tile[:, 0:64], m, v, RATE_I))
    turned = jnp.concatenate([misc, jnp.zeros((80, 128), f32)], axis=0).T
    at = (slice(None), slice(None))
    w, m, v = (r[at] for r in step)
    put(step_o, at, adam(w, turned[MISC : MISC + 3, 0:48], m, v, RATE_D))
    first = MISC + 16
    p = [turned[first + 9 * g : first + 9 * g + 9] for g in range(4)]
    lane = lanes(9)
    wrapped = rolled(p[2], 96)
    pair = (
        p[0] + rolled(p[1], 48) + jnp.where(lane >= 96, wrapped, 0.0),
        jnp.where(lane < 16, wrapped, 0.0) + rolled(p[3], 16),
    )
    for h in range(3):
        piece = half(pair[0]) if h == 1 else pair[h // 2]
        at = (slice(None), h, slice(None))
        w, m, v = (r[at] for r in chan)
        put(chan_o, at, adam(w, piece[0:6, 0:64], m, v, 0.5))
    at = (slice(None), slice(None))
    w, m, v = (r[at] for r in head)
    put(head_o, at, adam(w, pair[0][6:9, 0:3], m, v, 1.0))


def rest_kernel(*refs):
    got_ref, refs = refs[0], refs[1:]
    shared, gain, conv = (refs[3 * k : 3 * k + 3] for k in range(3))
    outs = refs[9:]
    shared_o, gain_o, conv_o = (outs[3 * k : 3 * k + 3] for k in range(3))
    total = got_ref[0]
    for q in range(1, N_HEAD):
        total = total + got_ref[q]
    at = (slice(None), slice(None))
    w, m, v = (r[at] for r in shared)
    put(shared_o, at, adam(w, total[0:6, 0:256], m, v, RATE_D))
    column = total[:, 256 + MISC + 3 : 256 + MISC + 4] + total[:, 256 + MISC + 4 : 256 + MISC + 5]
    sub = lax.broadcasted_iota(jnp.int32, (8, 128), 0)
    row = jnp.sum(jnp.where(sub == lanes(8), column, 0.0), axis=0, keepdims=True)
    w, m, v = (r[at] for r in gain)
    put(gain_o, at, adam(w, row[:, 0:6], m, v, 0.5))
    tile = total[0:2, 384:512]
    both = rolled(tile, -(MISC + 5)) + rolled(tile, -(MISC + 10))
    w, m, v = (r[at] for r in conv)
    put(conv_o, at, adam(w, both[:, 0:5], m, v, 0.5))


def exchange(blocks, axis):
    return lax.all_to_all(blocks, axis, 0, 0, tiled=True)


def around(a, axis, by):
    peers = lax.axis_size(axis)
    return lax.ppermute(a, axis, [(i, (i + by) % peers) for i in range(peers)])


def to_next(a):
    return lax.ppermute(a, SEQ, [(i, i + 1) for i in range(N_SEQ - 1)])


def to_previous(a, core):
    pairs = [(2 * i + 2 + core, 2 * i + 1) for i in range(N_SEQ - 1)]
    return lax.ppermute(a, SEQ + ("head_1",), pairs)


def body(
    hidden_in, cotangent, doc_starts, proj_weight, step_weight, out_weight, shared_weight,
    pre_gain, channel_params, head_params, shared_conv, proj_first, proj_second, step_first,
    step_second, out_first, out_second, shared_first, shared_second, gain_first, gain_second,
    channel_first, channel_second, head_first, head_second, conv_first, conv_second,
):
    where = jnp.stack(
        [lax.axis_index(SEQ), lax.axis_index("head_0"), lax.axis_index("head_1")]
    ).astype(jnp.int32)
    halo = to_next(hidden_in[T - HALO :])
    matrices = [jnp.transpose(a, (1, 0, 2)) for a in (proj_weight, proj_first, proj_second)]
    steps = [a.T for a in (step_weight, step_first, step_second)]
    out_weights = [jnp.transpose(a, (0, 2, 1)) for a in (out_weight, out_first, out_second)]
    gains_in = [a.reshape(1, 6) for a in (pre_gain, gain_first, gain_second)]

    (small,) = call(
        small_kernel, [((N_HEAD, 16, 256), bf16)], shared_weight, gains_in[0], shared_conv,
        scratch=[pltpu.VMEM((16, 256), f32)], name="small",
    )
    small = exchange(small, HEAD)
    small, halo = lax.optimization_barrier((small, halo))
    (pack,) = call(
        pack_kernel, [((N_SEQ, 48, NW), bf16)], small, matrices[0], out_weights[0], steps[0],
        scratch=[
            pltpu.VMEM((48, 256), f32), pltpu.VMEM((128, 128), f32), pltpu.VMEM((48, 128), f32)
        ],
        name="pack",
    )
    weights = exchange(pack, SEQ).reshape(D, NW)

    marks = doc_starts.astype(f32).reshape(1, T)
    fixed = jnp.broadcast_to(
        (jnp.arange(6) == 3).astype(f32)[:, None, None], channel_params.shape
    )
    taps = jnp.concatenate([fixed, channel_params], axis=2).reshape(6, 384)
    gains = jnp.pad(channel_params[5].reshape(1, 192), ((0, 5), (0, 64)))
    taps = jnp.pad(jnp.concatenate([taps, gains], axis=1), ((0, 2), (0, 0)))

    normed, values, conv, aux, sent, row = call(
        first_kernel,
        [
            ((HALO + T, D), bf16), ((HALO + T, NV), f32), ((T, NV), f32), ((T, 128), f32),
            ((N_SEQ, SROWS, 128), bf16), ((8, D), f32),
        ],
        hidden_in, halo, marks, weights, taps, head_params, smem=(5,), name="first",
    )
    states = exchange(sent, SEQ)
    y_own, d_normed, decays, mixing = call(
        own_kernel,
        [((T, 256), f32), ((T, 256), f32), ((3, T, T), bf16), ((3, T, T), bf16)],
        conv, aux, cotangent, weights, head_params, smem=(4,), name="own",
    )
    y_full, state, stat, fed = call(
        enter_kernel,
        [((T, 256), f32), ((256, 128), f32), ((N_HEAD, 8, T), f32), ((T, 256), bf16)],
        where, states, y_own, d_normed, conv, aux, taps, smem=(0,), name="enter",
    )
    stats = exchange(stat, HEAD)
    (partial_out,) = call(out_kernel, [((T, D), bf16)], fed, weights, name="out")
    block_sum = lax.psum(partial_out, HEAD)
    d_y, d_gate, normed_out, sent_adj, rows, rms = call(
        gated_kernel,
        [
            ((T, 256), f32), ((T, 256), f32), ((T, 256), bf16),
            ((N_SEQ, 192, 128), bf16), ((8, 256), f32), ((T, 128), f32),
        ],
        stats, y_full, d_normed, conv, aux, taps, name="gated",
    )
    adjoints = exchange(sent_adj, SEQ)
    d_x, d_b, d_c, d_cum = call(
        own_back_kernel,
        [((T, 256), f32), ((T, 128), f32), ((T, 128), f32), ((T, 128), f32)],
        d_y, y_full, y_own, conv, aux, decays, mixing, state, name="own_back",
    )
    d_values, d_step, keep, give, edge, chan, d_conv, d_gain = call(
        back_kernel,
        [
            ((HALO + T, NV), bf16), ((T, 128), bf16), ((T // 2, D), bf16), ((T // 2, D), bf16),
            ((HALO, D), bf16), ((16, 256), f32), ((8, 256), f32), ((8, D), f32),
        ],
        where, adjoints, states, state, d_x, d_b, d_c, d_cum, conv, aux,
        values, taps, head_params, marks, d_y, d_gate, weights, rows, hidden_in, halo,
        smem=(0, 12),
        scratch=[pltpu.VMEM((T + 2 * HALO, 128), f32), pltpu.VMEM((T, D), f32)],
        name="back",
    )
    taken = around(give, "head_1", 1)
    edges = [to_previous(edge, core) for core in range(2)]
    (grads,) = call(
        grad_kernel, [((D, NW), bf16)],
        normed, d_values, d_step, normed_out, cotangent, d_conv, d_gain, chan, name="grad",
    )
    grads = exchange(grads.reshape(N_SEQ, 48, NW), SEQ)

    piece = ((T // N_HEAD, D), bf16)
    pieces = call(
        pair_kernel, [piece] * 4, where, keep, taken, *edges, smem=(0,),
        scratch=[pltpu.VMEM((T // 2, D), f32)], name="pair",
    )
    parts = [pieces[0]] + [around(pieces[by], "head_0", by) for by in (1, 2, 3)]
    (own,) = call(four_kernel, [piece], *parts, name="four")
    near = [own] + [around(own, "head_0", by) for by in (1, 2, 3)]
    far = [around(a, "head_1", 1) for a in near]
    (input_grad,) = call(
        input_kernel, [((T, D), f32)], where, *near, *far, hidden_in, cotangent, row,
        smem=(0,), name="input",
    )

    proj, step, out = (3, 48, 128), (3, 48), (3, 48, 64)
    shapes = [proj] * 3 + [step] * 3 + [out] * 3 + [(6, 3, 64)] * 3 + [(3, 3)] * 3
    updated = call(
        update_kernel,
        [(s, f32) for s in shapes] + [((N_HEAD, 8, 512), f32)],
        grads, *matrices, *steps, *out_weights, channel_params, channel_first,
        channel_second, head_params, head_first, head_second, name="update",
    )
    rest = exchange(updated[15], HEAD)
    (block_out,) = call(
        block_kernel, [((T, D), bf16)], block_sum, rms, hidden_in, name="block"
    )
    shared = call(
        rest_kernel,
        [(s, f32) for s in [(6, 256)] * 3 + [(1, 6)] * 3 + [(2, 5)] * 3],
        rest, shared_weight, shared_first, shared_second, *gains_in, shared_conv, conv_first,
        conv_second, name="rest",
    )
    return (
        block_out, input_grad,
        *(jnp.transpose(a, (1, 0, 2)) for a in updated[0:3]),
        *(a.T for a in updated[3:6]),
        *(jnp.transpose(a, (0, 2, 1)) for a in updated[6:9]),
        *shared[0:3],
        *(g.reshape(6) for g in shared[3:6]),
        *updated[9:15],
        *shared[6:9],
    )


def solution(mesh):
    finer = Mesh(mesh.devices.reshape(4, 4, 4, 2), SEQ_HEAD)
    matrix = P(SEQ, HEAD, None)
    step = P(SEQ, HEAD)
    out = P(HEAD, None, SEQ)
    both = P(SEQ_HEAD, None)
    gain = P(SEQ_HEAD)
    channel = P(None, HEAD, None)
    head = P(None, HEAD)
    tokens = P(SEQ, None)
    return jax.shard_map(
        body,
        mesh=finer,
        in_specs=(
            tokens, tokens, P(SEQ), matrix, step, out, both, gain, channel, head, both,
            matrix, matrix, step, step, out, out, both, both, gain, gain, channel, channel,
            head, head, both, both,
        ),
        out_specs=(
            (tokens, tokens)
            + (matrix,) * 3 + (step,) * 3 + (out,) * 3 + (both,) * 3 + (gain,) * 3
            + (channel,) * 3 + (head,) * 3 + (both,) * 3
        ),
        check_vma=False,
    )
```

```python
import functools

import jax
import jax.numpy as jnp
from jax import lax
from jax.experimental import pallas as pl
from jax.experimental.pallas import tpu as pltpu
from jax.sharding import Mesh
from jax.sharding import PartitionSpec as P

D = 768
DI = 1536
STEP = 10
SEQ = ("seq_0", "seq_1")
HEAD = ("head_0", "head_1")
SEQ_HEAD = SEQ + HEAD
N_SEQ = 16
N_HEAD = 8

T = 512
HALO = 16
NV = 640
NW = 640
NG = 896
MISC = 64
SLAB = 96
SROWS = 208

f32 = jnp.float32
bf16 = jnp.bfloat16
norm_eps = 1e-05
beta_one = 0.9
beta_two = 0.999
adam_eps = 1e-08
decay_rate = 0.01
LOW = -1e30

PARAMS = pltpu.CompilerParams(vmem_limit_bytes=56 * 1024 * 1024)
VM = pl.BlockSpec(memory_space=pltpu.VMEM)
SM = pl.BlockSpec(memory_space=pltpu.SMEM)


def call(kernel, outs, *args, smem=(), scratch=(), name=None):
    return pl.pallas_call(
        kernel,
        out_shape=[jax.ShapeDtypeStruct(s, d) for s, d in outs],
        in_specs=[SM if i in smem else VM for i in range(len(args))],
        out_specs=[VM] * len(outs),
        scratch_shapes=list(scratch),
        compiler_params=PARAMS,
        name=name,
    )(*args)


def dot(a, b, ca=1, cb=0):
    return lax.dot_general(a, b, (((ca,), (cb,)), ((), ())), preferred_element_type=f32)


def lanes(rows):
    return lax.broadcasted_iota(jnp.int32, (rows, 128), 1)


def half(v):
    return pltpu.roll(v, 64, 1)


def rolled(v, by):
    return pltpu.roll(v, by % 128, 1)


def sig(v):
    return 1.0 / (1.0 + jnp.exp(-v))


def silu(v):
    return v * sig(v)


def dsilu(v):
    s = sig(v)
    return s * (1.0 + v * (1.0 - s))


def gate_pair(t0, t1, t2):
    lo = lanes(t0.shape[0]) < 64
    return jnp.where(lo, t0, half(t1)), jnp.where(lo, t2, 0.0)


def x_pair(t0, t1, t2):
    lo = lanes(t0.shape[0]) < 64
    return jnp.where(lo, half(t0), t1), jnp.where(lo, half(t2), 0.0)


def head_tiles(gate, x):
    lo = lanes(gate[0].shape[0]) < 64
    return (
        jnp.where(lo, gate[0], half(x[0])),
        jnp.where(lo, half(gate[0]), x[0]),
        jnp.where(lo, gate[1], half(x[1])),
    )


def spread(a, at):
    lo = lanes(a.shape[0]) < 64
    return (
        jnp.where(lo, a[:, at : at + 1], a[:, at + 1 : at + 2]),
        jnp.where(lo, a[:, at + 2 : at + 3], 0.0),
    )


def head_sums(pair):
    a, b = pair
    lane = lanes(a.shape[0])
    s0 = jnp.sum(jnp.where(lane < 64, a, 0.0), axis=1, keepdims=True)
    s1 = jnp.sum(jnp.where(lane < 64, 0.0, a), axis=1, keepdims=True)
    s2 = jnp.sum(b, axis=1, keepdims=True)
    return jnp.where(lane == 0, s0, jnp.where(lane == 1, s1, jnp.where(lane == 2, s2, 0.0)))


def pair_of(ref):
    return ref[:, 0:128], ref[:, 128:256]


def head_row(hp_ref, k, rows=1):
    lane = lanes(rows)
    return jnp.where(
        lane == 0,
        hp_ref[k, 0],
        jnp.where(lane == 1, hp_ref[k, 1], jnp.where(lane == 2, hp_ref[k, 2], 0.0)),
    )


def skip_pair(hp_ref):
    lane = lanes(1)
    return (
        jnp.where(lane < 64, hp_ref[2, 0], hp_ref[2, 1]),
        jnp.where(lane < 64, hp_ref[2, 2], 0.0),
    )


def three_parts(v):
    hi = v.astype(bf16).astype(f32)
    rest = v - hi
    mid = rest.astype(bf16).astype(f32)
    return hi + rolled(mid, 3) + rolled(rest - mid, 6)


def joined(v):
    total = v + rolled(v, -3) + rolled(v, -6)
    return jnp.where(lanes(v.shape[0]) < 3, total, 0.0)


def act_tiles(c_ref):
    return [silu(c_ref[:, 128 * k : 128 * (k + 1)]) for k in range(5)]


def valid_masks(starts_col):
    row = lax.broadcasted_iota(jnp.int32, starts_col.shape, 0)
    one = jnp.where(row < 1, 0.0, pltpu.roll(starts_col, 1, 0))
    two = jnp.where(row < 2, 0.0, pltpu.roll(starts_col, 2, 0))
    first = 1.0 - starts_col
    return first, first - one, first - one - two


def column_of(row_ref):
    return jnp.broadcast_to(row_ref[0:1, :], (128, T)).T


def selector():
    r = lax.broadcasted_iota(jnp.int32, (D, 256), 0)
    k = lax.broadcasted_iota(jnp.int32, (D, 256), 1)
    h = jnp.bitwise_and(jnp.right_shift(k, 1), 7)
    at = 48 * jnp.right_shift(k, 4) + 6 * h + jnp.bitwise_and(k, 1)
    return jnp.where(r == at, 1.0, 0.0).astype(bf16)


def slab_rows(a):
    s = jnp.right_shift(a * 43, 8)
    return 42 * s + a


def pack_kernel(
    proj_ref, outw_ref, step_ref, shared_ref, gain_ref, conv_ref, pack_ref, misc_ref, wide_ref
):
    misc_ref[...] = jnp.zeros_like(misc_ref)
    misc_ref[0:3, 0:48] = step_ref[...]
    misc_ref[0:48, :] = half(misc_ref[...].T)[0:48]
    wide_ref[...] = jnp.zeros_like(wide_ref)
    wide_ref[0:1, 0:6] = gain_ref[...]
    sub = lax.broadcasted_iota(jnp.int32, (6, 128), 0)
    lane = lanes(6)
    column = jnp.sum(jnp.where(sub == lane, wide_ref[0:1, :], 0.0), axis=1, keepdims=True)
    high = column.astype(bf16).astype(f32)
    misc_ref[0:6, :] += jnp.where(lane == MISC + 3, high, 0.0) + jnp.where(
        lane == MISC + 4, column - high, 0.0
    )
    conv = conv_ref[...]
    high = conv.astype(bf16).astype(f32)
    misc_ref[0:2, MISC + 5 : MISC + 10] = high
    misc_ref[0:2, MISC + 10 : MISC + 15] = conv - high
    for j in range(8):
        tile = rolled(shared_ref[:, 128 * (j // 4) : 128 * (j // 4) + 128], SLAB - 32 * (j % 4))
        misc_ref[6 * j : 6 * j + 6, :] += jnp.where(lane >= SLAB, tile, 0.0)
    misc = misc_ref[0:48, :]
    lo = lanes(48) < 64
    wide = []
    for h in range(3):
        wide_ref[:, 0:64] = outw_ref[h]
        wide.append(wide_ref[...])
    tiles = [proj_ref[h] for h in range(3)]
    tiles += [jnp.where(lo, wide[0], half(wide[1])), jnp.where(lo, wide[2], misc)]
    for k, tile in enumerate(tiles):
        low = tile.astype(bf16)
        for q in range(N_SEQ):
            pack_ref[q, :, 128 * k : 128 * (k + 1)] = low


def slab_kernel(w_ref, slab_ref):
    misc = w_ref[:, 512:640]
    a = lax.broadcasted_iota(jnp.int32, (96, D), 0)
    d = lax.broadcasted_iota(jnp.int32, (96, D), 1)
    gap = d - slab_rows(a)
    lane = lanes(96)
    tiles = [jnp.zeros((96, 128), f32)] * 2
    for j in range(8):
        got = dot(jnp.where(gap == 6 * j, 1.0, 0.0).astype(bf16), misc)
        if j == 0:
            slab_ref[:, 256:384] = jnp.where(lane < SLAB, got, 0.0).astype(bf16)
        own = jnp.where(lane >= SLAB, got, 0.0)
        tiles[j // 4] = tiles[j // 4] + rolled(own, 32 * (j % 4) - SLAB)
    slab_ref[:, 0:128] = tiles[0].astype(bf16)
    slab_ref[:, 128:256] = tiles[1].astype(bf16)


def first_kernel(*refs):
    at_ref, slabs, refs = refs[0], refs[1:9], refs[9:]
    hid_ref, halo_ref, st_ref, w_ref, tap_ref, hp_ref = refs[:6]
    normed_ref, v_ref, c_ref, aux_ref, send_ref, row_ref, wide_ref, ctap_ref = refs[6:14]
    all_ref = refs[14]
    d = lax.broadcasted_iota(jnp.int32, (D, 96), 0)
    a = lax.broadcasted_iota(jnp.int32, (D, 96), 1)
    gap = d - slab_rows(a)
    picks = []
    for b in range(8):
        core = at_ref[2] if b < 4 else 1 - at_ref[2]
        head = 2 * lax.rem(at_ref[1] + 4 - b % 4, 4) + core
        all_ref[96 * b : 96 * b + 96, :] = slabs[b][...]
        picks.append(jnp.where(gap == 6 * head, 1.0, 0.0))
    spread_rows = dot(jnp.concatenate(picks, axis=1).astype(bf16), all_ref[...])
    wide_ref[...] = spread_rows[:, 0:256].astype(bf16)
    misc_t = spread_rows[:, 256:384].T
    gain = misc_t[MISC + 3 : MISC + 4] + misc_t[MISC + 4 : MISC + 5]
    conv_t = dot(misc_t.astype(bf16), selector())
    conv_taps = conv_t[MISC + 5 : MISC + 10] + conv_t[MISC + 10 : MISC + 15]
    ctap_ref[0:5, :] = conv_taps
    ctap_ref[5:8, :] = jnp.zeros((3, 256), f32)
    row_ref[0:1, :] = gain
    row_ref[1:8, :] = jnp.zeros((7, D), f32)
    for src, at, rows in ((halo_ref, 0, HALO), (hid_ref, HALO, T)):
        h = src[...].astype(f32)
        inv = lax.rsqrt(jnp.mean(h * h, axis=1, keepdims=True) + norm_eps)
        normed_ref[at : at + rows, :] = (h * inv * gain).astype(bf16)
    normed = normed_ref[...]
    v_ref[:, 0:384] = dot(normed, w_ref[:, 0:384])
    v_ref[:, 384:640] = dot(normed, wide_ref[...])
    raw = half(dot(normed[HALO:], w_ref[:, 512:640]))

    lane = lanes(T)
    pre = raw + head_row(hp_ref, 0)
    delta = jnp.where(
        lane < 3, jnp.maximum(pre, 0.0) + jnp.log1p(jnp.exp(-jnp.abs(pre))), 0.0
    )
    slope = jnp.where(lane < 3, sig(pre), 0.0)
    log_decay = -jnp.exp(head_row(hp_ref, 1)) * delta
    starts = column_of(st_ref)
    parts = three_parts(log_decay) + jnp.where(lane == 9, starts, 0.0)
    ri = lax.broadcasted_iota(jnp.int32, (T, T), 0)
    ci = lax.broadcasted_iota(jnp.int32, (T, T), 1)
    summed = dot(jnp.where(ri >= ci, 1.0, 0.0).astype(bf16), parts.astype(bf16))
    cum = joined(summed)
    segment = summed[:, 9:10]
    last = cum[T - 1 : T, :]
    last_segment = segment[T - 1 : T, :]
    keeper = jnp.where((lane < 3) & (segment == 0.0), jnp.exp(cum), 0.0)
    ending = jnp.where((lane < 3) & (segment == last_segment), jnp.exp(last - cum), 0.0)
    aux_ref[...] = (
        cum
        + rolled(delta, 3)
        + rolled(slope, 6)
        + jnp.where(lane == 9, segment, 0.0)
        + rolled(keeper, 10)
        + rolled(ending, 13)
    )

    valid = valid_masks(starts)
    for k in range(5):
        at = slice(128 * k, 128 * (k + 1))
        if k < 3:
            taps = tap_ref[0:5, at]
        else:
            taps = conv_taps[:, 128 * (k - 3) : 128 * (k - 2)]
        total = taps[4:5] + taps[3:4] * v_ref[HALO:, at]
        for lag in (1, 2, 3):
            total = total + taps[3 - lag : 4 - lag] * (
                v_ref[pl.ds(HALO - lag, T), at] * valid[lag - 1]
            )
        c_ref[:, at] = total

    act = act_tiles(c_ref)
    x = x_pair(*act[:3])
    weight = spread(ending * delta, 0)
    ended = jnp.concatenate([x[0] * weight[0], x[1] * weight[1]], axis=1).astype(bf16)
    state = dot(ended, act[3].astype(bf16), 0, 0)
    through = jnp.where(last_segment == 0.0, jnp.exp(last), 0.0)
    high = through.astype(bf16).astype(f32)
    lower = through - high
    sub = lax.broadcasted_iota(jnp.int32, (16, 128), 0)
    tail = jnp.zeros((16, 128), f32)
    for h in range(3):
        tail = jnp.where(sub == h, high[:, h : h + 1], tail)
        tail = jnp.where(sub == 3 + h, lower[:, h : h + 1], tail)
    body = state[0:192].astype(bf16)
    tail = tail.astype(bf16)
    for q in range(N_SEQ):
        send_ref[q, 0:192, :] = body
        send_ref[q, 192:SROWS, :] = tail


def own_kernel(c_ref, aux_ref, cot_ref, w_ref, hp_ref, y_ref, dn_ref, m_ref, mg_ref):
    act = act_tiles(c_ref)
    x = x_pair(*act[:3])
    aux = aux_ref[...]
    aux_t = aux.T
    scores = dot(act[4].astype(bf16), act[3].astype(bf16), 1, 1)
    ri = lax.broadcasted_iota(jnp.int32, (T, T), 0)
    ci = lax.broadcasted_iota(jnp.int32, (T, T), 1)
    allowed = (ri >= ci) & (aux[:, 9:10] == aux_t[9:10, :])
    mask = jnp.where(allowed, 0.0, LOW)
    delta = spread(aux, 3)
    fed = x[0] * delta[0], x[1] * delta[1]
    lo = lanes(T) < 64
    fed_h = (
        jnp.where(lo, fed[0], 0.0).astype(bf16),
        jnp.where(lo, 0.0, fed[0]).astype(bf16),
        fed[1].astype(bf16),
    )
    skip = skip_pair(hp_ref)
    y = [x[0] * skip[0], x[1] * skip[1]]
    for h in range(3):
        decay = jnp.exp(aux[:, h : h + 1] - aux_t[h : h + 1, :] + mask)
        m_ref[h] = decay.astype(bf16)
        mixing = (decay * scores).astype(bf16)
        mg_ref[h] = mixing
        y[h // 2] = y[h // 2] + dot(mixing, fed_h[h])
    y_ref[:, 0:128] = y[0]
    y_ref[:, 128:256] = y[1]
    back = dot(cot_ref[...], w_ref[:, 384:640])
    dn_ref[:, 0:128] = back[:, 0:128]
    dn_ref[:, 128:256] = jnp.where(lo, back[:, 128:256], 0.0)


def decay_rows(tail, shape=(192, 128)):
    both = tail[0:3] + tail[3:6]
    return jnp.concatenate(
        [jnp.broadcast_to(both[h : h + 1], (64, 128)) for h in range(3)], axis=0
    )


def enter_kernel(
    at_ref, got_ref, y0_ref, dn_ref, c_ref, aux_ref, tap_ref,
    y_ref, state_ref, stat_ref,
):
    here = at_ref[0]
    state = jnp.zeros((192, 128), f32)
    for q in range(N_SEQ - 1):
        through = decay_rows(got_ref[q, 192:SROWS, :].astype(f32))
        merged = through * state + got_ref[q, 0:192, :].astype(f32)
        state = jnp.where(q < here, merged, state)
    state_ref[0:192] = state
    state_ref[192:256] = jnp.zeros((64, 128), f32)
    c_mat = silu(c_ref[:, 512:640]).astype(bf16)
    carried = dot(c_mat, state_ref[...].astype(bf16), 1, 1)
    aux = aux_ref[...]
    keeper = spread(aux, 10)
    gate = gate_pair(*[silu(c_ref[:, 128 * k : 128 * (k + 1)]) for k in range(3)])
    squares = jnp.zeros((T, 1), f32)
    inner = jnp.zeros((T, 1), f32)
    for k in range(2):
        at = slice(128 * k, 128 * (k + 1))
        y = y0_ref[:, at] + keeper[k] * carried[:, at]
        y_ref[:, at] = y
        gated = y * gate[k]
        fed = gated * tap_ref[0:1, 384 + 128 * k : 512 + 128 * k]
        squares = squares + jnp.sum(gated * gated, axis=1, keepdims=True)
        inner = inner + jnp.sum(fed * dn_ref[:, at], axis=1, keepdims=True)
    lane = lanes(T)
    both = jnp.where(lane == 0, squares, jnp.where(lane == 1, inner, 0.0)).T
    stat_ref[...] = both[0:8]


def gated_kernel(
    s0_ref, s1_ref, s2_ref, s3_ref, y_ref, dn_ref, c_ref, aux_ref, tap_ref,
    dy_ref, dgate_ref, nout_ref, send_ref, rows_ref,
):
    total = s0_ref[...] + s1_ref[...] + s2_ref[...] + s3_ref[...]
    total = jnp.concatenate([total, jnp.zeros((120, T), f32)], axis=0).T
    rms = lax.rsqrt(total[:, 0:1] / DI + norm_eps)
    coef = rms * rms * rms * total[:, 1:2] / DI
    aux = aux_ref[...]
    keeper = spread(aux, 10)
    raw = gate_pair(*[c_ref[:, 128 * k : 128 * (k + 1)] for k in range(3)])
    x = x_pair(*[silu(c_ref[:, 128 * k : 128 * (k + 1)]) for k in range(3)])
    kept = []
    rows_ref[...] = jnp.zeros_like(rows_ref)
    for k in range(2):
        at = slice(128 * k, 128 * (k + 1))
        gain = tap_ref[0:1, 384 + 128 * k : 512 + 128 * k]
        s = sig(raw[k])
        gate = raw[k] * s
        y = y_ref[:, at]
        gated = y * gate
        dn = dn_ref[:, at]
        scaled = gated * rms
        nout_ref[:, at] = (scaled * gain).astype(bf16)
        d_gated = rms * gain * dn - gated * coef
        dy = d_gated * gate
        dy_ref[:, at] = dy
        dgate_ref[:, at] = d_gated * y * s * (1.0 + raw[k] * (1.0 - s))
        kept.append((dy * keeper[k]).astype(bf16))
        rows_ref[0:1, at] = jnp.sum(dn * scaled, axis=0, keepdims=True)
        rows_ref[1:2, at] = jnp.sum(dy * x[k], axis=0, keepdims=True)
    c_mat = silu(c_ref[:, 512:640]).astype(bf16)
    adj = dot(jnp.concatenate(kept, axis=1), c_mat, 0, 0)[0:192].astype(bf16)
    for q in range(N_SEQ):
        send_ref[q] = adj


def halves(ref, core):
    keep = ref[pl.ds(pl.multiple_of(core * 256, 256), 256), :]
    give = ref[pl.ds(pl.multiple_of(256 - core * 256, 256), 256), :]
    return keep.astype(bf16), give.astype(bf16)


def clear_edges(pad_ref):
    pad_ref[0:HALO] = jnp.zeros((HALO, 128), f32)
    pad_ref[HALO + T :] = jnp.zeros((HALO, 128), f32)


def conv_back(d_conv, taps, v_ref, at, valid, pad_ref):
    sums = [None, None, None, None, jnp.sum(d_conv, axis=0, keepdims=True)]
    sums[3] = jnp.sum(d_conv * v_ref[HALO:, at], axis=0, keepdims=True)
    pad_ref[HALO : HALO + T] = taps[3:4] * d_conv
    acc = pad_ref[0 : HALO + T]
    for lag in (1, 2, 3):
        masked = d_conv * valid[lag - 1]
        sums[3 - lag] = jnp.sum(
            masked * v_ref[pl.ds(HALO - lag, T), at], axis=0, keepdims=True
        )
        pad_ref[HALO : HALO + T] = taps[3 - lag : 4 - lag] * masked
        acc = acc + pad_ref[pl.ds(lag, HALO + T)]
    return acc, sums


def own_back_kernel(
    at_ref, dy_ref, y_ref, y0_ref, c_ref, aux_ref, m_ref, mg_ref, state_ref, nout_ref, w_ref,
    v_ref, ctap_ref, st_ref,
    dx_ref, db_ref, dcum_ref, xs_ref, b_ref, slope_ref, keep_ref, give_ref, dvc_ref, crow_ref,
    pad_ref, norm_ref,
):
    norm_ref[...] = dot(nout_ref[...], w_ref[:, 384:640], 1, 1)
    keep_ref[...], give_ref[...] = halves(norm_ref, at_ref[2])
    aux = aux_ref[...]
    aux_t = aux.T
    act = []
    for k in range(5):
        at = slice(128 * k, 128 * (k + 1))
        v = c_ref[:, at]
        s = sig(v)
        act.append(v * s)
        slope = s * (1.0 + v * (1.0 - s))
        if k < 4:
            slope_ref[:, at] = slope
    x = x_pair(*act[:3])
    xs_ref[:, 0:128] = x[0]
    xs_ref[:, 128:256] = x[1]
    b_ref[...] = act[3].astype(bf16)
    b_low, c_low = act[3].astype(bf16), act[4].astype(bf16)
    dy = pair_of(dy_ref)
    lo = lanes(T) < 64
    dy_h = (
        jnp.where(lo, dy[0], 0.0).astype(bf16),
        jnp.where(lo, 0.0, dy[0]).astype(bf16),
        dy[1].astype(bf16),
    )
    x_low = x[0].astype(bf16), x[1].astype(bf16)
    lane = lanes(T)
    dx = [jnp.zeros((T, 128), f32), jnp.zeros((T, 128), f32)]
    spread_sum = jnp.zeros((T, T), f32)
    rows = jnp.zeros((T, 128), f32)
    cols = jnp.zeros((128, T), f32)
    sub = lax.broadcasted_iota(jnp.int32, (128, T), 0)
    for h in range(3):
        pairs = dot(dy_h[h], x_low[h // 2], 1, 1) * aux_t[3 + h : 4 + h, :]
        mixing = mg_ref[h]
        spread_sum = spread_sum + pairs * m_ref[h].astype(f32)
        weights = pairs * mixing.astype(f32)
        rows = jnp.where(lane == h, jnp.sum(weights, axis=1, keepdims=True), rows)
        cols = jnp.where(sub == h, jnp.sum(weights, axis=0, keepdims=True), cols)
        dx[h // 2] = dx[h // 2] + dot(mixing, dy_h[h], 0, 0)
    low = spread_sum.astype(bf16)
    keeper = spread(aux, 10)
    kept = jnp.concatenate([dy[0] * keeper[0], dy[1] * keeper[1]], axis=1).astype(bf16)
    d_c = dot(low, b_low) + dot(kept, state_ref[...].astype(bf16))
    valid = valid_masks(column_of(st_ref))
    clear_edges(pad_ref)
    dv, sums = conv_back(d_c * slope, ctap_ref[0:5, 128:256], v_ref, slice(512, 640), valid, pad_ref)
    dvc_ref[...] = dv.astype(bf16)
    crow_ref[...] = jnp.concatenate([*sums, jnp.zeros((3, 128), f32)], axis=0)
    db_ref[...] = dot(low, c_low, 0, 0)
    dx_ref[:, 0:128] = dx[0]
    dx_ref[:, 128:256] = dx[1]
    carried = [
        dy[k] * (y_ref[:, 128 * k : 128 * (k + 1)] - y0_ref[:, 128 * k : 128 * (k + 1)])
        for k in range(2)
    ]
    dcum_ref[...] = rows - cols.T + head_sums(carried)


def back_kernel(
    at_ref, got_ref, fwd_ref, state_ref, dx_ref, db_ref, dcum_ref, xs_ref, b_ref, slope_ref,
    dvc_ref, crow_ref, aux_ref, v_ref, tap_ref, ctap_ref, hp_ref, st_ref, dy_ref, dgate_ref,
    w_ref, wide_ref, rows_ref, hid_ref, halo_ref,
    dv_ref, dstep_ref, keep_ref, give_ref, edge_ref, chan_ref, conv_ref, gain_ref,
    pad_ref, norm_ref,
):
    here = at_ref[0]
    adj = jnp.zeros((192, 128), f32)
    for q in range(N_SEQ - 1, 0, -1):
        through = decay_rows(fwd_ref[q, 192:SROWS, :].astype(f32))
        merged = through * adj + got_ref[q].astype(f32)
        adj = jnp.where(q > here, merged, adj)
    aux = aux_ref[...]
    lane = lanes(T)
    x = pair_of(xs_ref)
    b_low = b_ref[...]
    delta, ending = spread(aux, 3), spread(aux, 13)
    adj_low = jnp.concatenate([adj, jnp.zeros((64, 128), f32)], axis=0).astype(bf16)
    through_b = dot(b_low, adj_low, 1, 1)
    skip = skip_pair(hp_ref)
    dy = pair_of(dy_ref)
    ended, extra, full, d_x = [], [], [], []
    for k in range(2):
        at = slice(128 * k, 128 * (k + 1))
        late = ending[k] * through_b[:, at]
        total = dx_ref[:, at] + late
        d_x.append(delta[k] * total + skip[k] * dy[k])
        full.append(x[k] * total)
        extra.append(x[k] * late)
        ended.append(x[k] * delta[k] * ending[k])
    d_b = db_ref[...] + dot(jnp.concatenate(ended, axis=1).astype(bf16), adj_low)
    d_delta = head_sums(full)
    tail = head_sums(extra) * rolled(aux, -3)
    tail = jnp.where(lane < 3, tail, 0.0)
    d_cum = dcum_ref[...] - tail
    ri = lax.broadcasted_iota(jnp.int32, (T, T), 0)
    ci = lax.broadcasted_iota(jnp.int32, (T, T), 1)
    upper = jnp.where(ci >= ri, 1.0, 0.0).astype(bf16)
    d_log = joined(dot(upper, three_parts(d_cum).astype(bf16)))
    own = decay_rows(fwd_ref[here, 192:SROWS, :].astype(f32))
    met = own * adj * state_ref[0:192]
    lane1 = lanes(1)
    meets = jnp.zeros((1, 128), f32)
    for h in range(3):
        meets = jnp.where(lane1 == h, jnp.sum(met[64 * h : 64 * h + 64]), meets)
    d_log = d_log + jnp.sum(tail, axis=0, keepdims=True) + meets
    d_log = jnp.where(lane < 3, d_log, 0.0)
    rate = jnp.exp(head_row(hp_ref, 1))
    d_raw = (d_delta - rate * d_log) * rolled(aux, -6)
    d_raw = jnp.where(lane < 3, d_raw, 0.0)
    delta_cols = jnp.where(lane < 3, rolled(aux, -3), 0.0)
    step_low = half(d_raw).astype(bf16)
    dstep_ref[...] = step_low

    d_gate = pair_of(dgate_ref)
    x_tiles = head_tiles((jnp.zeros_like(d_x[0]),) * 2, d_x)
    gate_tiles = head_tiles(d_gate, (jnp.zeros_like(d_x[0]),) * 2)
    lo = lane < 64
    valid = valid_masks(column_of(st_ref))
    clear_edges(pad_ref)
    tap_rows = []
    for k in range(4):
        at = slice(128 * k, 128 * (k + 1))
        slope = slope_ref[:, at]
        if k < 3:
            d_conv = jnp.where(lo, gate_tiles[k], x_tiles[k] * slope)
            taps = tap_ref[0:5, at]
        else:
            d_conv = d_b * slope
            taps = ctap_ref[0:5, 0:128]
        dv, sums = conv_back(d_conv, taps, v_ref, at, valid, pad_ref)
        dv_ref[:, at] = dv.astype(bf16)
        tap_rows.append(sums)
    dv_ref[:, 512:640] = dvc_ref[...]
    tap_rows.append([crow_ref[j : j + 1, :] for j in range(5)])

    chan_ref_rows = []
    for j in range(5):
        pair = x_pair(*[tap_rows[k][j] for k in range(3)])
        chan_ref_rows.append(jnp.concatenate(pair, axis=1))
    chan_ref_rows.append(rows_ref[0:1, :])
    h0 = jnp.sum(d_raw, axis=0, keepdims=True)
    h1 = jnp.sum(d_log * (-rate) * delta_cols, axis=0, keepdims=True)
    h2 = head_sums((rows_ref[1:2, 0:128], rows_ref[1:2, 128:256]))
    zero = jnp.zeros((1, 128), f32)
    for r in (h0, h1, h2):
        chan_ref_rows.append(jnp.concatenate([r, zero], axis=1))
    for j, r in enumerate(chan_ref_rows):
        chan_ref[j : j + 1, :] = r
    chan_ref[9:16, :] = jnp.zeros((7, 256), f32)
    for j in range(5):
        conv_ref[j : j + 1, :] = jnp.concatenate([tap_rows[3][j], tap_rows[4][j]], axis=1)
    conv_ref[5:8, :] = jnp.zeros((3, 256), f32)

    d_norm = dot(dv_ref[:, 0:384], w_ref[:, 0:384], 1, 1)
    d_norm = d_norm + dot(dv_ref[:, 384:640], wide_ref[...], 1, 1)
    main = d_norm[HALO:] + dot(step_low, w_ref[:, 512:640], 1, 1)
    norm_ref[...] = main
    keep_ref[...], give_ref[...] = halves(norm_ref, at_ref[2])
    edge_ref[...] = d_norm[0:HALO].astype(bf16)
    total = jnp.zeros((1, D), f32)
    for src, val in ((halo_ref, d_norm[0:HALO]), (hid_ref, main)):
        h = src[...].astype(f32)
        inv = lax.rsqrt(jnp.mean(h * h, axis=1, keepdims=True) + norm_eps)
        total = total + jnp.sum(val * (h * inv), axis=0, keepdims=True)
    gain_ref[0:1] = total
    gain_ref[1:8] = jnp.zeros((7, D), f32)


def grad_kernel(
    normed_ref, dv_ref, dstep_ref, nout_ref, cot_ref, conv_ref, gain_ref, chan_ref, out_ref
):
    normed = normed_ref[...]
    out_ref[:, 0:384] = dot(normed, dv_ref[:, 0:384], 0, 0).astype(bf16)
    out_ref[:, 640:896] = dot(normed, dv_ref[:, 384:640], 0, 0).astype(bf16)
    outs = dot(cot_ref[...], nout_ref[...], 0, 0)
    out_ref[:, 384:512] = outs[:, 0:128].astype(bf16)
    tile = outs[:, 128:256] + dot(normed_ref[HALO:, :], dstep_ref[...], 0, 0)
    grads = jnp.concatenate([jnp.zeros((MISC + 5, 256), f32), conv_ref[0:5, :]], axis=0)
    grads = jnp.concatenate([grads, jnp.zeros((128 - MISC - 10, 256), f32)], axis=0)
    high = grads.astype(bf16)
    lower = (grads - high.astype(f32)).astype(bf16)
    sel = selector()
    tile = tile + dot(sel, high, 1, 1) + pltpu.roll(dot(sel, lower, 1, 1), 5, 1)
    gain = gain_ref[0:1]
    gain_high = gain.astype(bf16).astype(f32)
    sub = lax.broadcasted_iota(jnp.int32, (128, D), 0)
    column = jnp.where(
        sub == MISC + 3, gain_high, jnp.where(sub == MISC + 4, gain - gain_high, 0.0)
    ).T
    turned = jnp.concatenate([chan_ref[...], jnp.zeros((112, 256), f32)], axis=0).T
    turned = jnp.where(lanes(256) < 9, turned, 0.0)
    shared = jnp.zeros((48, 128), f32)
    for g in range(4):
        shared = shared + rolled(turned[48 * g : 48 * g + 48], MISC + 16 + 9 * g)
    tile = tile + column + jnp.concatenate([shared] * N_SEQ, axis=0)
    out_ref[:, 512:640] = tile.astype(bf16)


def pair_kernel(
    at_ref, keep_ref, got_ref, edge0_ref, edge1_ref, out_keep_ref, out_got_ref,
    own_ref, s1, s2, s3, sum_ref,
):
    sum_ref[:, 0:D] = keep_ref[...].astype(f32) + got_ref[...].astype(f32)
    sum_ref[256 - HALO :, 0:D] += edge0_ref[...].astype(f32) + edge1_ref[...].astype(f32)
    sum_ref[:, D:] = out_keep_ref[...].astype(f32) + out_got_ref[...].astype(f32)
    for by, ref in enumerate((own_ref, s1, s2, s3)):
        start = pl.multiple_of(lax.rem(at_ref[1] + by, 4) * 64, 64)
        ref[...] = sum_ref[pl.ds(start, 64), :].astype(bf16)


def four_kernel(at_ref, a_ref, b_ref, c_ref, d_ref, hid_ref, out_ref):
    total = a_ref[...].astype(f32) + b_ref[...].astype(f32)
    total = total + c_ref[...].astype(f32) + d_ref[...].astype(f32)
    start = pl.multiple_of((4 * at_ref[2] + at_ref[1]) * 64, 64)
    out_ref[:, 0:D] = total[:, 0:D].astype(bf16)
    out_ref[:, D:] = (total[:, D:] + hid_ref[pl.ds(start, 64), :].astype(f32)).astype(bf16)


def input_kernel(*refs):
    at_ref, refs = refs[0], refs[1:]
    hid_ref, cot_ref, row_ref, out_ref, block_ref = refs[8:]
    for side in range(2):
        core = at_ref[2] if side == 0 else 1 - at_ref[2]
        for by in range(4):
            block = core * 4 + lax.rem(at_ref[1] + 4 - by, 4)
            rows = pl.ds(pl.multiple_of(block * 64, 64), 64)
            piece = refs[4 * side + by]
            h = hid_ref[rows, :].astype(f32)
            inv = lax.rsqrt(jnp.mean(h * h, axis=1, keepdims=True) + norm_eps)
            d_scaled = piece[:, 0:D].astype(f32) * row_ref[0:1, :]
            inner = jnp.sum(d_scaled * h, axis=1, keepdims=True)
            out_ref[rows, :] = (
                cot_ref[rows, :].astype(f32)
                + inv * d_scaled
                - h * (inv * inv * inv * inner / D)
            )
            block_ref[rows, :] = piece[:, D:]


def adam(weight, grad, first, second, rate):
    first_new = beta_one * first + (1.0 - beta_one) * grad
    second_new = beta_two * second + (1.0 - beta_two) * grad * grad
    first_hat = first_new / (1.0 - beta_one**STEP)
    second_hat = second_new / (1.0 - beta_two**STEP)
    weight_new = weight - rate * (
        first_hat / (jnp.sqrt(second_hat) + adam_eps) + decay_rate * weight
    )
    return first_new, second_new, weight_new


RATE_D = 1.4 * D ** (-0.5)
RATE_I = 1.4 * DI ** (-0.5)


def put(refs, at, values):
    for ref, value in zip(refs, values):
        ref[at] = value


def update_kernel(*refs):
    grad_ref, refs = refs[0], refs[1:]
    proj, step, out, chan, head = (refs[3 * k : 3 * k + 3] for k in range(5))
    outs = refs[15:]
    proj_o, step_o, out_o, chan_o, head_o = (outs[3 * k : 3 * k + 3] for k in range(5))
    rest_ref = outs[15]
    total = grad_ref[0].astype(f32)
    for q in range(1, N_SEQ):
        total = total + grad_ref[q].astype(f32)
    misc = total[:, 512:640]
    rest_ref[...] = jnp.zeros_like(rest_ref)
    for h in range(N_HEAD):
        rest_ref[h, 0:6, 0:256] = total[6 * h : 6 * h + 6, 640:896]
        rest_ref[h, 0:6, 256:384] = misc[6 * h : 6 * h + 6]
    for h in range(3):
        w, m, v = (r[h] for r in proj)
        put(proj_o, h, adam(w, total[:, 128 * h : 128 * (h + 1)], m, v, RATE_D))
        tile = total[:, 384 + 128 * (h // 2) : 512 + 128 * (h // 2)]
        tile = half(tile) if h == 1 else tile
        w, m, v = (r[h] for r in out)
        put(out_o, h, adam(w, tile[:, 0:64], m, v, RATE_I))
    turned = jnp.concatenate([misc, jnp.zeros((80, 128), f32)], axis=0).T
    at = (slice(None), slice(None))
    w, m, v = (r[at] for r in step)
    put(step_o, at, adam(w, turned[MISC : MISC + 3, 0:48], m, v, RATE_D))
    first = MISC + 16
    p = [turned[first + 9 * g : first + 9 * g + 9] for g in range(4)]
    lane = lanes(9)
    wrapped = rolled(p[2], 96)
    pair = (
        p[0] + rolled(p[1], 48) + jnp.where(lane >= 96, wrapped, 0.0),
        jnp.where(lane < 16, wrapped, 0.0) + rolled(p[3], 16),
    )
    for h in range(3):
        piece = half(pair[0]) if h == 1 else pair[h // 2]
        at = (slice(None), h, slice(None))
        w, m, v = (r[at] for r in chan)
        put(chan_o, at, adam(w, piece[0:6, 0:64], m, v, 0.5))
    at = (slice(None), slice(None))
    w, m, v = (r[at] for r in head)
    put(head_o, at, adam(w, pair[0][6:9, 0:3], m, v, 1.0))


def rest_kernel(*refs):
    got_ref, refs = refs[0], refs[1:]
    shared, gain, conv = (refs[3 * k : 3 * k + 3] for k in range(3))
    outs = refs[9:]
    shared_o, gain_o, conv_o = (outs[3 * k : 3 * k + 3] for k in range(3))
    total = got_ref[0]
    for q in range(1, N_HEAD):
        total = total + got_ref[q]
    at = (slice(None), slice(None))
    w, m, v = (r[at] for r in shared)
    put(shared_o, at, adam(w, total[0:6, 0:256], m, v, RATE_D))
    column = total[:, 256 + MISC + 3 : 256 + MISC + 4] + total[:, 256 + MISC + 4 : 256 + MISC + 5]
    sub = lax.broadcasted_iota(jnp.int32, (8, 128), 0)
    row = jnp.sum(jnp.where(sub == lanes(8), column, 0.0), axis=0, keepdims=True)
    w, m, v = (r[at] for r in gain)
    put(gain_o, at, adam(w, row[:, 0:6], m, v, 0.5))
    tile = total[0:2, 256:384]
    both = rolled(tile, -(MISC + 5)) + rolled(tile, -(MISC + 10))
    w, m, v = (r[at] for r in conv)
    put(conv_o, at, adam(w, both[:, 0:5], m, v, 0.5))


def exchange(blocks, axis):
    return lax.all_to_all(blocks, axis, 0, 0, tiled=True)


def around(a, axis, by):
    peers = lax.axis_size(axis)
    return lax.ppermute(a, axis, [(i, (i + by) % peers) for i in range(peers)])


def to_next(a):
    return lax.ppermute(a, SEQ, [(i, i + 1) for i in range(N_SEQ - 1)])


def to_previous(a, core):
    pairs = [(2 * i + 2 + core, 2 * i + 1) for i in range(N_SEQ - 1)]
    return lax.ppermute(a, SEQ + ("head_1",), pairs)


def body(
    hidden_in, cotangent, doc_starts, proj_weight, step_weight, out_weight, shared_weight,
    pre_gain, channel_params, head_params, shared_conv, proj_first, proj_second, step_first,
    step_second, out_first, out_second, shared_first, shared_second, gain_first, gain_second,
    channel_first, channel_second, head_first, head_second, conv_first, conv_second,
):
    where = jnp.stack(
        [lax.axis_index(SEQ), lax.axis_index("head_0"), lax.axis_index("head_1")]
    ).astype(jnp.int32)
    halo = to_next(hidden_in[T - HALO :])
    matrices = [jnp.transpose(a, (1, 0, 2)) for a in (proj_weight, proj_first, proj_second)]
    steps = [a.T for a in (step_weight, step_first, step_second)]
    out_weights = [jnp.transpose(a, (0, 2, 1)) for a in (out_weight, out_first, out_second)]
    gains_in = [a.reshape(1, 6) for a in (pre_gain, gain_first, gain_second)]

    (pack,) = call(
        pack_kernel, [((N_SEQ, 48, NW), bf16)],
        matrices[0], out_weights[0], steps[0], shared_weight, gains_in[0], shared_conv,
        scratch=[pltpu.VMEM((128, 128), f32), pltpu.VMEM((48, 128), f32)], name="pack",
    )
    weights = exchange(pack, SEQ).reshape(D, NW)
    (slab,) = call(slab_kernel, [((96, 384), bf16)], weights, name="slab")
    near = [slab] + [around(slab, "head_0", by) for by in (1, 2, 3)]
    slabs = near + [around(a, "head_1", 1) for a in near]

    marks = doc_starts.astype(f32).reshape(1, T)
    fixed = jnp.broadcast_to(
        (jnp.arange(6) == 3).astype(f32)[:, None, None], channel_params.shape
    )
    taps = jnp.concatenate([fixed, channel_params], axis=2).reshape(6, 384)
    gains = jnp.pad(channel_params[5].reshape(1, 192), ((0, 5), (0, 64)))
    taps = jnp.pad(jnp.concatenate([taps, gains], axis=1), ((0, 2), (0, 0)))

    normed, values, conv, aux, sent, row, wide, conv_taps = call(
        first_kernel,
        [
            ((HALO + T, D), bf16), ((HALO + T, NV), f32), ((T, NV), f32), ((T, 128), f32),
            ((N_SEQ, SROWS, 128), bf16), ((8, D), f32), ((D, 256), bf16), ((8, 256), f32),
        ],
        where, *slabs, hidden_in, halo, marks, weights, taps, head_params, smem=(0, 14),
        scratch=[pltpu.VMEM((D, 384), bf16)], name="first",
    )
    states = exchange(sent, SEQ)
    y_own, d_normed, decays, mixing = call(
        own_kernel,
        [((T, 256), f32), ((T, 256), f32), ((3, T, T), bf16), ((3, T, T), bf16)],
        conv, aux, cotangent, weights, head_params, smem=(4,), name="own",
    )
    y_full, state, stat = call(
        enter_kernel,
        [((T, 256), f32), ((256, 128), f32), ((8, T), f32)],
        where, states, y_own, d_normed, conv, aux, taps, smem=(0,), name="enter",
    )
    stat = stat + around(stat, "head_1", 1)
    stats = [stat] + [around(stat, "head_0", by) for by in (1, 2, 3)]
    d_y, d_gate, normed_out, sent_adj, rows = call(
        gated_kernel,
        [
            ((T, 256), f32), ((T, 256), f32), ((T, 256), bf16),
            ((N_SEQ, 192, 128), bf16), ((8, 256), f32),
        ],
        *stats, y_full, d_normed, conv, aux, taps, name="gated",
    )
    adjoints = exchange(sent_adj, SEQ)
    half_rows = ((T // 2, D), bf16)
    (
        d_x, d_b, d_cum, x_act, b_act, slopes, out_keep, out_give, d_value_c, c_rows
    ) = call(
        own_back_kernel,
        [
            ((T, 256), f32), ((T, 128), f32), ((T, 128), f32), ((T, 256), f32),
            ((T, 128), bf16), ((T, 512), f32), half_rows, half_rows,
            ((HALO + T, 128), bf16), ((8, 128), f32),
        ],
        where, d_y, y_full, y_own, conv, aux, decays, mixing, state, normed_out, weights,
        values, conv_taps, marks, smem=(0,),
        scratch=[pltpu.VMEM((T + 2 * HALO, 128), f32), pltpu.VMEM((T, D), f32)],
        name="own_back",
    )
    out_taken = around(out_give, "head_1", 1)
    d_values, d_step, keep, give, edge, chan, d_conv, d_gain = call(
        back_kernel,
        [
            ((HALO + T, NV), bf16), ((T, 128), bf16), half_rows, half_rows,
            ((HALO, D), bf16), ((16, 256), f32), ((8, 256), f32), ((8, D), f32),
        ],
        where, adjoints, states, state, d_x, d_b, d_cum, x_act, b_act, slopes, d_value_c,
        c_rows, aux, values, taps, conv_taps, head_params, marks, d_y, d_gate, weights, wide,
        rows, hidden_in, halo,
        smem=(0, 16),
        scratch=[pltpu.VMEM((T + 2 * HALO, 128), f32), pltpu.VMEM((T, D), f32)],
        name="back",
    )
    taken = around(give, "head_1", 1)
    edges = [to_previous(edge, core) for core in range(2)]
    (grads,) = call(
        grad_kernel, [((D, NG), bf16)],
        normed, d_values, d_step, normed_out, cotangent, d_conv, d_gain, chan, name="grad",
    )
    grads = exchange(grads.reshape(N_SEQ, 48, NG), SEQ)

    piece = ((T // N_HEAD, 2 * D), bf16)
    pieces = call(
        pair_kernel, [piece] * 4, where, keep, taken, *edges, out_keep, out_taken,
        smem=(0,), scratch=[pltpu.VMEM((T // 2, 2 * D), f32)], name="pair",
    )
    parts = [pieces[0]] + [around(pieces[by], "head_0", by) for by in (1, 2, 3)]
    (own,) = call(four_kernel, [piece], where, *parts, hidden_in, smem=(0,), name="four")
    near = [own] + [around(own, "head_0", by) for by in (1, 2, 3)]
    far = [around(a, "head_1", 1) for a in near]
    input_grad, block_out = call(
        input_kernel, [((T, D), f32), ((T, D), bf16)], where, *near, *far, hidden_in, cotangent, row,
        smem=(0,), name="input",
    )

    proj, step, out = (3, 48, 128), (3, 48), (3, 48, 64)
    shapes = [proj] * 3 + [step] * 3 + [out] * 3 + [(6, 3, 64)] * 3 + [(3, 3)] * 3
    updated = call(
        update_kernel,
        [(s, f32) for s in shapes] + [((N_HEAD, 8, 384), f32)],
        grads, *matrices, *steps, *out_weights, channel_params, channel_first,
        channel_second, head_params, head_first, head_second, name="update",
    )
    rest = exchange(updated[15], HEAD)
    shared = call(
        rest_kernel,
        [(s, f32) for s in [(6, 256)] * 3 + [(1, 6)] * 3 + [(2, 5)] * 3],
        rest, shared_weight, shared_first, shared_second, *gains_in, shared_conv, conv_first,
        conv_second, name="rest",
    )
    return (
        block_out, input_grad,
        *(jnp.transpose(a, (1, 0, 2)) for a in updated[0:3]),
        *(a.T for a in updated[3:6]),
        *(jnp.transpose(a, (0, 2, 1)) for a in updated[6:9]),
        *shared[0:3],
        *(g.reshape(6) for g in shared[3:6]),
        *updated[9:15],
        *shared[6:9],
    )


def solution(mesh):
    finer = Mesh(mesh.devices.reshape(4, 4, 4, 2), SEQ_HEAD)
    matrix = P(SEQ, HEAD, None)
    step = P(SEQ, HEAD)
    out = P(HEAD, None, SEQ)
    both = P(SEQ_HEAD, None)
    gain = P(SEQ_HEAD)
    channel = P(None, HEAD, None)
    head = P(None, HEAD)
    tokens = P(SEQ, None)
    return jax.shard_map(
        body,
        mesh=finer,
        in_specs=(
            tokens, tokens, P(SEQ), matrix, step, out, both, gain, channel, head, both,
            matrix, matrix, step, step, out, out, both, both, gain, gain, channel, channel,
            head, head, both, both,
        ),
        out_specs=(
            (tokens, tokens)
            + (matrix,) * 3 + (step,) * 3 + (out,) * 3 + (both,) * 3 + (gain,) * 3
            + (channel,) * 3 + (head,) * 3 + (both,) * 3
        ),
        check_vma=False,
    )
```

```python
import functools

import jax
import jax.numpy as jnp
from jax import lax
from jax.experimental import pallas as pl
from jax.experimental.pallas import tpu as pltpu
from jax.sharding import Mesh
from jax.sharding import PartitionSpec as P

D = 768
DI = 1536
STEP = 10
SEQ = ("seq_0", "seq_1")
HEAD = ("head_0", "head_1")
SEQ_HEAD = SEQ + HEAD
N_SEQ = 16
N_HEAD = 8

T = 512
HALO = 16
NV = 640
NW = 640
NG = 896
MISC = 64
SLAB = 96
SROWS = 208

f32 = jnp.float32
bf16 = jnp.bfloat16
norm_eps = 1e-05
beta_one = 0.9
beta_two = 0.999
adam_eps = 1e-08
decay_rate = 0.01
LOW = -1e30

PARAMS = pltpu.CompilerParams(vmem_limit_bytes=32 * 1024 * 1024)
VM = pl.BlockSpec(memory_space=pltpu.VMEM)
SM = pl.BlockSpec(memory_space=pltpu.SMEM)


def call(kernel, outs, *args, smem=(), scratch=(), name=None):
    return pl.pallas_call(
        kernel,
        out_shape=[jax.ShapeDtypeStruct(s, d) for s, d in outs],
        in_specs=[SM if i in smem else VM for i in range(len(args))],
        out_specs=[VM] * len(outs),
        scratch_shapes=list(scratch),
        compiler_params=PARAMS,
        name=name,
    )(*args)


def dot(a, b, ca=1, cb=0):
    return lax.dot_general(a, b, (((ca,), (cb,)), ((), ())), preferred_element_type=f32)


def lanes(rows):
    return lax.broadcasted_iota(jnp.int32, (rows, 128), 1)


def half(v):
    return pltpu.roll(v, 64, 1)


def rolled(v, by):
    return pltpu.roll(v, by % 128, 1)


def sig(v):
    return 1.0 / (1.0 + jnp.exp(-v))


def silu(v):
    return v * sig(v)


def dsilu(v):
    s = sig(v)
    return s * (1.0 + v * (1.0 - s))


def gate_pair(t0, t1, t2):
    lo = lanes(t0.shape[0]) < 64
    return jnp.where(lo, t0, half(t1)), jnp.where(lo, t2, 0.0)


def x_pair(t0, t1, t2):
    lo = lanes(t0.shape[0]) < 64
    return jnp.where(lo, half(t0), t1), jnp.where(lo, half(t2), 0.0)


def head_tiles(gate, x):
    lo = lanes(gate[0].shape[0]) < 64
    return (
        jnp.where(lo, gate[0], half(x[0])),
        jnp.where(lo, half(gate[0]), x[0]),
        jnp.where(lo, gate[1], half(x[1])),
    )


def spread(a, at):
    lo = lanes(a.shape[0]) < 64
    return (
        jnp.where(lo, a[:, at : at + 1], a[:, at + 1 : at + 2]),
        jnp.where(lo, a[:, at + 2 : at + 3], 0.0),
    )


def head_sums(pair):
    a, b = pair
    lane = lanes(a.shape[0])
    s0 = jnp.sum(jnp.where(lane < 64, a, 0.0), axis=1, keepdims=True)
    s1 = jnp.sum(jnp.where(lane < 64, 0.0, a), axis=1, keepdims=True)
    s2 = jnp.sum(b, axis=1, keepdims=True)
    return jnp.where(lane == 0, s0, jnp.where(lane == 1, s1, jnp.where(lane == 2, s2, 0.0)))


def pair_of(ref):
    return ref[:, 0:128], ref[:, 128:256]


def head_row(hp_ref, k, rows=1):
    lane = lanes(rows)
    return jnp.where(
        lane == 0,
        hp_ref[k, 0],
        jnp.where(lane == 1, hp_ref[k, 1], jnp.where(lane == 2, hp_ref[k, 2], 0.0)),
    )


def skip_pair(hp_ref):
    lane = lanes(1)
    return (
        jnp.where(lane < 64, hp_ref[2, 0], hp_ref[2, 1]),
        jnp.where(lane < 64, hp_ref[2, 2], 0.0),
    )


def three_parts(v):
    hi = v.astype(bf16).astype(f32)
    rest = v - hi
    mid = rest.astype(bf16).astype(f32)
    return hi + rolled(mid, 3) + rolled(rest - mid, 6)


def joined(v):
    total = v + rolled(v, -3) + rolled(v, -6)
    return jnp.where(lanes(v.shape[0]) < 3, total, 0.0)


def act_tiles(c_ref):
    return [silu(c_ref[:, 128 * k : 128 * (k + 1)]) for k in range(5)]


def valid_masks(starts_col):
    row = lax.broadcasted_iota(jnp.int32, starts_col.shape, 0)
    one = jnp.where(row < 1, 0.0, pltpu.roll(starts_col, 1, 0))
    two = jnp.where(row < 2, 0.0, pltpu.roll(starts_col, 2, 0))
    first = 1.0 - starts_col
    return first, first - one, first - one - two


def column_of(row_ref):
    return jnp.broadcast_to(row_ref[0:1, :], (128, T)).T


def selector():
    r = lax.broadcasted_iota(jnp.int32, (D, 256), 0)
    k = lax.broadcasted_iota(jnp.int32, (D, 256), 1)
    h = jnp.bitwise_and(jnp.right_shift(k, 1), 7)
    at = 48 * jnp.right_shift(k, 4) + 6 * h + jnp.bitwise_and(k, 1)
    return jnp.where(r == at, 1.0, 0.0).astype(bf16)


def slab_rows(a):
    s = jnp.right_shift(a * 43, 8)
    return 42 * s + a


def pack_kernel(
    proj_ref, outw_ref, step_ref, shared_ref, gain_ref, conv_ref, pack_ref, misc_ref, wide_ref
):
    misc_ref[...] = jnp.zeros_like(misc_ref)
    misc_ref[0:3, 0:48] = step_ref[...]
    misc_ref[0:48, :] = half(misc_ref[...].T)[0:48]
    wide_ref[...] = jnp.zeros_like(wide_ref)
    wide_ref[0:1, 0:6] = gain_ref[...]
    sub = lax.broadcasted_iota(jnp.int32, (6, 128), 0)
    lane = lanes(6)
    column = jnp.sum(jnp.where(sub == lane, wide_ref[0:1, :], 0.0), axis=1, keepdims=True)
    high = column.astype(bf16).astype(f32)
    misc_ref[0:6, :] += jnp.where(lane == MISC + 3, high, 0.0) + jnp.where(
        lane == MISC + 4, column - high, 0.0
    )
    conv = conv_ref[...]
    high = conv.astype(bf16).astype(f32)
    misc_ref[0:2, MISC + 5 : MISC + 10] = high
    misc_ref[0:2, MISC + 10 : MISC + 15] = conv - high
    for j in range(8):
        tile = rolled(shared_ref[:, 128 * (j // 4) : 128 * (j // 4) + 128], SLAB - 32 * (j % 4))
        misc_ref[6 * j : 6 * j + 6, :] += jnp.where(lane >= SLAB, tile, 0.0)
    misc = misc_ref[0:48, :]
    lo = lanes(48) < 64
    wide = []
    for h in range(3):
        wide_ref[:, 0:64] = outw_ref[h]
        wide.append(wide_ref[...])
    tiles = [proj_ref[h] for h in range(3)]
    tiles += [jnp.where(lo, wide[0], half(wide[1])), jnp.where(lo, wide[2], misc)]
    for k, tile in enumerate(tiles):
        low = tile.astype(bf16)
        for q in range(N_SEQ):
            pack_ref[q, :, 128 * k : 128 * (k + 1)] = low


def slab_kernel(w_ref, slab_ref):
    misc = w_ref[:, 512:640]
    a = lax.broadcasted_iota(jnp.int32, (96, D), 0)
    d = lax.broadcasted_iota(jnp.int32, (96, D), 1)
    gap = d - slab_rows(a)
    lane = lanes(96)
    tiles = [jnp.zeros((96, 128), f32)] * 2
    for j in range(8):
        got = dot(jnp.where(gap == 6 * j, 1.0, 0.0).astype(bf16), misc)
        if j == 0:
            slab_ref[:, 256:384] = jnp.where(lane < SLAB, got, 0.0).astype(bf16)
        own = jnp.where(lane >= SLAB, got, 0.0)
        tiles[j // 4] = tiles[j // 4] + rolled(own, 32 * (j % 4) - SLAB)
    slab_ref[:, 0:128] = tiles[0].astype(bf16)
    slab_ref[:, 128:256] = tiles[1].astype(bf16)


def first_kernel(*refs):
    at_ref, slabs, refs = refs[0], refs[1:9], refs[9:]
    hid_ref, halo_ref, st_ref, w_ref, tap_ref, hp_ref = refs[:6]
    normed_ref, v_ref, c_ref, aux_ref, send_ref, row_ref, wide_ref, ctap_ref = refs[6:14]
    all_ref = refs[14]
    d = lax.broadcasted_iota(jnp.int32, (D, 96), 0)
    a = lax.broadcasted_iota(jnp.int32, (D, 96), 1)
    gap = d - slab_rows(a)
    picks = []
    for b in range(8):
        core = at_ref[2] if b < 4 else 1 - at_ref[2]
        head = 2 * lax.rem(at_ref[1] + 4 - b % 4, 4) + core
        all_ref[96 * b : 96 * b + 96, :] = slabs[b][...]
        picks.append(jnp.where(gap == 6 * head, 1.0, 0.0))
    spread_rows = dot(jnp.concatenate(picks, axis=1).astype(bf16), all_ref[...])
    wide_ref[...] = spread_rows[:, 0:256].astype(bf16)
    misc_t = spread_rows[:, 256:384].T
    gain = misc_t[MISC + 3 : MISC + 4] + misc_t[MISC + 4 : MISC + 5]
    conv_t = dot(misc_t.astype(bf16), selector())
    conv_taps = conv_t[MISC + 5 : MISC + 10] + conv_t[MISC + 10 : MISC + 15]
    ctap_ref[0:5, :] = conv_taps
    ctap_ref[5:8, :] = jnp.zeros((3, 256), f32)
    row_ref[0:1, :] = gain
    row_ref[1:8, :] = jnp.zeros((7, D), f32)
    for src, at, rows in ((halo_ref, 0, HALO), (hid_ref, HALO, T)):
        h = src[...].astype(f32)
        inv = lax.rsqrt(jnp.mean(h * h, axis=1, keepdims=True) + norm_eps)
        normed_ref[at : at + rows, :] = (h * inv * gain).astype(bf16)
    normed = normed_ref[...]
    v_ref[:, 0:384] = dot(normed, w_ref[:, 0:384])
    v_ref[:, 384:640] = dot(normed, wide_ref[...])
    raw = half(dot(normed[HALO:], w_ref[:, 512:640]))

    lane = lanes(T)
    pre = raw + head_row(hp_ref, 0)
    delta = jnp.where(
        lane < 3, jnp.maximum(pre, 0.0) + jnp.log1p(jnp.exp(-jnp.abs(pre))), 0.0
    )
    slope = jnp.where(lane < 3, sig(pre), 0.0)
    log_decay = -jnp.exp(head_row(hp_ref, 1)) * delta
    starts = column_of(st_ref)
    parts = three_parts(log_decay) + jnp.where(lane == 9, starts, 0.0)
    ri = lax.broadcasted_iota(jnp.int32, (T, T), 0)
    ci = lax.broadcasted_iota(jnp.int32, (T, T), 1)
    summed = dot(jnp.where(ri >= ci, 1.0, 0.0).astype(bf16), parts.astype(bf16))
    cum = joined(summed)
    segment = summed[:, 9:10]
    last = cum[T - 1 : T, :]
    last_segment = segment[T - 1 : T, :]
    keeper = jnp.where((lane < 3) & (segment == 0.0), jnp.exp(cum), 0.0)
    ending = jnp.where((lane < 3) & (segment == last_segment), jnp.exp(last - cum), 0.0)
    aux_ref[...] = (
        cum
        + rolled(delta, 3)
        + rolled(slope, 6)
        + jnp.where(lane == 9, segment, 0.0)
        + rolled(keeper, 10)
        + rolled(ending, 13)
    )

    valid = valid_masks(starts)
    for k in range(5):
        at = slice(128 * k, 128 * (k + 1))
        if k < 3:
            taps = tap_ref[0:5, at]
        else:
            taps = conv_taps[:, 128 * (k - 3) : 128 * (k - 2)]
        total = taps[4:5] + taps[3:4] * v_ref[HALO:, at]
        for lag in (1, 2, 3):
            total = total + taps[3 - lag : 4 - lag] * (
                v_ref[pl.ds(HALO - lag, T), at] * valid[lag - 1]
            )
        c_ref[:, at] = total

    act = act_tiles(c_ref)
    x = x_pair(*act[:3])
    weight = spread(ending * delta, 0)
    ended = jnp.concatenate([x[0] * weight[0], x[1] * weight[1]], axis=1).astype(bf16)
    state = dot(ended, act[3].astype(bf16), 0, 0)
    through = jnp.where(last_segment == 0.0, jnp.exp(last), 0.0)
    high = through.astype(bf16).astype(f32)
    lower = through - high
    sub = lax.broadcasted_iota(jnp.int32, (16, 128), 0)
    tail = jnp.zeros((16, 128), f32)
    for h in range(3):
        tail = jnp.where(sub == h, high[:, h : h + 1], tail)
        tail = jnp.where(sub == 3 + h, lower[:, h : h + 1], tail)
    send_ref[0:192, :] = state[0:192].astype(bf16)
    send_ref[192:SROWS, :] = tail.astype(bf16)


def own_kernel(c_ref, aux_ref, cot_ref, w_ref, hp_ref, y_ref, dn_ref, m_ref, mg_ref):
    act = act_tiles(c_ref)
    x = x_pair(*act[:3])
    aux = aux_ref[...]
    aux_t = aux.T
    scores = dot(act[4].astype(bf16), act[3].astype(bf16), 1, 1)
    ri = lax.broadcasted_iota(jnp.int32, (T, T), 0)
    ci = lax.broadcasted_iota(jnp.int32, (T, T), 1)
    allowed = (ri >= ci) & (aux[:, 9:10] == aux_t[9:10, :])
    mask = jnp.where(allowed, 0.0, LOW)
    delta = spread(aux, 3)
    fed = x[0] * delta[0], x[1] * delta[1]
    lo = lanes(T) < 64
    fed_h = (
        jnp.where(lo, fed[0], 0.0).astype(bf16),
        jnp.where(lo, 0.0, fed[0]).astype(bf16),
        fed[1].astype(bf16),
    )
    skip = skip_pair(hp_ref)
    y = [x[0] * skip[0], x[1] * skip[1]]
    for h in range(3):
        decay = jnp.exp(aux[:, h : h + 1] - aux_t[h : h + 1, :] + mask)
        m_ref[h] = decay.astype(bf16)
        mixing = (decay * scores).astype(bf16)
        mg_ref[h] = mixing
        y[h // 2] = y[h // 2] + dot(mixing, fed_h[h])
    y_ref[:, 0:128] = y[0]
    y_ref[:, 128:256] = y[1]
    back = dot(cot_ref[...], w_ref[:, 384:640])
    dn_ref[:, 0:128] = back[:, 0:128]
    dn_ref[:, 128:256] = jnp.where(lo, back[:, 128:256], 0.0)


def decay_rows(tail):
    both = tail[0:3] + tail[3:6]
    return jnp.concatenate(
        [jnp.broadcast_to(both[h : h + 1], (64, 128)) for h in range(3)], axis=0
    )


def in_place(here, refs, rows):
    pieces = [r[rows, :].astype(f32) for r in refs]
    placed = []
    for p in range(4):
        by = lax.rem(here + 4 - p, 4)
        piece = pieces[0]
        for k in (1, 2, 3):
            piece = jnp.where(by == k, pieces[k], piece)
        placed.append(piece)
    return placed


def fold(here, states, tails, reverse):
    total = entering = jnp.zeros((192, 128), f32)
    passed = whole = jnp.ones((192, 128), f32)
    for p in reversed(range(4)) if reverse else range(4):
        decay = decay_rows(tails[p])
        before = (p > here) if reverse else (p < here)
        total = decay * total + states[p]
        entering = jnp.where(before, total, entering)
        passed = jnp.where(before, passed * decay, passed)
        whole = whole * decay
    return total, entering, passed, whole


def group_kernel(at_ref, a_ref, b_ref, c_ref, d_ref, send_ref, own_ref, passed_ref, tail_ref):
    here = lax.rem(at_ref[0], 4)
    refs = (a_ref, b_ref, c_ref, d_ref)
    states = in_place(here, refs, slice(0, 192))
    tails = in_place(here, refs, slice(192, SROWS))
    total, entering, passed, whole = fold(here, states, tails, False)
    own_ref[...] = entering
    passed_ref[...] = passed
    send_ref[0:192, :] = total.astype(bf16)
    sub = lax.broadcasted_iota(jnp.int32, (16, 128), 0)
    tail = jnp.zeros((16, 128), f32)
    for h in range(3):
        row = whole[64 * h : 64 * h + 1]
        high = row.astype(bf16).astype(f32)
        tail = jnp.where(sub == h, high, tail)
        tail = jnp.where(sub == 3 + h, row - high, tail)
    send_ref[192:SROWS, :] = tail.astype(bf16)
    for p in range(4):
        tail_ref[16 * p : 16 * p + 16, :] = tails[p]


def group_back_kernel(at_ref, a_ref, b_ref, c_ref, d_ref, tail_ref, send_ref, own_ref, passed_ref):
    here = lax.rem(at_ref[0], 4)
    states = in_place(here, (a_ref, b_ref, c_ref, d_ref), slice(0, 192))
    tails = [tail_ref[16 * p : 16 * p + 16, :] for p in range(4)]
    total, entering, passed, _ = fold(here, states, tails, True)
    own_ref[...] = entering
    passed_ref[...] = passed
    send_ref[...] = total.astype(bf16)


def enter_kernel(
    at_ref, s0_ref, s1_ref, s2_ref, s3_ref, own_ref, passed_ref, y0_ref, dn_ref, c_ref,
    aux_ref, tap_ref, y_ref, state_ref, stat_ref, tail_ref,
):
    here = jnp.right_shift(at_ref[0], 2)
    refs = (s0_ref, s1_ref, s2_ref, s3_ref)
    states = in_place(here, refs, slice(0, 192))
    tails = in_place(here, refs, slice(192, SROWS))
    for p in range(4):
        tail_ref[16 * p : 16 * p + 16, :] = tails[p]
    _, entering, _, _ = fold(here, states, tails, False)
    state = passed_ref[...] * entering + own_ref[...]
    state_ref[0:192] = state
    state_ref[192:256] = jnp.zeros((64, 128), f32)
    c_mat = silu(c_ref[:, 512:640]).astype(bf16)
    carried = dot(c_mat, state_ref[...].astype(bf16), 1, 1)
    aux = aux_ref[...]
    keeper = spread(aux, 10)
    gate = gate_pair(*[silu(c_ref[:, 128 * k : 128 * (k + 1)]) for k in range(3)])
    squares = jnp.zeros((T, 1), f32)
    inner = jnp.zeros((T, 1), f32)
    for k in range(2):
        at = slice(128 * k, 128 * (k + 1))
        y = y0_ref[:, at] + keeper[k] * carried[:, at]
        y_ref[:, at] = y
        gated = y * gate[k]
        fed = gated * tap_ref[0:1, 384 + 128 * k : 512 + 128 * k]
        squares = squares + jnp.sum(gated * gated, axis=1, keepdims=True)
        inner = inner + jnp.sum(fed * dn_ref[:, at], axis=1, keepdims=True)
    lane = lanes(T)
    both = jnp.where(lane == 0, squares, jnp.where(lane == 1, inner, 0.0)).T
    stat_ref[...] = both[0:8]


def gated_kernel(
    s0_ref, s1_ref, s2_ref, s3_ref, y_ref, dn_ref, c_ref, aux_ref, tap_ref,
    dy_ref, dgate_ref, nout_ref, send_ref, rows_ref,
):
    total = s0_ref[...] + s1_ref[...] + s2_ref[...] + s3_ref[...]
    total = jnp.concatenate([total, jnp.zeros((120, T), f32)], axis=0).T
    rms = lax.rsqrt(total[:, 0:1] / DI + norm_eps)
    coef = rms * rms * rms * total[:, 1:2] / DI
    aux = aux_ref[...]
    keeper = spread(aux, 10)
    raw = gate_pair(*[c_ref[:, 128 * k : 128 * (k + 1)] for k in range(3)])
    x = x_pair(*[silu(c_ref[:, 128 * k : 128 * (k + 1)]) for k in range(3)])
    kept = []
    rows_ref[...] = jnp.zeros_like(rows_ref)
    for k in range(2):
        at = slice(128 * k, 128 * (k + 1))
        gain = tap_ref[0:1, 384 + 128 * k : 512 + 128 * k]
        s = sig(raw[k])
        gate = raw[k] * s
        y = y_ref[:, at]
        gated = y * gate
        dn = dn_ref[:, at]
        scaled = gated * rms
        nout_ref[:, at] = (scaled * gain).astype(bf16)
        d_gated = rms * gain * dn - gated * coef
        dy = d_gated * gate
        dy_ref[:, at] = dy
        dgate_ref[:, at] = d_gated * y * s * (1.0 + raw[k] * (1.0 - s))
        kept.append((dy * keeper[k]).astype(bf16))
        rows_ref[0:1, at] = jnp.sum(dn * scaled, axis=0, keepdims=True)
        rows_ref[1:2, at] = jnp.sum(dy * x[k], axis=0, keepdims=True)
    c_mat = silu(c_ref[:, 512:640]).astype(bf16)
    send_ref[...] = dot(jnp.concatenate(kept, axis=1), c_mat, 0, 0)[0:192].astype(bf16)


def halves(ref, core):
    keep = ref[pl.ds(pl.multiple_of(core * 256, 256), 256), :]
    give = ref[pl.ds(pl.multiple_of(256 - core * 256, 256), 256), :]
    return keep.astype(bf16), give.astype(bf16)


def clear_edges(pad_ref):
    pad_ref[0:HALO] = jnp.zeros((HALO, 128), f32)
    pad_ref[HALO + T :] = jnp.zeros((HALO, 128), f32)


def conv_back(d_conv, taps, v_ref, at, valid, pad_ref):
    sums = [None, None, None, None, jnp.sum(d_conv, axis=0, keepdims=True)]
    sums[3] = jnp.sum(d_conv * v_ref[HALO:, at], axis=0, keepdims=True)
    pad_ref[HALO : HALO + T] = taps[3:4] * d_conv
    acc = pad_ref[0 : HALO + T]
    for lag in (1, 2, 3):
        masked = d_conv * valid[lag - 1]
        sums[3 - lag] = jnp.sum(
            masked * v_ref[pl.ds(HALO - lag, T), at], axis=0, keepdims=True
        )
        pad_ref[HALO : HALO + T] = taps[3 - lag : 4 - lag] * masked
        acc = acc + pad_ref[pl.ds(lag, HALO + T)]
    return acc, sums


def own_back_kernel(
    at_ref, dy_ref, y_ref, y0_ref, c_ref, aux_ref, m_ref, mg_ref, state_ref, nout_ref, w_ref,
    v_ref, ctap_ref, st_ref,
    dx_ref, db_ref, dcum_ref, xs_ref, b_ref, slope_ref, keep_ref, give_ref, dvc_ref, crow_ref,
    pad_ref, norm_ref,
):
    norm_ref[...] = dot(nout_ref[...], w_ref[:, 384:640], 1, 1)
    keep_ref[...], give_ref[...] = halves(norm_ref, at_ref[2])
    aux = aux_ref[...]
    aux_t = aux.T
    act = []
    for k in range(5):
        at = slice(128 * k, 128 * (k + 1))
        v = c_ref[:, at]
        s = sig(v)
        act.append(v * s)
        slope = s * (1.0 + v * (1.0 - s))
        if k < 4:
            slope_ref[:, at] = slope
    x = x_pair(*act[:3])
    xs_ref[:, 0:128] = x[0]
    xs_ref[:, 128:256] = x[1]
    b_ref[...] = act[3].astype(bf16)
    b_low, c_low = act[3].astype(bf16), act[4].astype(bf16)
    dy = pair_of(dy_ref)
    lo = lanes(T) < 64
    dy_h = (
        jnp.where(lo, dy[0], 0.0).astype(bf16),
        jnp.where(lo, 0.0, dy[0]).astype(bf16),
        dy[1].astype(bf16),
    )
    x_low = x[0].astype(bf16), x[1].astype(bf16)
    lane = lanes(T)
    dx = [jnp.zeros((T, 128), f32), jnp.zeros((T, 128), f32)]
    spread_sum = jnp.zeros((T, T), f32)
    rows = jnp.zeros((T, 128), f32)
    cols = jnp.zeros((128, T), f32)
    sub = lax.broadcasted_iota(jnp.int32, (128, T), 0)
    for h in range(3):
        pairs = dot(dy_h[h], x_low[h // 2], 1, 1) * aux_t[3 + h : 4 + h, :]
        mixing = mg_ref[h]
        spread_sum = spread_sum + pairs * m_ref[h].astype(f32)
        weights = pairs * mixing.astype(f32)
        rows = jnp.where(lane == h, jnp.sum(weights, axis=1, keepdims=True), rows)
        cols = jnp.where(sub == h, jnp.sum(weights, axis=0, keepdims=True), cols)
        dx[h // 2] = dx[h // 2] + dot(mixing, dy_h[h], 0, 0)
    low = spread_sum.astype(bf16)
    keeper = spread(aux, 10)
    kept = jnp.concatenate([dy[0] * keeper[0], dy[1] * keeper[1]], axis=1).astype(bf16)
    d_c = dot(low, b_low) + dot(kept, state_ref[...].astype(bf16))
    valid = valid_masks(column_of(st_ref))
    clear_edges(pad_ref)
    dv, sums = conv_back(d_c * slope, ctap_ref[0:5, 128:256], v_ref, slice(512, 640), valid, pad_ref)
    dvc_ref[...] = dv.astype(bf16)
    crow_ref[...] = jnp.concatenate([*sums, jnp.zeros((3, 128), f32)], axis=0)
    db_ref[...] = dot(low, c_low, 0, 0)
    dx_ref[:, 0:128] = dx[0]
    dx_ref[:, 128:256] = dx[1]
    carried = [
        dy[k] * (y_ref[:, 128 * k : 128 * (k + 1)] - y0_ref[:, 128 * k : 128 * (k + 1)])
        for k in range(2)
    ]
    dcum_ref[...] = rows - cols.T + head_sums(carried)


def back_kernel(
    at_ref, a0_ref, a1_ref, a2_ref, a3_ref, own_ref, passed_ref, tails_ref, mine_ref,
    state_ref, dx_ref, db_ref, dcum_ref, xs_ref, b_ref, slope_ref,
    dvc_ref, crow_ref, aux_ref, v_ref, tap_ref, ctap_ref, hp_ref, st_ref, dy_ref, dgate_ref,
    w_ref, wide_ref, rows_ref, hid_ref, halo_ref,
    dv_ref, dstep_ref, keep_ref, give_ref, edge_ref, chan_ref, conv_ref, gain_ref,
    pad_ref, norm_ref,
):
    here = jnp.right_shift(at_ref[0], 2)
    states = in_place(here, (a0_ref, a1_ref, a2_ref, a3_ref), slice(0, 192))
    tails = [tails_ref[16 * p : 16 * p + 16, :] for p in range(4)]
    _, entering, _, _ = fold(here, states, tails, True)
    adj = passed_ref[...] * entering + own_ref[...]
    aux = aux_ref[...]
    lane = lanes(T)
    x = pair_of(xs_ref)
    b_low = b_ref[...]
    delta, ending = spread(aux, 3), spread(aux, 13)
    adj_low = jnp.concatenate([adj, jnp.zeros((64, 128), f32)], axis=0).astype(bf16)
    through_b = dot(b_low, adj_low, 1, 1)
    skip = skip_pair(hp_ref)
    dy = pair_of(dy_ref)
    ended, extra, full, d_x = [], [], [], []
    for k in range(2):
        at = slice(128 * k, 128 * (k + 1))
        late = ending[k] * through_b[:, at]
        total = dx_ref[:, at] + late
        d_x.append(delta[k] * total + skip[k] * dy[k])
        full.append(x[k] * total)
        extra.append(x[k] * late)
        ended.append(x[k] * delta[k] * ending[k])
    d_b = db_ref[...] + dot(jnp.concatenate(ended, axis=1).astype(bf16), adj_low)
    d_delta = head_sums(full)
    tail = head_sums(extra) * rolled(aux, -3)
    tail = jnp.where(lane < 3, tail, 0.0)
    d_cum = dcum_ref[...] - tail
    ri = lax.broadcasted_iota(jnp.int32, (T, T), 0)
    ci = lax.broadcasted_iota(jnp.int32, (T, T), 1)
    upper = jnp.where(ci >= ri, 1.0, 0.0).astype(bf16)
    d_log = joined(dot(upper, three_parts(d_cum).astype(bf16)))
    own = decay_rows(mine_ref[192:SROWS, :].astype(f32))
    met = own * adj * state_ref[0:192]
    lane1 = lanes(1)
    meets = jnp.zeros((1, 128), f32)
    for h in range(3):
        meets = jnp.where(lane1 == h, jnp.sum(met[64 * h : 64 * h + 64]), meets)
    d_log = d_log + jnp.sum(tail, axis=0, keepdims=True) + meets
    d_log = jnp.where(lane < 3, d_log, 0.0)
    rate = jnp.exp(head_row(hp_ref, 1))
    d_raw = (d_delta - rate * d_log) * rolled(aux, -6)
    d_raw = jnp.where(lane < 3, d_raw, 0.0)
    delta_cols = jnp.where(lane < 3, rolled(aux, -3), 0.0)
    step_low = half(d_raw).astype(bf16)
    dstep_ref[...] = step_low

    d_gate = pair_of(dgate_ref)
    x_tiles = head_tiles((jnp.zeros_like(d_x[0]),) * 2, d_x)
    gate_tiles = head_tiles(d_gate, (jnp.zeros_like(d_x[0]),) * 2)
    lo = lane < 64
    valid = valid_masks(column_of(st_ref))
    clear_edges(pad_ref)
    tap_rows = []
    for k in range(4):
        at = slice(128 * k, 128 * (k + 1))
        slope = slope_ref[:, at]
        if k < 3:
            d_conv = jnp.where(lo, gate_tiles[k], x_tiles[k] * slope)
            taps = tap_ref[0:5, at]
        else:
            d_conv = d_b * slope
            taps = ctap_ref[0:5, 0:128]
        dv, sums = conv_back(d_conv, taps, v_ref, at, valid, pad_ref)
        dv_ref[:, at] = dv.astype(bf16)
        tap_rows.append(sums)
    dv_ref[:, 512:640] = dvc_ref[...]
    tap_rows.append([crow_ref[j : j + 1, :] for j in range(5)])

    chan_ref_rows = []
    for j in range(5):
        pair = x_pair(*[tap_rows[k][j] for k in range(3)])
        chan_ref_rows.append(jnp.concatenate(pair, axis=1))
    chan_ref_rows.append(rows_ref[0:1, :])
    h0 = jnp.sum(d_raw, axis=0, keepdims=True)
    h1 = jnp.sum(d_log * (-rate) * delta_cols, axis=0, keepdims=True)
    h2 = head_sums((rows_ref[1:2, 0:128], rows_ref[1:2, 128:256]))
    zero = jnp.zeros((1, 128), f32)
    for r in (h0, h1, h2):
        chan_ref_rows.append(jnp.concatenate([r, zero], axis=1))
    for j, r in enumerate(chan_ref_rows):
        chan_ref[j : j + 1, :] = r
    chan_ref[9:16, :] = jnp.zeros((7, 256), f32)
    for j in range(5):
        conv_ref[j : j + 1, :] = jnp.concatenate([tap_rows[3][j], tap_rows[4][j]], axis=1)
    conv_ref[5:8, :] = jnp.zeros((3, 256), f32)

    d_norm = dot(dv_ref[:, 0:384], w_ref[:, 0:384], 1, 1)
    d_norm = d_norm + dot(dv_ref[:, 384:640], wide_ref[...], 1, 1)
    main = d_norm[HALO:] + dot(step_low, w_ref[:, 512:640], 1, 1)
    norm_ref[...] = main
    keep_ref[...], give_ref[...] = halves(norm_ref, at_ref[2])
    edge_ref[...] = d_norm[0:HALO].astype(bf16)
    total = jnp.zeros((1, D), f32)
    for src, val in ((halo_ref, d_norm[0:HALO]), (hid_ref, main)):
        h = src[...].astype(f32)
        inv = lax.rsqrt(jnp.mean(h * h, axis=1, keepdims=True) + norm_eps)
        total = total + jnp.sum(val * (h * inv), axis=0, keepdims=True)
    gain_ref[0:1] = total
    gain_ref[1:8] = jnp.zeros((7, D), f32)


def grad_kernel(
    normed_ref, dv_ref, dstep_ref, nout_ref, cot_ref, conv_ref, gain_ref, chan_ref, out_ref
):
    normed = normed_ref[...]
    out_ref[:, 0:384] = dot(normed, dv_ref[:, 0:384], 0, 0).astype(bf16)
    out_ref[:, 640:896] = dot(normed, dv_ref[:, 384:640], 0, 0).astype(bf16)
    outs = dot(cot_ref[...], nout_ref[...], 0, 0)
    out_ref[:, 384:512] = outs[:, 0:128].astype(bf16)
    tile = outs[:, 128:256] + dot(normed_ref[HALO:, :], dstep_ref[...], 0, 0)
    grads = jnp.concatenate([jnp.zeros((MISC + 5, 256), f32), conv_ref[0:5, :]], axis=0)
    grads = jnp.concatenate([grads, jnp.zeros((128 - MISC - 10, 256), f32)], axis=0)
    high = grads.astype(bf16)
    lower = (grads - high.astype(f32)).astype(bf16)
    sel = selector()
    tile = tile + dot(sel, high, 1, 1) + pltpu.roll(dot(sel, lower, 1, 1), 5, 1)
    gain = gain_ref[0:1]
    gain_high = gain.astype(bf16).astype(f32)
    sub = lax.broadcasted_iota(jnp.int32, (128, D), 0)
    column = jnp.where(
        sub == MISC + 3, gain_high, jnp.where(sub == MISC + 4, gain - gain_high, 0.0)
    ).T
    turned = jnp.concatenate([chan_ref[...], jnp.zeros((112, 256), f32)], axis=0).T
    turned = jnp.where(lanes(256) < 9, turned, 0.0)
    shared = jnp.zeros((48, 128), f32)
    for g in range(4):
        shared = shared + rolled(turned[48 * g : 48 * g + 48], MISC + 16 + 9 * g)
    tile = tile + column + jnp.concatenate([shared] * N_SEQ, axis=0)
    out_ref[:, 512:640] = tile.astype(bf16)


def pair_kernel(
    at_ref, keep_ref, got_ref, edge0_ref, edge1_ref, out_keep_ref, out_got_ref,
    own_ref, s1, s2, s3, sum_ref,
):
    sum_ref[:, 0:D] = keep_ref[...].astype(f32) + got_ref[...].astype(f32)
    sum_ref[256 - HALO :, 0:D] += edge0_ref[...].astype(f32) + edge1_ref[...].astype(f32)
    sum_ref[:, D:] = out_keep_ref[...].astype(f32) + out_got_ref[...].astype(f32)
    for by, ref in enumerate((own_ref, s1, s2, s3)):
        start = pl.multiple_of(lax.rem(at_ref[1] + by, 4) * 64, 64)
        ref[...] = sum_ref[pl.ds(start, 64), :].astype(bf16)


def four_kernel(at_ref, a_ref, b_ref, c_ref, d_ref, hid_ref, out_ref):
    total = a_ref[...].astype(f32) + b_ref[...].astype(f32)
    total = total + c_ref[...].astype(f32) + d_ref[...].astype(f32)
    start = pl.multiple_of((4 * at_ref[2] + at_ref[1]) * 64, 64)
    out_ref[:, 0:D] = total[:, 0:D].astype(bf16)
    out_ref[:, D:] = (total[:, D:] + hid_ref[pl.ds(start, 64), :].astype(f32)).astype(bf16)


def input_kernel(*refs):
    at_ref, refs = refs[0], refs[1:]
    hid_ref, cot_ref, row_ref, out_ref, block_ref = refs[8:]
    for side in range(2):
        core = at_ref[2] if side == 0 else 1 - at_ref[2]
        for by in range(4):
            block = core * 4 + lax.rem(at_ref[1] + 4 - by, 4)
            rows = pl.ds(pl.multiple_of(block * 64, 64), 64)
            piece = refs[4 * side + by]
            h = hid_ref[rows, :].astype(f32)
            inv = lax.rsqrt(jnp.mean(h * h, axis=1, keepdims=True) + norm_eps)
            d_scaled = piece[:, 0:D].astype(f32) * row_ref[0:1, :]
            inner = jnp.sum(d_scaled * h, axis=1, keepdims=True)
            out_ref[rows, :] = (
                cot_ref[rows, :].astype(f32)
                + inv * d_scaled
                - h * (inv * inv * inv * inner / D)
            )
            block_ref[rows, :] = piece[:, D:]


def adam(weight, grad, first, second, rate):
    first_new = beta_one * first + (1.0 - beta_one) * grad
    second_new = beta_two * second + (1.0 - beta_two) * grad * grad
    first_hat = first_new / (1.0 - beta_one**STEP)
    second_hat = second_new / (1.0 - beta_two**STEP)
    weight_new = weight - rate * (
        first_hat / (jnp.sqrt(second_hat) + adam_eps) + decay_rate * weight
    )
    return first_new, second_new, weight_new


RATE_D = 1.4 * D ** (-0.5)
RATE_I = 1.4 * DI ** (-0.5)


def put(refs, at, values):
    for ref, value in zip(refs, values):
        ref[at] = value


def update_kernel(*refs):
    grad_ref, refs = refs[0], refs[1:]
    proj, step, out, chan, head = (refs[3 * k : 3 * k + 3] for k in range(5))
    outs = refs[15:]
    proj_o, step_o, out_o, chan_o, head_o = (outs[3 * k : 3 * k + 3] for k in range(5))
    rest_ref = outs[15]
    total = grad_ref[0].astype(f32)
    for q in range(1, N_SEQ):
        total = total + grad_ref[q].astype(f32)
    misc = total[:, 512:640]
    rest_ref[...] = jnp.zeros_like(rest_ref)
    for h in range(N_HEAD):
        rest_ref[h, 0:6, 0:256] = total[6 * h : 6 * h + 6, 640:896]
        rest_ref[h, 0:6, 256:384] = misc[6 * h : 6 * h + 6]
    for h in range(3):
        w, m, v = (r[h] for r in proj)
        put(proj_o, h, adam(w, total[:, 128 * h : 128 * (h + 1)], m, v, RATE_D))
        tile = total[:, 384 + 128 * (h // 2) : 512 + 128 * (h // 2)]
        tile = half(tile) if h == 1 else tile
        w, m, v = (r[h] for r in out)
        put(out_o, h, adam(w, tile[:, 0:64], m, v, RATE_I))
    turned = jnp.concatenate([misc, jnp.zeros((80, 128), f32)], axis=0).T
    at = (slice(None), slice(None))
    w, m, v = (r[at] for r in step)
    put(step_o, at, adam(w, turned[MISC : MISC + 3, 0:48], m, v, RATE_D))
    first = MISC + 16
    p = [turned[first + 9 * g : first + 9 * g + 9] for g in range(4)]
    lane = lanes(9)
    wrapped = rolled(p[2], 96)
    pair = (
        p[0] + rolled(p[1], 48) + jnp.where(lane >= 96, wrapped, 0.0),
        jnp.where(lane < 16, wrapped, 0.0) + rolled(p[3], 16),
    )
    for h in range(3):
        piece = half(pair[0]) if h == 1 else pair[h // 2]
        at = (slice(None), h, slice(None))
        w, m, v = (r[at] for r in chan)
        put(chan_o, at, adam(w, piece[0:6, 0:64], m, v, 0.5))
    at = (slice(None), slice(None))
    w, m, v = (r[at] for r in head)
    put(head_o, at, adam(w, pair[0][6:9, 0:3], m, v, 1.0))


def rest_kernel(*refs):
    got_ref, refs = refs[0], refs[1:]
    shared, gain, conv = (refs[3 * k : 3 * k + 3] for k in range(3))
    outs = refs[9:]
    shared_o, gain_o, conv_o = (outs[3 * k : 3 * k + 3] for k in range(3))
    total = got_ref[0]
    for q in range(1, N_HEAD):
        total = total + got_ref[q]
    at = (slice(None), slice(None))
    w, m, v = (r[at] for r in shared)
    put(shared_o, at, adam(w, total[0:6, 0:256], m, v, RATE_D))
    column = total[:, 256 + MISC + 3 : 256 + MISC + 4] + total[:, 256 + MISC + 4 : 256 + MISC + 5]
    sub = lax.broadcasted_iota(jnp.int32, (8, 128), 0)
    row = jnp.sum(jnp.where(sub == lanes(8), column, 0.0), axis=0, keepdims=True)
    w, m, v = (r[at] for r in gain)
    put(gain_o, at, adam(w, row[:, 0:6], m, v, 0.5))
    tile = total[0:2, 256:384]
    both = rolled(tile, -(MISC + 5)) + rolled(tile, -(MISC + 10))
    w, m, v = (r[at] for r in conv)
    put(conv_o, at, adam(w, both[:, 0:5], m, v, 0.5))


def exchange(blocks, axis):
    return lax.all_to_all(blocks, axis, 0, 0, tiled=True)


def around(a, axis, by):
    peers = lax.axis_size(axis)
    return lax.ppermute(a, axis, [(i, (i + by) % peers) for i in range(peers)])


def to_next(a):
    return lax.ppermute(a, SEQ, [(i, i + 1) for i in range(N_SEQ - 1)])


def to_previous(a, core):
    pairs = [(2 * i + 2 + core, 2 * i + 1) for i in range(N_SEQ - 1)]
    return lax.ppermute(a, SEQ + ("head_1",), pairs)


def body(
    hidden_in, cotangent, doc_starts, proj_weight, step_weight, out_weight, shared_weight,
    pre_gain, channel_params, head_params, shared_conv, proj_first, proj_second, step_first,
    step_second, out_first, out_second, shared_first, shared_second, gain_first, gain_second,
    channel_first, channel_second, head_first, head_second, conv_first, conv_second,
):
    where = jnp.stack(
        [lax.axis_index(SEQ), lax.axis_index("head_0"), lax.axis_index("head_1")]
    ).astype(jnp.int32)
    halo = to_next(hidden_in[T - HALO :])
    matrices = [jnp.transpose(a, (1, 0, 2)) for a in (proj_weight, proj_first, proj_second)]
    steps = [a.T for a in (step_weight, step_first, step_second)]
    out_weights = [jnp.transpose(a, (0, 2, 1)) for a in (out_weight, out_first, out_second)]
    gains_in = [a.reshape(1, 6) for a in (pre_gain, gain_first, gain_second)]

    (pack,) = call(
        pack_kernel, [((N_SEQ, 48, NW), bf16)],
        matrices[0], out_weights[0], steps[0], shared_weight, gains_in[0], shared_conv,
        scratch=[pltpu.VMEM((128, 128), f32), pltpu.VMEM((48, 128), f32)], name="pack",
    )
    weights = exchange(pack, SEQ).reshape(D, NW)
    (slab,) = call(slab_kernel, [((96, 384), bf16)], weights, name="slab")
    near = [slab] + [around(slab, "head_0", by) for by in (1, 2, 3)]
    slabs = near + [around(a, "head_1", 1) for a in near]

    marks = doc_starts.astype(f32).reshape(1, T)
    fixed = jnp.broadcast_to(
        (jnp.arange(6) == 3).astype(f32)[:, None, None], channel_params.shape
    )
    taps = jnp.concatenate([fixed, channel_params], axis=2).reshape(6, 384)
    gains = jnp.pad(channel_params[5].reshape(1, 192), ((0, 5), (0, 64)))
    taps = jnp.pad(jnp.concatenate([taps, gains], axis=1), ((0, 2), (0, 0)))

    normed, values, conv, aux, sent, row, wide, conv_taps = call(
        first_kernel,
        [
            ((HALO + T, D), bf16), ((HALO + T, NV), f32), ((T, NV), f32), ((T, 128), f32),
            ((SROWS, 128), bf16), ((8, D), f32), ((D, 256), bf16), ((8, 256), f32),
        ],
        where, *slabs, hidden_in, halo, marks, weights, taps, head_params, smem=(0, 14),
        scratch=[pltpu.VMEM((D, 384), bf16)], name="first",
    )
    states = [sent] + [around(sent, "seq_1", by) for by in (1, 2, 3)]
    group, group_in, group_passed, group_tails = call(
        group_kernel,
        [((SROWS, 128), bf16), ((192, 128), f32), ((192, 128), f32), ((64, 128), f32)],
        where, *states, smem=(0,), name="group",
    )
    groups = [group] + [around(group, "seq_0", by) for by in (1, 2, 3)]
    y_own, d_normed, decays, mixing = call(
        own_kernel,
        [((T, 256), f32), ((T, 256), f32), ((3, T, T), bf16), ((3, T, T), bf16)],
        conv, aux, cotangent, weights, head_params, smem=(4,), name="own",
    )
    y_full, state, stat, all_tails = call(
        enter_kernel,
        [((T, 256), f32), ((256, 128), f32), ((8, T), f32), ((64, 128), f32)],
        where, *groups, group_in, group_passed, y_own, d_normed, conv, aux, taps, smem=(0,), name="enter",
    )
    stat = stat + around(stat, "head_1", 1)
    stats = [stat] + [around(stat, "head_0", by) for by in (1, 2, 3)]
    d_y, d_gate, normed_out, sent_adj, rows = call(
        gated_kernel,
        [
            ((T, 256), f32), ((T, 256), f32), ((T, 256), bf16),
            ((192, 128), bf16), ((8, 256), f32),
        ],
        *stats, y_full, d_normed, conv, aux, taps, name="gated",
    )
    adjoints = [sent_adj] + [around(sent_adj, "seq_1", by) for by in (1, 2, 3)]
    group, adj_in, adj_passed = call(
        group_back_kernel,
        [((192, 128), bf16), ((192, 128), f32), ((192, 128), f32)],
        where, *adjoints, group_tails, smem=(0,), name="group_back",
    )
    groups = [group] + [around(group, "seq_0", by) for by in (1, 2, 3)]
    half_rows = ((T // 2, D), bf16)
    (
        d_x, d_b, d_cum, x_act, b_act, slopes, out_keep, out_give, d_value_c, c_rows
    ) = call(
        own_back_kernel,
        [
            ((T, 256), f32), ((T, 128), f32), ((T, 128), f32), ((T, 256), f32),
            ((T, 128), bf16), ((T, 512), f32), half_rows, half_rows,
            ((HALO + T, 128), bf16), ((8, 128), f32),
        ],
        where, d_y, y_full, y_own, conv, aux, decays, mixing, state, normed_out, weights,
        values, conv_taps, marks, smem=(0,),
        scratch=[pltpu.VMEM((T + 2 * HALO, 128), f32), pltpu.VMEM((T, D), f32)],
        name="own_back",
    )
    out_taken = around(out_give, "head_1", 1)
    d_values, d_step, keep, give, edge, chan, d_conv, d_gain = call(
        back_kernel,
        [
            ((HALO + T, NV), bf16), ((T, 128), bf16), half_rows, half_rows,
            ((HALO, D), bf16), ((16, 256), f32), ((8, 256), f32), ((8, D), f32),
        ],
        where, *groups, adj_in, adj_passed, all_tails, sent, state, d_x, d_b, d_cum, x_act, b_act, slopes, d_value_c,
        c_rows, aux, values, taps, conv_taps, head_params, marks, d_y, d_gate, weights, wide,
        rows, hidden_in, halo,
        smem=(0, 22),
        scratch=[pltpu.VMEM((T + 2 * HALO, 128), f32), pltpu.VMEM((T, D), f32)],
        name="back",
    )
    taken = around(give, "head_1", 1)
    edges = [to_previous(edge, core) for core in range(2)]
    (grads,) = call(
        grad_kernel, [((D, NG), bf16)],
        normed, d_values, d_step, normed_out, cotangent, d_conv, d_gain, chan, name="grad",
    )
    grads, taken, out_taken, edges = lax.optimization_barrier(
        (grads, taken, out_taken, edges)
    )
    grads = exchange(grads.reshape(N_SEQ, 48, NG), SEQ)

    piece = ((T // N_HEAD, 2 * D), bf16)
    pieces = call(
        pair_kernel, [piece] * 4, where, keep, taken, *edges, out_keep, out_taken,
        smem=(0,), scratch=[pltpu.VMEM((T // 2, 2 * D), f32)], name="pair",
    )
    parts = [pieces[0]] + [around(pieces[by], "head_0", by) for by in (1, 2, 3)]
    (own,) = call(four_kernel, [piece], where, *parts, hidden_in, smem=(0,), name="four")
    near = [own] + [around(own, "head_0", by) for by in (1, 2, 3)]
    far = [around(a, "head_1", 1) for a in near]
    input_grad, block_out = call(
        input_kernel, [((T, D), f32), ((T, D), bf16)], where, *near, *far, hidden_in, cotangent, row,
        smem=(0,), name="input",
    )

    proj, step, out = (3, 48, 128), (3, 48), (3, 48, 64)
    shapes = [proj] * 3 + [step] * 3 + [out] * 3 + [(6, 3, 64)] * 3 + [(3, 3)] * 3
    updated = call(
        update_kernel,
        [(s, f32) for s in shapes] + [((N_HEAD, 8, 384), f32)],
        grads, *matrices, *steps, *out_weights, channel_params, channel_first,
        channel_second, head_params, head_first, head_second, name="update",
    )
    rest = exchange(updated[15], HEAD)
    shared = call(
        rest_kernel,
        [(s, f32) for s in [(6, 256)] * 3 + [(1, 6)] * 3 + [(2, 5)] * 3],
        rest, shared_weight, shared_first, shared_second, *gains_in, shared_conv, conv_first,
        conv_second, name="rest",
    )
    return (
        block_out, input_grad,
        *(jnp.transpose(a, (1, 0, 2)) for a in updated[0:3]),
        *(a.T for a in updated[3:6]),
        *(jnp.transpose(a, (0, 2, 1)) for a in updated[6:9]),
        *shared[0:3],
        *(g.reshape(6) for g in shared[3:6]),
        *updated[9:15],
        *shared[6:9],
    )


def solution(mesh):
    finer = Mesh(mesh.devices.reshape(4, 4, 4, 2), SEQ_HEAD)
    matrix = P(SEQ, HEAD, None)
    step = P(SEQ, HEAD)
    out = P(HEAD, None, SEQ)
    both = P(SEQ_HEAD, None)
    gain = P(SEQ_HEAD)
    channel = P(None, HEAD, None)
    head = P(None, HEAD)
    tokens = P(SEQ, None)
    return jax.shard_map(
        body,
        mesh=finer,
        in_specs=(
            tokens, tokens, P(SEQ), matrix, step, out, both, gain, channel, head, both,
            matrix, matrix, step, step, out, out, both, both, gain, gain, channel, channel,
            head, head, both, both,
        ),
        out_specs=(
            (tokens, tokens)
            + (matrix,) * 3 + (step,) * 3 + (out,) * 3 + (both,) * 3 + (gain,) * 3
            + (channel,) * 3 + (head,) * 3 + (both,) * 3
        ),
        check_vma=False,
    )
```

```python
import functools

import jax
import jax.numpy as jnp
from jax import lax
from jax.experimental import pallas as pl
from jax.experimental.pallas import tpu as pltpu
from jax.sharding import Mesh
from jax.sharding import PartitionSpec as P

D = 768
DI = 1536
STEP = 10
SEQ = ("seq_0", "seq_1")
HEAD = ("head_0", "head_1")
SEQ_HEAD = SEQ + HEAD
N_SEQ = 16
N_HEAD = 8

T = 512
HALO = 16
NV = 640
NW = 640
MISC = 64
CHAN = (69, 78, 84, 90)
SLAB = 96
SROWS = 208

f32 = jnp.float32
bf16 = jnp.bfloat16
norm_eps = 1e-05
beta_one = 0.9
beta_two = 0.999
adam_eps = 1e-08
decay_rate = 0.01
LOW = -1e30

PARAMS = pltpu.CompilerParams(vmem_limit_bytes=32 * 1024 * 1024)
WIDE = pltpu.CompilerParams(vmem_limit_bytes=56 * 1024 * 1024)
VM = pl.BlockSpec(memory_space=pltpu.VMEM)
SM = pl.BlockSpec(memory_space=pltpu.SMEM)
ANY = pl.BlockSpec(memory_space=pl.ANY)


def call(kernel, outs, *args, smem=(), anywhere=(), scratch=(), params=PARAMS, name=None):
    return pl.pallas_call(
        kernel,
        out_shape=[jax.ShapeDtypeStruct(s, d) for s, d in outs],
        in_specs=[
            SM if i in smem else ANY if i in anywhere else VM for i in range(len(args))
        ],
        out_specs=[VM] * len(outs),
        scratch_shapes=list(scratch),
        compiler_params=params,
        name=name,
    )(*args)


def dot(a, b, ca=1, cb=0):
    return lax.dot_general(a, b, (((ca,), (cb,)), ((), ())), preferred_element_type=f32)


def lanes(rows):
    return lax.broadcasted_iota(jnp.int32, (rows, 128), 1)


def half(v):
    return pltpu.roll(v, 64, 1)


def rolled(v, by):
    return pltpu.roll(v, by % 128, 1)


def sig(v):
    return 1.0 / (1.0 + jnp.exp(-v))


def silu(v):
    return v * sig(v)


def dsilu(v):
    s = sig(v)
    return s * (1.0 + v * (1.0 - s))


def gate_pair(t0, t1, t2):
    lo = lanes(t0.shape[0]) < 64
    return jnp.where(lo, t0, half(t1)), jnp.where(lo, t2, 0.0)


def x_pair(t0, t1, t2):
    lo = lanes(t0.shape[0]) < 64
    return jnp.where(lo, half(t0), t1), jnp.where(lo, half(t2), 0.0)


def head_tiles(gate, x):
    lo = lanes(gate[0].shape[0]) < 64
    return (
        jnp.where(lo, gate[0], half(x[0])),
        jnp.where(lo, half(gate[0]), x[0]),
        jnp.where(lo, gate[1], half(x[1])),
    )


def spread(a, at):
    lo = lanes(a.shape[0]) < 64
    return (
        jnp.where(lo, a[:, at : at + 1], a[:, at + 1 : at + 2]),
        jnp.where(lo, a[:, at + 2 : at + 3], 0.0),
    )


def head_sums(pair):
    a, b = pair
    lane = lanes(a.shape[0])
    s0 = jnp.sum(jnp.where(lane < 64, a, 0.0), axis=1, keepdims=True)
    s1 = jnp.sum(jnp.where(lane < 64, 0.0, a), axis=1, keepdims=True)
    s2 = jnp.sum(b, axis=1, keepdims=True)
    return jnp.where(lane == 0, s0, jnp.where(lane == 1, s1, jnp.where(lane == 2, s2, 0.0)))


def pair_of(ref):
    return ref[:, 0:128], ref[:, 128:256]


def head_row(hp_ref, k, rows=1):
    lane = lanes(rows)
    return jnp.where(
        lane == 0,
        hp_ref[k, 0],
        jnp.where(lane == 1, hp_ref[k, 1], jnp.where(lane == 2, hp_ref[k, 2], 0.0)),
    )


def skip_pair(hp_ref):
    lane = lanes(1)
    return (
        jnp.where(lane < 64, hp_ref[2, 0], hp_ref[2, 1]),
        jnp.where(lane < 64, hp_ref[2, 2], 0.0),
    )


def three_parts(v):
    hi = v.astype(bf16).astype(f32)
    rest = v - hi
    mid = rest.astype(bf16).astype(f32)
    return hi + rolled(mid, 3) + rolled(rest - mid, 6)


def joined(v):
    total = v + rolled(v, -3) + rolled(v, -6)
    return jnp.where(lanes(v.shape[0]) < 3, total, 0.0)


def act_tiles(c_ref):
    return [silu(c_ref[:, 128 * k : 128 * (k + 1)]) for k in range(5)]


def valid_masks(starts_col):
    row = lax.broadcasted_iota(jnp.int32, starts_col.shape, 0)
    one = jnp.where(row < 1, 0.0, pltpu.roll(starts_col, 1, 0))
    two = jnp.where(row < 2, 0.0, pltpu.roll(starts_col, 2, 0))
    first = 1.0 - starts_col
    return first, first - one, first - one - two


def column_of(row_ref):
    return jnp.broadcast_to(row_ref[0:1, :], (128, T)).T


def selector():
    r = lax.broadcasted_iota(jnp.int32, (D, 256), 0)
    k = lax.broadcasted_iota(jnp.int32, (D, 256), 1)
    h = jnp.bitwise_and(jnp.right_shift(k, 1), 7)
    at = 48 * jnp.right_shift(k, 4) + 6 * h + jnp.bitwise_and(k, 1)
    return jnp.where(r == at, 1.0, 0.0).astype(bf16)


def slab_rows(a):
    s = jnp.right_shift(a * 43, 8)
    return 42 * s + a


def pack_kernel(
    proj_ref, outw_ref, step_ref, shared_ref, gain_ref, conv_ref, pack_ref, misc_ref, wide_ref
):
    misc_ref[...] = jnp.zeros_like(misc_ref)
    misc_ref[0:3, 0:48] = step_ref[...]
    misc_ref[0:48, :] = half(misc_ref[...].T)[0:48]
    wide_ref[...] = jnp.zeros_like(wide_ref)
    wide_ref[0:1, 0:6] = gain_ref[...]
    sub = lax.broadcasted_iota(jnp.int32, (6, 128), 0)
    lane = lanes(6)
    column = jnp.sum(jnp.where(sub == lane, wide_ref[0:1, :], 0.0), axis=1, keepdims=True)
    high = column.astype(bf16).astype(f32)
    misc_ref[0:6, :] += jnp.where(lane == MISC + 3, high, 0.0) + jnp.where(
        lane == MISC + 4, column - high, 0.0
    )
    conv = conv_ref[...]
    high = conv.astype(bf16).astype(f32)
    misc_ref[0:2, MISC + 5 : MISC + 10] = high
    misc_ref[0:2, MISC + 10 : MISC + 15] = conv - high
    for j in range(8):
        tile = rolled(shared_ref[:, 128 * (j // 4) : 128 * (j // 4) + 128], SLAB - 32 * (j % 4))
        misc_ref[6 * j : 6 * j + 6, :] += jnp.where(lane >= SLAB, tile, 0.0)
    misc = misc_ref[0:48, :]
    lo = lanes(48) < 64
    wide = []
    for h in range(3):
        wide_ref[:, 0:64] = outw_ref[h]
        wide.append(wide_ref[...])
    tiles = [proj_ref[h] for h in range(3)]
    tiles += [jnp.where(lo, wide[0], half(wide[1])), jnp.where(lo, wide[2], misc)]
    for k, tile in enumerate(tiles):
        low = tile.astype(bf16)
        for q in range(N_SEQ):
            pack_ref[q, :, 128 * k : 128 * (k + 1)] = low


def slab_kernel(w_ref, slab_ref):
    misc = w_ref[:, 512:640]
    a = lax.broadcasted_iota(jnp.int32, (96, D), 0)
    d = lax.broadcasted_iota(jnp.int32, (96, D), 1)
    gap = d - slab_rows(a)
    lane = lanes(96)
    tiles = [jnp.zeros((96, 128), f32)] * 2
    for j in range(8):
        got = dot(jnp.where(gap == 6 * j, 1.0, 0.0).astype(bf16), misc)
        if j == 0:
            slab_ref[:, 256:384] = jnp.where(lane < SLAB, got, 0.0).astype(bf16)
        own = jnp.where(lane >= SLAB, got, 0.0)
        tiles[j // 4] = tiles[j // 4] + rolled(own, 32 * (j % 4) - SLAB)
    slab_ref[:, 0:128] = tiles[0].astype(bf16)
    slab_ref[:, 128:256] = tiles[1].astype(bf16)


def first_kernel(*refs):
    at_ref, slabs, refs = refs[0], refs[1:9], refs[9:]
    hid_ref, halo_ref, st_ref, w_ref, tap_ref, hp_ref = refs[:6]
    normed_ref, v_ref, c_ref, aux_ref, send_ref, row_ref, wide_ref, ctap_ref = refs[6:14]
    all_ref = refs[14]
    d = lax.broadcasted_iota(jnp.int32, (D, 96), 0)
    a = lax.broadcasted_iota(jnp.int32, (D, 96), 1)
    gap = d - slab_rows(a)
    picks = []
    for b in range(8):
        core = at_ref[2] if b < 4 else 1 - at_ref[2]
        head = 2 * lax.rem(at_ref[1] + 4 - b % 4, 4) + core
        all_ref[96 * b : 96 * b + 96, :] = slabs[b][...]
        picks.append(jnp.where(gap == 6 * head, 1.0, 0.0))
    spread_rows = dot(jnp.concatenate(picks, axis=1).astype(bf16), all_ref[...])
    wide_ref[...] = spread_rows[:, 0:256].astype(bf16)
    misc_t = spread_rows[:, 256:384].T
    gain = misc_t[MISC + 3 : MISC + 4] + misc_t[MISC + 4 : MISC + 5]
    conv_t = dot(misc_t.astype(bf16), selector())
    conv_taps = conv_t[MISC + 5 : MISC + 10] + conv_t[MISC + 10 : MISC + 15]
    ctap_ref[0:5, :] = conv_taps
    ctap_ref[5:8, :] = jnp.zeros((3, 256), f32)
    row_ref[0:1, :] = gain
    row_ref[1:8, :] = jnp.zeros((7, D), f32)
    for src, at, rows in ((halo_ref, 0, HALO), (hid_ref, HALO, T)):
        h = src[...].astype(f32)
        inv = lax.rsqrt(jnp.mean(h * h, axis=1, keepdims=True) + norm_eps)
        normed_ref[at : at + rows, :] = (h * inv * gain).astype(bf16)
    normed = normed_ref[...]
    v_ref[:, 0:384] = dot(normed, w_ref[:, 0:384])
    v_ref[:, 384:640] = dot(normed, wide_ref[...])
    raw = half(dot(normed[HALO:], w_ref[:, 512:640]))

    lane = lanes(T)
    pre = raw + head_row(hp_ref, 0)
    delta = jnp.where(
        lane < 3, jnp.maximum(pre, 0.0) + jnp.log1p(jnp.exp(-jnp.abs(pre))), 0.0
    )
    slope = jnp.where(lane < 3, sig(pre), 0.0)
    log_decay = -jnp.exp(head_row(hp_ref, 1)) * delta
    starts = column_of(st_ref)
    parts = three_parts(log_decay) + jnp.where(lane == 9, starts, 0.0)
    ri = lax.broadcasted_iota(jnp.int32, (T, T), 0)
    ci = lax.broadcasted_iota(jnp.int32, (T, T), 1)
    summed = dot(jnp.where(ri >= ci, 1.0, 0.0).astype(bf16), parts.astype(bf16))
    cum = joined(summed)
    segment = summed[:, 9:10]
    last = cum[T - 1 : T, :]
    last_segment = segment[T - 1 : T, :]
    keeper = jnp.where((lane < 3) & (segment == 0.0), jnp.exp(cum), 0.0)
    ending = jnp.where((lane < 3) & (segment == last_segment), jnp.exp(last - cum), 0.0)
    aux_ref[...] = (
        cum
        + rolled(delta, 3)
        + rolled(slope, 6)
        + jnp.where(lane == 9, segment, 0.0)
        + rolled(keeper, 10)
        + rolled(ending, 13)
    )

    valid = valid_masks(starts)
    for k in range(5):
        at = slice(128 * k, 128 * (k + 1))
        if k < 3:
            taps = tap_ref[0:5, at]
        else:
            taps = conv_taps[:, 128 * (k - 3) : 128 * (k - 2)]
        total = taps[4:5] + taps[3:4] * v_ref[HALO:, at]
        for lag in (1, 2, 3):
            total = total + taps[3 - lag : 4 - lag] * (
                v_ref[pl.ds(HALO - lag, T), at] * valid[lag - 1]
            )
        c_ref[:, at] = total

    act = act_tiles(c_ref)
    x = x_pair(*act[:3])
    weight = spread(ending * delta, 0)
    ended = jnp.concatenate([x[0] * weight[0], x[1] * weight[1]], axis=1).astype(bf16)
    state = dot(ended, act[3].astype(bf16), 0, 0)
    through = jnp.where(last_segment == 0.0, jnp.exp(last), 0.0)
    high = through.astype(bf16).astype(f32)
    lower = through - high
    sub = lax.broadcasted_iota(jnp.int32, (16, 128), 0)
    tail = jnp.zeros((16, 128), f32)
    for h in range(3):
        tail = jnp.where(sub == h, high[:, h : h + 1], tail)
        tail = jnp.where(sub == 3 + h, lower[:, h : h + 1], tail)
    send_ref[0:192, :] = state[0:192].astype(bf16)
    send_ref[192:SROWS, :] = tail.astype(bf16)


def own_kernel(c_ref, aux_ref, cot_ref, w_ref, hp_ref, y_ref, dn_ref, m_ref, mg_ref):
    act = act_tiles(c_ref)
    x = x_pair(*act[:3])
    aux = aux_ref[...]
    aux_t = aux.T
    scores = dot(act[4].astype(bf16), act[3].astype(bf16), 1, 1)
    ri = lax.broadcasted_iota(jnp.int32, (T, T), 0)
    ci = lax.broadcasted_iota(jnp.int32, (T, T), 1)
    allowed = (ri >= ci) & (aux[:, 9:10] == aux_t[9:10, :])
    mask = jnp.where(allowed, 0.0, LOW)
    delta = spread(aux, 3)
    fed = x[0] * delta[0], x[1] * delta[1]
    lo = lanes(T) < 64
    fed_h = (
        jnp.where(lo, fed[0], 0.0).astype(bf16),
        jnp.where(lo, 0.0, fed[0]).astype(bf16),
        fed[1].astype(bf16),
    )
    skip = skip_pair(hp_ref)
    y = [x[0] * skip[0], x[1] * skip[1]]
    for h in range(3):
        decay = jnp.exp(aux[:, h : h + 1] - aux_t[h : h + 1, :] + mask)
        m_ref[h] = decay.astype(bf16)
        mixing = (decay * scores).astype(bf16)
        mg_ref[h] = mixing
        y[h // 2] = y[h // 2] + dot(mixing, fed_h[h])
    y_ref[:, 0:128] = y[0]
    y_ref[:, 128:256] = y[1]
    back = dot(cot_ref[...], w_ref[:, 384:640])
    dn_ref[:, 0:128] = back[:, 0:128]
    dn_ref[:, 128:256] = jnp.where(lo, back[:, 128:256], 0.0)


def decay_rows(tail):
    both = tail[0:3] + tail[3:6]
    return jnp.concatenate(
        [jnp.broadcast_to(both[h : h + 1], (64, 128)) for h in range(3)], axis=0
    )


def in_place(here, refs, rows):
    pieces = [r[rows, :].astype(f32) for r in refs]
    placed = []
    for p in range(4):
        by = lax.rem(here + 4 - p, 4)
        piece = pieces[0]
        for k in (1, 2, 3):
            piece = jnp.where(by == k, pieces[k], piece)
        placed.append(piece)
    return placed


def fold(here, states, tails, reverse):
    total = entering = jnp.zeros((192, 128), f32)
    passed = whole = jnp.ones((192, 128), f32)
    for p in reversed(range(4)) if reverse else range(4):
        decay = decay_rows(tails[p])
        before = (p > here) if reverse else (p < here)
        total = decay * total + states[p]
        entering = jnp.where(before, total, entering)
        passed = jnp.where(before, passed * decay, passed)
        whole = whole * decay
    return total, entering, passed, whole


def group_kernel(at_ref, a_ref, b_ref, c_ref, d_ref, send_ref, own_ref, passed_ref, tail_ref):
    here = lax.rem(at_ref[0], 4)
    refs = (a_ref, b_ref, c_ref, d_ref)
    states = in_place(here, refs, slice(0, 192))
    tails = in_place(here, refs, slice(192, SROWS))
    total, entering, passed, whole = fold(here, states, tails, False)
    own_ref[...] = entering
    passed_ref[...] = passed
    send_ref[0:192, :] = total.astype(bf16)
    sub = lax.broadcasted_iota(jnp.int32, (16, 128), 0)
    tail = jnp.zeros((16, 128), f32)
    for h in range(3):
        row = whole[64 * h : 64 * h + 1]
        high = row.astype(bf16).astype(f32)
        tail = jnp.where(sub == h, high, tail)
        tail = jnp.where(sub == 3 + h, row - high, tail)
    send_ref[192:SROWS, :] = tail.astype(bf16)
    for p in range(4):
        tail_ref[16 * p : 16 * p + 16, :] = tails[p]


def group_back_kernel(
    at_ref, a_ref, b_ref, c_ref, d_ref, tail_ref, after_ref, send_ref, own_ref, passed_ref
):
    del after_ref
    here = lax.rem(at_ref[0], 4)
    states = in_place(here, (a_ref, b_ref, c_ref, d_ref), slice(0, 192))
    tails = [tail_ref[16 * p : 16 * p + 16, :] for p in range(4)]
    total, entering, passed, _ = fold(here, states, tails, True)
    own_ref[...] = entering
    passed_ref[...] = passed
    send_ref[...] = total.astype(bf16)


def enter_kernel(
    at_ref, s0_ref, s1_ref, s2_ref, s3_ref, own_ref, passed_ref, y0_ref, dn_ref, c_ref,
    aux_ref, tap_ref, y_ref, state_ref, stat_ref, tail_ref,
):
    here = jnp.right_shift(at_ref[0], 2)
    refs = (s0_ref, s1_ref, s2_ref, s3_ref)
    states = in_place(here, refs, slice(0, 192))
    tails = in_place(here, refs, slice(192, SROWS))
    for p in range(4):
        tail_ref[16 * p : 16 * p + 16, :] = tails[p]
    _, entering, _, _ = fold(here, states, tails, False)
    state = passed_ref[...] * entering + own_ref[...]
    state_ref[0:192] = state
    state_ref[192:256] = jnp.zeros((64, 128), f32)
    c_mat = silu(c_ref[:, 512:640]).astype(bf16)
    carried = dot(c_mat, state_ref[...].astype(bf16), 1, 1)
    aux = aux_ref[...]
    keeper = spread(aux, 10)
    gate = gate_pair(*[silu(c_ref[:, 128 * k : 128 * (k + 1)]) for k in range(3)])
    squares = jnp.zeros((T, 1), f32)
    inner = jnp.zeros((T, 1), f32)
    for k in range(2):
        at = slice(128 * k, 128 * (k + 1))
        y = y0_ref[:, at] + keeper[k] * carried[:, at]
        y_ref[:, at] = y
        gated = y * gate[k]
        fed = gated * tap_ref[0:1, 384 + 128 * k : 512 + 128 * k]
        squares = squares + jnp.sum(gated * gated, axis=1, keepdims=True)
        inner = inner + jnp.sum(fed * dn_ref[:, at], axis=1, keepdims=True)
    lane = lanes(T)
    both = jnp.where(lane == 0, squares, jnp.where(lane == 1, inner, 0.0)).T
    stat_ref[...] = both[0:8]


def gated_kernel(
    s0_ref, s1_ref, s2_ref, s3_ref, y_ref, dn_ref, c_ref, aux_ref, tap_ref,
    dy_ref, dgate_ref, nout_ref, send_ref, rows_ref,
):
    total = s0_ref[...] + s1_ref[...] + s2_ref[...] + s3_ref[...]
    total = jnp.concatenate([total, jnp.zeros((120, T), f32)], axis=0).T
    rms = lax.rsqrt(total[:, 0:1] / DI + norm_eps)
    coef = rms * rms * rms * total[:, 1:2] / DI
    aux = aux_ref[...]
    keeper = spread(aux, 10)
    raw = gate_pair(*[c_ref[:, 128 * k : 128 * (k + 1)] for k in range(3)])
    x = x_pair(*[silu(c_ref[:, 128 * k : 128 * (k + 1)]) for k in range(3)])
    kept = []
    rows_ref[...] = jnp.zeros_like(rows_ref)
    for k in range(2):
        at = slice(128 * k, 128 * (k + 1))
        gain = tap_ref[0:1, 384 + 128 * k : 512 + 128 * k]
        s = sig(raw[k])
        gate = raw[k] * s
        y = y_ref[:, at]
        gated = y * gate
        dn = dn_ref[:, at]
        scaled = gated * rms
        nout_ref[:, at] = (scaled * gain).astype(bf16)
        d_gated = rms * gain * dn - gated * coef
        dy = d_gated * gate
        dy_ref[:, at] = dy
        dgate_ref[:, at] = d_gated * y * s * (1.0 + raw[k] * (1.0 - s))
        kept.append((dy * keeper[k]).astype(bf16))
        rows_ref[0:1, at] = jnp.sum(dn * scaled, axis=0, keepdims=True)
        rows_ref[1:2, at] = jnp.sum(dy * x[k], axis=0, keepdims=True)
    c_mat = silu(c_ref[:, 512:640]).astype(bf16)
    send_ref[...] = dot(jnp.concatenate(kept, axis=1), c_mat, 0, 0)[0:192].astype(bf16)


def halves(ref, core):
    keep = ref[pl.ds(pl.multiple_of(core * 256, 256), 256), :]
    give = ref[pl.ds(pl.multiple_of(256 - core * 256, 256), 256), :]
    return keep.astype(bf16), give.astype(bf16)


def out_kernel(at_ref, nout_ref, w_ref, keep_ref, give_ref, norm_ref):
    norm_ref[...] = dot(nout_ref[...], w_ref[:, 384:640], 1, 1)
    keep_ref[...], give_ref[...] = halves(norm_ref, at_ref[2])


def clear_edges(pad_ref):
    pad_ref[0:HALO] = jnp.zeros((HALO, 128), f32)
    pad_ref[HALO + T :] = jnp.zeros((HALO, 128), f32)


def conv_back(d_conv, taps, v_ref, at, valid, pad_ref):
    sums = [None, None, None, None, jnp.sum(d_conv, axis=0, keepdims=True)]
    sums[3] = jnp.sum(d_conv * v_ref[HALO:, at], axis=0, keepdims=True)
    pad_ref[HALO : HALO + T] = taps[3:4] * d_conv
    acc = pad_ref[0 : HALO + T]
    for lag in (1, 2, 3):
        masked = d_conv * valid[lag - 1]
        sums[3 - lag] = jnp.sum(
            masked * v_ref[pl.ds(HALO - lag, T), at], axis=0, keepdims=True
        )
        pad_ref[HALO : HALO + T] = taps[3 - lag : 4 - lag] * masked
        acc = acc + pad_ref[pl.ds(lag, HALO + T)]
    return acc, sums


def own_back_kernel(
    dy_ref, y_ref, y0_ref, c_ref, aux_ref, m_ref, mg_ref, state_ref,
    v_ref, ctap_ref, st_ref,
    dx_ref, db_ref, dcum_ref, xs_ref, b_ref, slope_ref, dvc_ref, crow_ref,
    pad_ref,
):
    aux = aux_ref[...]
    aux_t = aux.T
    act = []
    for k in range(5):
        at = slice(128 * k, 128 * (k + 1))
        v = c_ref[:, at]
        s = sig(v)
        act.append(v * s)
        slope = s * (1.0 + v * (1.0 - s))
        if k < 4:
            slope_ref[:, at] = slope
    x = x_pair(*act[:3])
    xs_ref[:, 0:128] = x[0]
    xs_ref[:, 128:256] = x[1]
    b_ref[...] = act[3].astype(bf16)
    b_low, c_low = act[3].astype(bf16), act[4].astype(bf16)
    dy = pair_of(dy_ref)
    lo = lanes(T) < 64
    dy_h = (
        jnp.where(lo, dy[0], 0.0).astype(bf16),
        jnp.where(lo, 0.0, dy[0]).astype(bf16),
        dy[1].astype(bf16),
    )
    x_low = x[0].astype(bf16), x[1].astype(bf16)
    lane = lanes(T)
    dx = [jnp.zeros((T, 128), f32), jnp.zeros((T, 128), f32)]
    spread_sum = jnp.zeros((T, T), f32)
    rows = jnp.zeros((T, 128), f32)
    cols = jnp.zeros((128, T), f32)
    sub = lax.broadcasted_iota(jnp.int32, (128, T), 0)
    for h in range(3):
        pairs = dot(dy_h[h], x_low[h // 2], 1, 1) * aux_t[3 + h : 4 + h, :]
        mixing = mg_ref[h]
        spread_sum = spread_sum + pairs * m_ref[h].astype(f32)
        weights = pairs * mixing.astype(f32)
        rows = jnp.where(lane == h, jnp.sum(weights, axis=1, keepdims=True), rows)
        cols = jnp.where(sub == h, jnp.sum(weights, axis=0, keepdims=True), cols)
        dx[h // 2] = dx[h // 2] + dot(mixing, dy_h[h], 0, 0)
    low = spread_sum.astype(bf16)
    keeper = spread(aux, 10)
    kept = jnp.concatenate([dy[0] * keeper[0], dy[1] * keeper[1]], axis=1).astype(bf16)
    d_c = dot(low, b_low) + dot(kept, state_ref[...].astype(bf16))
    valid = valid_masks(column_of(st_ref))
    clear_edges(pad_ref)
    dv, sums = conv_back(d_c * slope, ctap_ref[0:5, 128:256], v_ref, slice(512, 640), valid, pad_ref)
    dvc_ref[...] = dv.astype(bf16)
    crow_ref[...] = jnp.concatenate([*sums, jnp.zeros((3, 128), f32)], axis=0)
    db_ref[...] = dot(low, c_low, 0, 0)
    dx_ref[:, 0:128] = dx[0]
    dx_ref[:, 128:256] = dx[1]
    carried = [
        dy[k] * (y_ref[:, 128 * k : 128 * (k + 1)] - y0_ref[:, 128 * k : 128 * (k + 1)])
        for k in range(2)
    ]
    dcum_ref[...] = rows - cols.T + head_sums(carried)


def back_kernel(
    at_ref, a0_ref, a1_ref, a2_ref, a3_ref, own_ref, passed_ref, tails_ref, mine_ref,
    state_ref, dx_ref, db_ref, dcum_ref, xs_ref, b_ref, slope_ref,
    dvc_ref, crow_ref, aux_ref, v_ref, tap_ref, ctap_ref, hp_ref, st_ref, dy_ref, dgate_ref,
    w_ref, wide_ref, rows_ref, hid_ref, halo_ref,
    dv_ref, dstep_ref, keep_ref, give_ref, edge_ref, chan_ref, conv_ref, gain_ref,
    pad_ref, norm_ref,
):
    here = jnp.right_shift(at_ref[0], 2)
    states = in_place(here, (a0_ref, a1_ref, a2_ref, a3_ref), slice(0, 192))
    tails = [tails_ref[16 * p : 16 * p + 16, :] for p in range(4)]
    _, entering, _, _ = fold(here, states, tails, True)
    adj = passed_ref[...] * entering + own_ref[...]
    aux = aux_ref[...]
    lane = lanes(T)
    x = pair_of(xs_ref)
    b_low = b_ref[...]
    delta, ending = spread(aux, 3), spread(aux, 13)
    adj_low = jnp.concatenate([adj, jnp.zeros((64, 128), f32)], axis=0).astype(bf16)
    through_b = dot(b_low, adj_low, 1, 1)
    skip = skip_pair(hp_ref)
    dy = pair_of(dy_ref)
    ended, extra, full, d_x = [], [], [], []
    for k in range(2):
        at = slice(128 * k, 128 * (k + 1))
        late = ending[k] * through_b[:, at]
        total = dx_ref[:, at] + late
        d_x.append(delta[k] * total + skip[k] * dy[k])
        full.append(x[k] * total)
        extra.append(x[k] * late)
        ended.append(x[k] * delta[k] * ending[k])
    d_b = db_ref[...] + dot(jnp.concatenate(ended, axis=1).astype(bf16), adj_low)
    d_delta = head_sums(full)
    tail = head_sums(extra) * rolled(aux, -3)
    tail = jnp.where(lane < 3, tail, 0.0)
    d_cum = dcum_ref[...] - tail
    ri = lax.broadcasted_iota(jnp.int32, (T, T), 0)
    ci = lax.broadcasted_iota(jnp.int32, (T, T), 1)
    upper = jnp.where(ci >= ri, 1.0, 0.0).astype(bf16)
    d_log = joined(dot(upper, three_parts(d_cum).astype(bf16)))
    own = decay_rows(mine_ref[192:SROWS, :].astype(f32))
    met = own * adj * state_ref[0:192]
    lane1 = lanes(1)
    meets = jnp.zeros((1, 128), f32)
    for h in range(3):
        meets = jnp.where(lane1 == h, jnp.sum(met[64 * h : 64 * h + 64]), meets)
    d_log = d_log + jnp.sum(tail, axis=0, keepdims=True) + meets
    d_log = jnp.where(lane < 3, d_log, 0.0)
    rate = jnp.exp(head_row(hp_ref, 1))
    d_raw = (d_delta - rate * d_log) * rolled(aux, -6)
    d_raw = jnp.where(lane < 3, d_raw, 0.0)
    delta_cols = jnp.where(lane < 3, rolled(aux, -3), 0.0)
    step_low = half(d_raw).astype(bf16)
    dstep_ref[...] = step_low

    d_gate = pair_of(dgate_ref)
    x_tiles = head_tiles((jnp.zeros_like(d_x[0]),) * 2, d_x)
    gate_tiles = head_tiles(d_gate, (jnp.zeros_like(d_x[0]),) * 2)
    lo = lane < 64
    valid = valid_masks(column_of(st_ref))
    clear_edges(pad_ref)
    tap_rows = []
    for k in range(4):
        at = slice(128 * k, 128 * (k + 1))
        slope = slope_ref[:, at]
        if k < 3:
            d_conv = jnp.where(lo, gate_tiles[k], x_tiles[k] * slope)
            taps = tap_ref[0:5, at]
        else:
            d_conv = d_b * slope
            taps = ctap_ref[0:5, 0:128]
        dv, sums = conv_back(d_conv, taps, v_ref, at, valid, pad_ref)
        dv_ref[:, at] = dv.astype(bf16)
        tap_rows.append(sums)
    dv_ref[:, 512:640] = dvc_ref[...]
    tap_rows.append([crow_ref[j : j + 1, :] for j in range(5)])

    chan_ref_rows = []
    for j in range(5):
        pair = x_pair(*[tap_rows[k][j] for k in range(3)])
        chan_ref_rows.append(jnp.concatenate(pair, axis=1))
    chan_ref_rows.append(rows_ref[0:1, :])
    h0 = jnp.sum(d_raw, axis=0, keepdims=True)
    h1 = jnp.sum(d_log * (-rate) * delta_cols, axis=0, keepdims=True)
    h2 = head_sums((rows_ref[1:2, 0:128], rows_ref[1:2, 128:256]))
    zero = jnp.zeros((1, 128), f32)
    for r in (h0, h1, h2):
        chan_ref_rows.append(jnp.concatenate([r, zero], axis=1))
    for j, r in enumerate(chan_ref_rows):
        chan_ref[j : j + 1, :] = r
    chan_ref[9:16, :] = jnp.zeros((7, 256), f32)
    for j in range(5):
        conv_ref[j : j + 1, :] = jnp.concatenate([tap_rows[3][j], tap_rows[4][j]], axis=1)
    conv_ref[5:8, :] = jnp.zeros((3, 256), f32)

    d_norm = dot(dv_ref[:, 0:384], w_ref[:, 0:384], 1, 1)
    d_norm = d_norm + dot(dv_ref[:, 384:640], wide_ref[...], 1, 1)
    main = d_norm[HALO:] + dot(step_low, w_ref[:, 512:640], 1, 1)
    norm_ref[...] = main
    keep_ref[...], give_ref[...] = halves(norm_ref, at_ref[2])
    edge_ref[...] = d_norm[0:HALO].astype(bf16)
    total = jnp.zeros((1, D), f32)
    for src, val in ((halo_ref, d_norm[0:HALO]), (hid_ref, main)):
        h = src[...].astype(f32)
        inv = lax.rsqrt(jnp.mean(h * h, axis=1, keepdims=True) + norm_eps)
        total = total + jnp.sum(val * (h * inv), axis=0, keepdims=True)
    gain_ref[0:1] = total
    gain_ref[1:8] = jnp.zeros((7, D), f32)


def picked(rows, head):
    a = lax.broadcasted_iota(jnp.int32, (rows, D), 0)
    d = lax.broadcasted_iota(jnp.int32, (rows, D), 1)
    return jnp.where(d - slab_rows(a) == 6 * head, 1.0, 0.0).astype(bf16)


def grad_kernel(
    at_ref, normed_ref, dv_ref, dstep_ref, nout_ref, cot_ref, conv_ref, gain_ref, chan_ref,
    a0, a1, out_ref, keep_ref, give_ref, slab_ref,
):
    del a0, a1
    normed = normed_ref[...]
    slab_ref[:, 0:256] = dot(normed, dv_ref[:, 384:640], 0, 0).astype(bf16)
    grads = jnp.concatenate([jnp.zeros((MISC + 5, 256), f32), conv_ref[0:5, :]], axis=0)
    grads = jnp.concatenate([grads, jnp.zeros((128 - MISC - 10, 256), f32)], axis=0)
    sub = lax.broadcasted_iota(jnp.int32, (128, D), 0)
    column = jnp.where(sub == MISC + 3, gain_ref[0:1], 0.0).T
    slab_ref[:, 256:384] = (dot(selector(), grads.astype(bf16), 1, 1) + column).astype(bf16)
    slab = slab_ref[...]
    for x in range(4):
        rows = slice(96 * x, 96 * x + 96)
        keep_ref[rows, :] = dot(picked(96, 2 * x + at_ref[2]), slab).astype(bf16)
        give_ref[rows, :] = dot(picked(96, 2 * x + 1 - at_ref[2]), slab).astype(bf16)
    out_ref[:, 0:384] = dot(normed, dv_ref[:, 0:384], 0, 0).astype(bf16)
    outs = dot(cot_ref[...], nout_ref[...], 0, 0)
    out_ref[:, 384:512] = outs[:, 0:128].astype(bf16)
    tile = outs[:, 128:256] + dot(normed_ref[HALO:, :], dstep_ref[...], 0, 0)
    turned = jnp.concatenate([chan_ref[...], jnp.zeros((112, 256), f32)], axis=0).T
    shared = jnp.zeros((48, 128), f32)
    for g in range(4):
        piece = turned[48 * g : 48 * g + 48]
        piece = jnp.where(lanes(48) < (9 if g == 0 else 6), piece, 0.0)
        shared = shared + rolled(piece, CHAN[g])
    out_ref[:, 512:640] = (tile + jnp.concatenate([shared] * N_SEQ, axis=0)).astype(bf16)


def slab_pair_kernel(at_ref, keep_ref, got_ref, after_ref, own_ref, s1, s2, s3, sum_ref):
    del after_ref
    sum_ref[...] = keep_ref[...].astype(f32) + got_ref[...].astype(f32)
    for by, ref in enumerate((own_ref, s1, s2, s3)):
        start = pl.multiple_of(lax.rem(at_ref[1] + by, 4) * 96, 96)
        ref[...] = sum_ref[pl.ds(start, 96), :].astype(bf16)


def merge_kernel(a_ref, b_ref, c_ref, d_ref, pack_ref, out_ref):
    total = a_ref[...].astype(f32) + b_ref[...].astype(f32)
    total = total + c_ref[...].astype(f32) + d_ref[...].astype(f32)
    misc = total[:, 256:384]
    lane = lanes(96)
    d = lax.broadcasted_iota(jnp.int32, (D, 96), 0)
    a = lax.broadcasted_iota(jnp.int32, (D, 96), 1)
    gap = d - slab_rows(a)
    places, laid = [], []
    for j in range(8):
        tile = rolled(total[:, 128 * (j // 4) : 128 * (j // 4) + 128], SLAB - 32 * (j % 4))
        one = misc if j == 0 else rolled(misc, -1 - j)
        laid.append(
            jnp.where(lane >= SLAB, tile, jnp.where((lane == MISC + 3) & (j < 6), one, 0.0))
        )
        places.append(jnp.where(gap == 6 * j, 1.0, 0.0))
    added = dot(
        jnp.concatenate(places, axis=1).astype(bf16),
        jnp.concatenate(laid, axis=0).astype(bf16),
    )
    out_ref[:, 0:512] = pack_ref[:, 0:512]
    out_ref[:, 512:640] = (pack_ref[:, 512:640].astype(f32) + added).astype(bf16)


def pair_kernel(
    at_ref, keep_ref, got_ref, edge0_ref, edge1_ref, out_keep_ref, out_got_ref,
    own_ref, s1, s2, s3, sum_ref,
):
    sum_ref[0:256] = keep_ref[...].astype(f32) + got_ref[...].astype(f32)
    sum_ref[256 - HALO : 256] += edge0_ref[...].astype(f32) + edge1_ref[...].astype(f32)
    sum_ref[256:512] = out_keep_ref[...].astype(f32) + out_got_ref[...].astype(f32)
    for by, ref in enumerate((own_ref, s1, s2, s3)):
        start = pl.multiple_of(lax.rem(at_ref[1] + by, 4) * 64, 64)
        for k in range(2):
            ref[64 * k : 64 * k + 64] = sum_ref[pl.ds(256 * k + start, 64), :].astype(bf16)


def four_kernel(at_ref, a_ref, b_ref, c_ref, d_ref, hid_ref, out_ref):
    total = a_ref[...].astype(f32) + b_ref[...].astype(f32)
    total = total + c_ref[...].astype(f32) + d_ref[...].astype(f32)
    start = pl.multiple_of((4 * at_ref[2] + at_ref[1]) * 64, 64)
    out_ref[:, 0:D] = total[0:64].astype(bf16)
    out_ref[:, D:] = (total[64:128] + hid_ref[pl.ds(start, 64), :].astype(f32)).astype(bf16)


def input_kernel(*refs):
    at_ref, refs = refs[0], refs[1:]
    hid_ref, cot_ref, row_ref, out_ref, block_ref = refs[8:]
    for side in range(2):
        core = at_ref[2] if side == 0 else 1 - at_ref[2]
        for by in range(4):
            block = core * 4 + lax.rem(at_ref[1] + 4 - by, 4)
            rows = pl.ds(pl.multiple_of(block * 64, 64), 64)
            piece = refs[4 * side + by]
            h = hid_ref[rows, :].astype(f32)
            inv = lax.rsqrt(jnp.mean(h * h, axis=1, keepdims=True) + norm_eps)
            d_scaled = piece[:, 0:D].astype(f32) * row_ref[0:1, :]
            inner = jnp.sum(d_scaled * h, axis=1, keepdims=True)
            out_ref[rows, :] = (
                cot_ref[rows, :].astype(f32)
                + inv * d_scaled
                - h * (inv * inv * inv * inner / D)
            )
            block_ref[rows, :] = piece[:, D:]


def adam(weight, grad, first, second, rate):
    first_new = beta_one * first + (1.0 - beta_one) * grad
    second_new = beta_two * second + (1.0 - beta_two) * grad * grad
    first_hat = first_new / (1.0 - beta_one**STEP)
    second_hat = second_new / (1.0 - beta_two**STEP)
    weight_new = weight - rate * (
        first_hat / (jnp.sqrt(second_hat) + adam_eps) + decay_rate * weight
    )
    return first_new, second_new, weight_new


RATE_D = 1.4 * D ** (-0.5)
RATE_I = 1.4 * DI ** (-0.5)


def put(refs, at, values):
    for ref, value in zip(refs, values):
        ref[at] = value


def update_kernel(*refs):
    grad_ref, refs = refs[0], refs[1:]
    proj, step, out, chan, head, shared, gain, conv = (
        refs[3 * k : 3 * k + 3] for k in range(8)
    )
    outs = refs[24:]
    proj_o, step_o, out_o, chan_o, head_o, shared_o, gain_o, conv_o = (
        outs[3 * k : 3 * k + 3] for k in range(8)
    )
    wide_ref, conv_ref = outs[24:]
    total = grad_ref[0].astype(f32)
    for q in range(1, N_SEQ):
        total = total + grad_ref[q].astype(f32)
    misc = total[:, 512:640]
    for h in range(3):
        w, m, v = (r[h] for r in proj)
        put(proj_o, h, adam(w, total[:, 128 * h : 128 * (h + 1)], m, v, RATE_D))
        tile = total[:, 384 + 128 * (h // 2) : 512 + 128 * (h // 2)]
        tile = half(tile) if h == 1 else tile
        w, m, v = (r[h] for r in out)
        put(out_o, h, adam(w, tile[:, 0:64], m, v, RATE_I))
    turned = jnp.concatenate([misc, jnp.zeros((80, 128), f32)], axis=0).T
    at = (slice(None), slice(None))
    w, m, v = (r[at] for r in step)
    put(step_o, at, adam(w, turned[MISC : MISC + 3, 0:48], m, v, RATE_D))
    p = [turned[CHAN[g] : CHAN[g] + 9] for g in range(4)]
    lane = lanes(9)
    wrapped = rolled(p[2], 96)
    pair = (
        p[0] + rolled(p[1], 48) + jnp.where(lane >= 96, wrapped, 0.0),
        jnp.where(lane < 16, wrapped, 0.0) + rolled(p[3], 16),
    )
    for h in range(3):
        piece = half(pair[0]) if h == 1 else pair[h // 2]
        spot = (slice(None), h, slice(None))
        w, m, v = (r[spot] for r in chan)
        put(chan_o, spot, adam(w, piece[0:6, 0:64], m, v, 0.5))
    w, m, v = (r[at] for r in head)
    put(head_o, at, adam(w, p[0][6:9, 0:3], m, v, 1.0))
    lane = lanes(6)
    for t in range(2):
        tile = jnp.zeros((6, 128), f32)
        for i in range(4):
            j = 4 * t + i
            own = jnp.where(lane >= SLAB, misc[6 * j : 6 * j + 6], 0.0)
            tile = tile + rolled(own, 32 * i - SLAB)
        wide_ref[:, 128 * t : 128 * t + 128] = tile
    w, m, v = (r[at] for r in shared)
    put(shared_o, at, adam(w, wide_ref[...], m, v, RATE_D))
    column = turned[MISC + 3 : MISC + 4]
    w, m, v = (r[at] for r in gain)
    put(gain_o, at, adam(w, column[:, 0:6], m, v, 0.5))
    lane = lanes(2)
    taps = jnp.zeros((2, 128), f32)
    for t in range(5):
        taps = jnp.where(
            lane == t, misc[6 + 6 * t : 8 + 6 * t, MISC + 3 : MISC + 4], taps
        )
    conv_ref[...] = taps
    w, m, v = (r[at] for r in conv)
    put(conv_o, at, adam(w, conv_ref[:, 0:5], m, v, 0.5))


def exchange(blocks, axis):
    return lax.all_to_all(blocks, axis, 0, 0, tiled=True)


def around(a, axis, by):
    peers = lax.axis_size(axis)
    return lax.ppermute(a, axis, [(i, (i + by) % peers) for i in range(peers)])


def to_next(a):
    return lax.ppermute(a, SEQ, [(i, i + 1) for i in range(N_SEQ - 1)])


def to_previous(a, core):
    pairs = [(2 * i + 2 + core, 2 * i + 1) for i in range(N_SEQ - 1)]
    return lax.ppermute(a, SEQ + ("head_1",), pairs)


def body(
    hidden_in, cotangent, doc_starts, proj_weight, step_weight, out_weight, shared_weight,
    pre_gain, channel_params, head_params, shared_conv, proj_first, proj_second, step_first,
    step_second, out_first, out_second, shared_first, shared_second, gain_first, gain_second,
    channel_first, channel_second, head_first, head_second, conv_first, conv_second,
):
    where = jnp.stack(
        [lax.axis_index(SEQ), lax.axis_index("head_0"), lax.axis_index("head_1")]
    ).astype(jnp.int32)
    halo = to_next(hidden_in[T - HALO :])
    matrices = [jnp.transpose(a, (1, 0, 2)) for a in (proj_weight, proj_first, proj_second)]
    steps = [a.T for a in (step_weight, step_first, step_second)]
    out_weights = [jnp.transpose(a, (0, 2, 1)) for a in (out_weight, out_first, out_second)]
    gains_in = [a.reshape(1, 6) for a in (pre_gain, gain_first, gain_second)]

    (pack,) = call(
        pack_kernel, [((N_SEQ, 48, NW), bf16)],
        matrices[0], out_weights[0], steps[0], shared_weight, gains_in[0], shared_conv,
        scratch=[pltpu.VMEM((128, 128), f32), pltpu.VMEM((48, 128), f32)], name="pack",
    )
    weights = exchange(pack, SEQ).reshape(D, NW)
    (slab,) = call(slab_kernel, [((96, 384), bf16)], weights, name="slab")
    near = [slab] + [around(slab, "head_0", by) for by in (1, 2, 3)]
    slabs = near + [around(a, "head_1", 1) for a in near]

    marks = doc_starts.astype(f32).reshape(1, T)
    fixed = jnp.broadcast_to(
        (jnp.arange(6) == 3).astype(f32)[:, None, None], channel_params.shape
    )
    taps = jnp.concatenate([fixed, channel_params], axis=2).reshape(6, 384)
    gains = jnp.pad(channel_params[5].reshape(1, 192), ((0, 5), (0, 64)))
    taps = jnp.pad(jnp.concatenate([taps, gains], axis=1), ((0, 2), (0, 0)))

    normed, values, conv, aux, sent, row, wide, conv_taps = call(
        first_kernel,
        [
            ((HALO + T, D), bf16), ((HALO + T, NV), f32), ((T, NV), f32), ((T, 128), f32),
            ((SROWS, 128), bf16), ((8, D), f32), ((D, 256), bf16), ((8, 256), f32),
        ],
        where, *slabs, hidden_in, halo, marks, weights, taps, head_params, smem=(0, 14),
        scratch=[pltpu.VMEM((D, 384), bf16)], name="first",
    )
    states = [sent] + [around(sent, "seq_1", by) for by in (1, 2, 3)]
    group, group_in, group_passed, group_tails = call(
        group_kernel,
        [((SROWS, 128), bf16), ((192, 128), f32), ((192, 128), f32), ((64, 128), f32)],
        where, *states, smem=(0,), name="group",
    )
    groups = [group] + [around(group, "seq_0", by) for by in (1, 2, 3)]
    y_own, d_normed, decays, mixing = call(
        own_kernel,
        [((T, 256), f32), ((T, 256), f32), ((3, T, T), bf16), ((3, T, T), bf16)],
        conv, aux, cotangent, weights, head_params, smem=(4,), name="own",
    )
    y_full, state, stat, all_tails = call(
        enter_kernel,
        [((T, 256), f32), ((256, 128), f32), ((8, T), f32), ((64, 128), f32)],
        where, *groups, group_in, group_passed, y_own, d_normed, conv, aux, taps, smem=(0,), name="enter",
    )
    stat = stat + around(stat, "head_1", 1)
    stats = [stat] + [around(stat, "head_0", by) for by in (1, 2, 3)]
    d_y, d_gate, normed_out, sent_adj, rows = call(
        gated_kernel,
        [
            ((T, 256), f32), ((T, 256), f32), ((T, 256), bf16),
            ((192, 128), bf16), ((8, 256), f32),
        ],
        *stats, y_full, d_normed, conv, aux, taps, name="gated",
    )
    adjoints = [sent_adj] + [around(sent_adj, "seq_1", by) for by in (1, 2, 3)]
    half_rows = ((T // 2, D), bf16)
    out_keep, out_give = call(
        out_kernel, [half_rows] * 2, where, normed_out, weights, smem=(0,),
        scratch=[pltpu.VMEM((T, D), f32)], name="out",
    )
    out_taken = around(out_give, "head_1", 1)
    group, adj_in, adj_passed = call(
        group_back_kernel,
        [((192, 128), bf16), ((192, 128), f32), ((192, 128), f32)],
        where, *adjoints, group_tails, out_keep, smem=(0,), anywhere=(6,), name="group_back",
    )
    groups = [group] + [around(group, "seq_0", by) for by in (1, 2, 3)]
    piece = ((T // N_HEAD, D), bf16)
    d_x, d_b, d_cum, x_act, b_act, slopes, d_value_c, c_rows = call(
        own_back_kernel,
        [
            ((T, 256), f32), ((T, 128), f32), ((T, 128), f32), ((T, 256), f32),
            ((T, 128), bf16), ((T, 512), f32), ((HALO + T, 128), bf16), ((8, 128), f32),
        ],
        d_y, y_full, y_own, conv, aux, decays, mixing, state, values, conv_taps, marks,
        scratch=[pltpu.VMEM((T + 2 * HALO, 128), f32)], name="own_back",
    )
    d_values, d_step, keep, give, edge, chan, d_conv, d_gain = call(
        back_kernel,
        [
            ((HALO + T, NV), bf16), ((T, 128), bf16), half_rows, half_rows,
            ((HALO, D), bf16), ((16, 256), f32), ((8, 256), f32), ((8, D), f32),
        ],
        where, *groups, adj_in, adj_passed, all_tails, sent, state, d_x, d_b, d_cum, x_act, b_act, slopes, d_value_c,
        c_rows, aux, values, taps, conv_taps, head_params, marks, d_y, d_gate, weights, wide,
        rows, hidden_in, halo,
        smem=(0, 22),
        scratch=[pltpu.VMEM((T + 2 * HALO, 128), f32), pltpu.VMEM((T, D), f32)],
        name="back",
    )
    taken = around(give, "head_1", 1)
    edges = [to_previous(edge, core) for core in range(2)]
    slab_rows_all = ((384, 384), bf16)
    grads, slab_keep, slab_give = call(
        grad_kernel, [((D, NW), bf16), slab_rows_all, slab_rows_all],
        where, normed, d_values, d_step, normed_out, cotangent, d_conv, d_gain, chan,
        *edges, smem=(0,), anywhere=(9, 10),
        scratch=[pltpu.VMEM((D, 384), bf16)], name="grad",
    )
    slab_taken = around(slab_give, "head_1", 1)
    pieces = call(
        pair_kernel, [((T // 4, D), bf16)] * 4, where, keep, taken, *edges, out_keep,
        out_taken, smem=(0,), scratch=[pltpu.VMEM((T, D), f32)], name="pair",
    )
    parts = [pieces[0]] + [around(pieces[by], "head_0", by) for by in (1, 2, 3)]
    slab_piece = ((96, 384), bf16)
    slabs = call(
        slab_pair_kernel, [slab_piece] * 4, where, slab_keep, slab_taken, pieces[0],
        smem=(0,), anywhere=(3,),
        scratch=[pltpu.VMEM((384, 384), f32)], name="slab_pair",
    )
    slabs = [slabs[0]] + [around(slabs[by], "head_0", by) for by in (1, 2, 3)]

    (grads,) = call(merge_kernel, [((D, NW), bf16)], *slabs, grads, name="merge")
    grads, parts = lax.optimization_barrier((grads, parts))
    grads = exchange(grads.reshape(N_SEQ, 48, NW), SEQ)
    (own,) = call(
        four_kernel, [((T // N_HEAD, 2 * D), bf16)], where, *parts, hidden_in,
        smem=(0,), name="four",
    )
    near = [own] + [around(own, "head_0", by) for by in (1, 2, 3)]
    far = [around(a, "head_1", 1) for a in near]
    input_grad, block_out = call(
        input_kernel, [((T, D), f32), ((T, D), bf16)], where, *near, *far, hidden_in, cotangent, row,
        smem=(0,), name="input",
    )

    proj, step, out = (3, 48, 128), (3, 48), (3, 48, 64)
    shapes = [proj] * 3 + [step] * 3 + [out] * 3 + [(6, 3, 64)] * 3 + [(3, 3)] * 3
    shapes += [(6, 256)] * 3 + [(1, 6)] * 3 + [(2, 5)] * 3
    updated = call(
        update_kernel, [(s, f32) for s in shapes],
        grads, *matrices, *steps, *out_weights, channel_params, channel_first,
        channel_second, head_params, head_first, head_second, shared_weight, shared_first,
        shared_second, *gains_in, shared_conv, conv_first, conv_second,
        scratch=[pltpu.VMEM((6, 256), f32), pltpu.VMEM((2, 128), f32)],
        params=WIDE, name="update",
    )
    return (
        block_out, input_grad,
        *(jnp.transpose(a, (1, 0, 2)) for a in updated[0:3]),
        *(a.T for a in updated[3:6]),
        *(jnp.transpose(a, (0, 2, 1)) for a in updated[6:9]),
        *updated[15:18],
        *(g.reshape(6) for g in updated[18:21]),
        *updated[9:15],
        *updated[21:24],
    )


def solution(mesh):
    finer = Mesh(mesh.devices.reshape(4, 4, 4, 2), SEQ_HEAD)
    matrix = P(SEQ, HEAD, None)
    step = P(SEQ, HEAD)
    out = P(HEAD, None, SEQ)
    both = P(SEQ_HEAD, None)
    gain = P(SEQ_HEAD)
    channel = P(None, HEAD, None)
    head = P(None, HEAD)
    tokens = P(SEQ, None)
    return jax.shard_map(
        body,
        mesh=finer,
        in_specs=(
            tokens, tokens, P(SEQ), matrix, step, out, both, gain, channel, head, both,
            matrix, matrix, step, step, out, out, both, both, gain, gain, channel, channel,
            head, head, both, both,
        ),
        out_specs=(
            (tokens, tokens)
            + (matrix,) * 3 + (step,) * 3 + (out,) * 3 + (both,) * 3 + (gain,) * 3
            + (channel,) * 3 + (head,) * 3 + (both,) * 3
        ),
        check_vma=False,
    )
```

```python
import functools

import jax
import jax.numpy as jnp
from jax import lax
from jax.experimental import pallas as pl
from jax.experimental.pallas import tpu as pltpu
from jax.sharding import Mesh
from jax.sharding import PartitionSpec as P

D = 768
DI = 1536
STEP = 10
SEQ = ("seq_0", "seq_1")
HEAD = ("head_0", "head_1")
SEQ_HEAD = SEQ + HEAD
N_SEQ = 16
N_HEAD = 8

T = 512
HALO = 16
NV = 640
NW = 640
MISC = 64
CHAN = (69, 78, 84, 90)
SLAB = 96
SROWS = 208

f32 = jnp.float32
bf16 = jnp.bfloat16
norm_eps = 1e-05
beta_one = 0.9
beta_two = 0.999
adam_eps = 1e-08
decay_rate = 0.01
LOW = -1e30

PARAMS = pltpu.CompilerParams(vmem_limit_bytes=32 * 1024 * 1024)
WIDE = pltpu.CompilerParams(vmem_limit_bytes=56 * 1024 * 1024)
VM = pl.BlockSpec(memory_space=pltpu.VMEM)
SM = pl.BlockSpec(memory_space=pltpu.SMEM)
ANY = pl.BlockSpec(memory_space=pl.ANY)


def call(kernel, outs, *args, smem=(), anywhere=(), scratch=(), params=PARAMS, name=None):
    return pl.pallas_call(
        kernel,
        out_shape=[jax.ShapeDtypeStruct(s, d) for s, d in outs],
        in_specs=[
            SM if i in smem else ANY if i in anywhere else VM for i in range(len(args))
        ],
        out_specs=[VM] * len(outs),
        scratch_shapes=list(scratch),
        compiler_params=params,
        name=name,
    )(*args)


def dot(a, b, ca=1, cb=0):
    return lax.dot_general(a, b, (((ca,), (cb,)), ((), ())), preferred_element_type=f32)


def lanes(rows):
    return lax.broadcasted_iota(jnp.int32, (rows, 128), 1)


def half(v):
    return pltpu.roll(v, 64, 1)


def rolled(v, by):
    return pltpu.roll(v, by % 128, 1)


def sig(v):
    return 1.0 / (1.0 + jnp.exp(-v))


def silu(v):
    return v * sig(v)


def dsilu(v):
    s = sig(v)
    return s * (1.0 + v * (1.0 - s))


def gate_pair(t0, t1, t2):
    lo = lanes(t0.shape[0]) < 64
    return jnp.where(lo, t0, half(t1)), jnp.where(lo, t2, 0.0)


def x_pair(t0, t1, t2):
    lo = lanes(t0.shape[0]) < 64
    return jnp.where(lo, half(t0), t1), jnp.where(lo, half(t2), 0.0)


def head_tiles(gate, x):
    lo = lanes(gate[0].shape[0]) < 64
    return (
        jnp.where(lo, gate[0], half(x[0])),
        jnp.where(lo, half(gate[0]), x[0]),
        jnp.where(lo, gate[1], half(x[1])),
    )


def spread(a, at):
    lo = lanes(a.shape[0]) < 64
    return (
        jnp.where(lo, a[:, at : at + 1], a[:, at + 1 : at + 2]),
        jnp.where(lo, a[:, at + 2 : at + 3], 0.0),
    )


def head_sums(pair):
    a, b = pair
    lane = lanes(a.shape[0])
    s0 = jnp.sum(jnp.where(lane < 64, a, 0.0), axis=1, keepdims=True)
    s1 = jnp.sum(jnp.where(lane < 64, 0.0, a), axis=1, keepdims=True)
    s2 = jnp.sum(b, axis=1, keepdims=True)
    return jnp.where(lane == 0, s0, jnp.where(lane == 1, s1, jnp.where(lane == 2, s2, 0.0)))


def pair_of(ref):
    return ref[:, 0:128], ref[:, 128:256]


def head_row(hp_ref, k, rows=1):
    lane = lanes(rows)
    return jnp.where(
        lane == 0,
        hp_ref[k, 0],
        jnp.where(lane == 1, hp_ref[k, 1], jnp.where(lane == 2, hp_ref[k, 2], 0.0)),
    )


def skip_pair(hp_ref):
    lane = lanes(1)
    return (
        jnp.where(lane < 64, hp_ref[2, 0], hp_ref[2, 1]),
        jnp.where(lane < 64, hp_ref[2, 2], 0.0),
    )


def three_parts(v):
    hi = v.astype(bf16).astype(f32)
    rest = v - hi
    mid = rest.astype(bf16).astype(f32)
    return hi + rolled(mid, 3) + rolled(rest - mid, 6)


def joined(v):
    total = v + rolled(v, -3) + rolled(v, -6)
    return jnp.where(lanes(v.shape[0]) < 3, total, 0.0)


def act_tiles(c_ref):
    return [silu(c_ref[:, 128 * k : 128 * (k + 1)]) for k in range(5)]


def valid_masks(starts_col):
    row = lax.broadcasted_iota(jnp.int32, starts_col.shape, 0)
    one = jnp.where(row < 1, 0.0, pltpu.roll(starts_col, 1, 0))
    two = jnp.where(row < 2, 0.0, pltpu.roll(starts_col, 2, 0))
    first = 1.0 - starts_col
    return first, first - one, first - one - two


def column_of(row_ref):
    return jnp.broadcast_to(row_ref[0:1, :], (128, T)).T


def selector():
    r = lax.broadcasted_iota(jnp.int32, (D, 256), 0)
    k = lax.broadcasted_iota(jnp.int32, (D, 256), 1)
    h = jnp.bitwise_and(jnp.right_shift(k, 1), 7)
    at = 48 * jnp.right_shift(k, 4) + 6 * h + jnp.bitwise_and(k, 1)
    return jnp.where(r == at, 1.0, 0.0).astype(bf16)


def slab_rows(a):
    s = jnp.right_shift(a * 43, 8)
    return 42 * s + a


def pack_kernel(
    proj_ref, outw_ref, step_ref, shared_ref, gain_ref, conv_ref, pack_ref, misc_ref, wide_ref
):
    misc_ref[...] = jnp.zeros_like(misc_ref)
    misc_ref[0:3, 0:48] = step_ref[...]
    misc_ref[0:48, :] = half(misc_ref[...].T)[0:48]
    wide_ref[...] = jnp.zeros_like(wide_ref)
    wide_ref[0:1, 0:6] = gain_ref[...]
    sub = lax.broadcasted_iota(jnp.int32, (6, 128), 0)
    lane = lanes(6)
    column = jnp.sum(jnp.where(sub == lane, wide_ref[0:1, :], 0.0), axis=1, keepdims=True)
    high = column.astype(bf16).astype(f32)
    misc_ref[0:6, :] += jnp.where(lane == MISC + 3, high, 0.0) + jnp.where(
        lane == MISC + 4, column - high, 0.0
    )
    conv = conv_ref[...]
    high = conv.astype(bf16).astype(f32)
    misc_ref[0:2, MISC + 5 : MISC + 10] = high
    misc_ref[0:2, MISC + 10 : MISC + 15] = conv - high
    for j in range(8):
        tile = rolled(shared_ref[:, 128 * (j // 4) : 128 * (j // 4) + 128], SLAB - 32 * (j % 4))
        misc_ref[6 * j : 6 * j + 6, :] += jnp.where(lane >= SLAB, tile, 0.0)
    misc = misc_ref[0:48, :]
    lo = lanes(48) < 64
    wide = []
    for h in range(3):
        wide_ref[:, 0:64] = outw_ref[h]
        wide.append(wide_ref[...])
    tiles = [proj_ref[h] for h in range(3)]
    tiles += [jnp.where(lo, wide[0], half(wide[1])), jnp.where(lo, wide[2], misc)]
    for k, tile in enumerate(tiles):
        low = tile.astype(bf16)
        for q in range(N_SEQ):
            pack_ref[q, :, 128 * k : 128 * (k + 1)] = low


def slab_kernel(w_ref, slab_ref):
    misc = w_ref[:, 512:640]
    a = lax.broadcasted_iota(jnp.int32, (96, D), 0)
    d = lax.broadcasted_iota(jnp.int32, (96, D), 1)
    gap = d - slab_rows(a)
    lane = lanes(96)
    tiles = [jnp.zeros((96, 128), f32)] * 2
    for j in range(8):
        got = dot(jnp.where(gap == 6 * j, 1.0, 0.0).astype(bf16), misc)
        if j == 0:
            slab_ref[:, 256:384] = jnp.where(lane < SLAB, got, 0.0).astype(bf16)
        own = jnp.where(lane >= SLAB, got, 0.0)
        tiles[j // 4] = tiles[j // 4] + rolled(own, 32 * (j % 4) - SLAB)
    slab_ref[:, 0:128] = tiles[0].astype(bf16)
    slab_ref[:, 128:256] = tiles[1].astype(bf16)


def first_kernel(*refs):
    at_ref, slabs, refs = refs[0], refs[1:9], refs[9:]
    hid_ref, halo_ref, st_ref, w_ref, tap_ref, hp_ref = refs[:6]
    normed_ref, v_ref, c_ref, aux_ref, send_ref, row_ref, wide_ref, ctap_ref = refs[6:14]
    all_ref = refs[14]
    d = lax.broadcasted_iota(jnp.int32, (D, 96), 0)
    a = lax.broadcasted_iota(jnp.int32, (D, 96), 1)
    gap = d - slab_rows(a)
    picks = []
    for b in range(8):
        core = at_ref[2] if b < 4 else 1 - at_ref[2]
        head = 2 * lax.rem(at_ref[1] + 4 - b % 4, 4) + core
        all_ref[96 * b : 96 * b + 96, :] = slabs[b][...]
        picks.append(jnp.where(gap == 6 * head, 1.0, 0.0))
    spread_rows = dot(jnp.concatenate(picks, axis=1).astype(bf16), all_ref[...])
    wide_ref[...] = spread_rows[:, 0:256].astype(bf16)
    misc_t = spread_rows[:, 256:384].T
    gain = misc_t[MISC + 3 : MISC + 4] + misc_t[MISC + 4 : MISC + 5]
    conv_t = dot(misc_t.astype(bf16), selector())
    conv_taps = conv_t[MISC + 5 : MISC + 10] + conv_t[MISC + 10 : MISC + 15]
    ctap_ref[0:5, :] = conv_taps
    ctap_ref[5:8, :] = jnp.zeros((3, 256), f32)
    row_ref[0:1, :] = gain
    row_ref[1:8, :] = jnp.zeros((7, D), f32)
    for src, at, rows in ((halo_ref, 0, HALO), (hid_ref, HALO, T)):
        h = src[...].astype(f32)
        inv = lax.rsqrt(jnp.mean(h * h, axis=1, keepdims=True) + norm_eps)
        normed_ref[at : at + rows, :] = (h * inv * gain).astype(bf16)
    normed = normed_ref[...]
    v_ref[:, 0:384] = dot(normed, w_ref[:, 0:384])
    v_ref[:, 384:640] = dot(normed, wide_ref[...])
    raw = half(dot(normed[HALO:], w_ref[:, 512:640]))

    lane = lanes(T)
    pre = raw + head_row(hp_ref, 0)
    delta = jnp.where(
        lane < 3, jnp.maximum(pre, 0.0) + jnp.log1p(jnp.exp(-jnp.abs(pre))), 0.0
    )
    slope = jnp.where(lane < 3, sig(pre), 0.0)
    log_decay = -jnp.exp(head_row(hp_ref, 1)) * delta
    starts = column_of(st_ref)
    parts = three_parts(log_decay) + jnp.where(lane == 9, starts, 0.0)
    ri = lax.broadcasted_iota(jnp.int32, (T, T), 0)
    ci = lax.broadcasted_iota(jnp.int32, (T, T), 1)
    summed = dot(jnp.where(ri >= ci, 1.0, 0.0).astype(bf16), parts.astype(bf16))
    cum = joined(summed)
    segment = summed[:, 9:10]
    last = cum[T - 1 : T, :]
    last_segment = segment[T - 1 : T, :]
    keeper = jnp.where((lane < 3) & (segment == 0.0), jnp.exp(cum), 0.0)
    ending = jnp.where((lane < 3) & (segment == last_segment), jnp.exp(last - cum), 0.0)
    aux_ref[...] = (
        cum
        + rolled(delta, 3)
        + rolled(slope, 6)
        + jnp.where(lane == 9, segment, 0.0)
        + rolled(keeper, 10)
        + rolled(ending, 13)
    )

    valid = valid_masks(starts)
    for k in range(5):
        at = slice(128 * k, 128 * (k + 1))
        if k < 3:
            taps = tap_ref[0:5, at]
        else:
            taps = conv_taps[:, 128 * (k - 3) : 128 * (k - 2)]
        total = taps[4:5] + taps[3:4] * v_ref[HALO:, at]
        for lag in (1, 2, 3):
            total = total + taps[3 - lag : 4 - lag] * (
                v_ref[pl.ds(HALO - lag, T), at] * valid[lag - 1]
            )
        c_ref[:, at] = total

    act = act_tiles(c_ref)
    x = x_pair(*act[:3])
    weight = spread(ending * delta, 0)
    ended = jnp.concatenate([x[0] * weight[0], x[1] * weight[1]], axis=1).astype(bf16)
    state = dot(ended, act[3].astype(bf16), 0, 0)
    through = jnp.where(last_segment == 0.0, jnp.exp(last), 0.0)
    high = through.astype(bf16).astype(f32)
    lower = through - high
    sub = lax.broadcasted_iota(jnp.int32, (16, 128), 0)
    tail = jnp.zeros((16, 128), f32)
    for h in range(3):
        tail = jnp.where(sub == h, high[:, h : h + 1], tail)
        tail = jnp.where(sub == 3 + h, lower[:, h : h + 1], tail)
    send_ref[0:192, :] = state[0:192].astype(bf16)
    send_ref[192:SROWS, :] = tail.astype(bf16)


def own_kernel(c_ref, aux_ref, cot_ref, w_ref, hp_ref, y_ref, dn_ref, m_ref, mg_ref):
    act = act_tiles(c_ref)
    x = x_pair(*act[:3])
    aux = aux_ref[...]
    aux_t = aux.T
    scores = dot(act[4].astype(bf16), act[3].astype(bf16), 1, 1)
    ri = lax.broadcasted_iota(jnp.int32, (T, T), 0)
    ci = lax.broadcasted_iota(jnp.int32, (T, T), 1)
    allowed = (ri >= ci) & (aux[:, 9:10] == aux_t[9:10, :])
    mask = jnp.where(allowed, 0.0, LOW)
    delta = spread(aux, 3)
    fed = x[0] * delta[0], x[1] * delta[1]
    lo = lanes(T) < 64
    fed_h = (
        jnp.where(lo, fed[0], 0.0).astype(bf16),
        jnp.where(lo, 0.0, fed[0]).astype(bf16),
        fed[1].astype(bf16),
    )
    skip = skip_pair(hp_ref)
    y = [x[0] * skip[0], x[1] * skip[1]]
    for h in range(3):
        decay = jnp.exp(aux[:, h : h + 1] - aux_t[h : h + 1, :] + mask)
        m_ref[h] = decay.astype(bf16)
        mixing = (decay * scores).astype(bf16)
        mg_ref[h] = mixing
        y[h // 2] = y[h // 2] + dot(mixing, fed_h[h])
    y_ref[:, 0:128] = y[0]
    y_ref[:, 128:256] = y[1]
    back = dot(cot_ref[...], w_ref[:, 384:640])
    dn_ref[:, 0:128] = back[:, 0:128]
    dn_ref[:, 128:256] = jnp.where(lo, back[:, 128:256], 0.0)


def decay_rows(tail):
    both = tail[0:3] + tail[3:6]
    return jnp.concatenate(
        [jnp.broadcast_to(both[h : h + 1], (64, 128)) for h in range(3)], axis=0
    )


def in_place(here, refs, rows):
    pieces = [r[rows, :].astype(f32) for r in refs]
    placed = []
    for p in range(4):
        by = lax.rem(here + 4 - p, 4)
        piece = pieces[0]
        for k in (1, 2, 3):
            piece = jnp.where(by == k, pieces[k], piece)
        placed.append(piece)
    return placed


def fold(here, states, tails, reverse):
    total = entering = jnp.zeros((192, 128), f32)
    passed = whole = jnp.ones((192, 128), f32)
    for p in reversed(range(4)) if reverse else range(4):
        decay = decay_rows(tails[p])
        before = (p > here) if reverse else (p < here)
        total = decay * total + states[p]
        entering = jnp.where(before, total, entering)
        passed = jnp.where(before, passed * decay, passed)
        whole = whole * decay
    return total, entering, passed, whole


def group_kernel(at_ref, a_ref, b_ref, c_ref, d_ref, send_ref, own_ref, passed_ref, tail_ref):
    here = lax.rem(at_ref[0], 4)
    refs = (a_ref, b_ref, c_ref, d_ref)
    states = in_place(here, refs, slice(0, 192))
    tails = in_place(here, refs, slice(192, SROWS))
    total, entering, passed, whole = fold(here, states, tails, False)
    own_ref[...] = entering
    passed_ref[...] = passed
    send_ref[0:192, :] = total.astype(bf16)
    sub = lax.broadcasted_iota(jnp.int32, (16, 128), 0)
    tail = jnp.zeros((16, 128), f32)
    for h in range(3):
        row = whole[64 * h : 64 * h + 1]
        high = row.astype(bf16).astype(f32)
        tail = jnp.where(sub == h, high, tail)
        tail = jnp.where(sub == 3 + h, row - high, tail)
    send_ref[192:SROWS, :] = tail.astype(bf16)
    for p in range(4):
        tail_ref[16 * p : 16 * p + 16, :] = tails[p]


def group_back_kernel(
    at_ref, a_ref, b_ref, c_ref, d_ref, tail_ref, after_ref, send_ref, own_ref, passed_ref
):
    del after_ref
    here = lax.rem(at_ref[0], 4)
    states = in_place(here, (a_ref, b_ref, c_ref, d_ref), slice(0, 192))
    tails = [tail_ref[16 * p : 16 * p + 16, :] for p in range(4)]
    total, entering, passed, _ = fold(here, states, tails, True)
    own_ref[...] = entering
    passed_ref[...] = passed
    send_ref[...] = total.astype(bf16)


def enter_kernel(
    at_ref, s0_ref, s1_ref, s2_ref, s3_ref, own_ref, passed_ref, y0_ref, dn_ref, c_ref,
    aux_ref, tap_ref, y_ref, state_ref, stat_ref, tail_ref,
):
    here = jnp.right_shift(at_ref[0], 2)
    refs = (s0_ref, s1_ref, s2_ref, s3_ref)
    states = in_place(here, refs, slice(0, 192))
    tails = in_place(here, refs, slice(192, SROWS))
    for p in range(4):
        tail_ref[16 * p : 16 * p + 16, :] = tails[p]
    _, entering, _, _ = fold(here, states, tails, False)
    state = passed_ref[...] * entering + own_ref[...]
    state_ref[0:192] = state
    state_ref[192:256] = jnp.zeros((64, 128), f32)
    c_mat = silu(c_ref[:, 512:640]).astype(bf16)
    carried = dot(c_mat, state_ref[...].astype(bf16), 1, 1)
    aux = aux_ref[...]
    keeper = spread(aux, 10)
    gate = gate_pair(*[silu(c_ref[:, 128 * k : 128 * (k + 1)]) for k in range(3)])
    squares = jnp.zeros((T, 1), f32)
    inner = jnp.zeros((T, 1), f32)
    for k in range(2):
        at = slice(128 * k, 128 * (k + 1))
        y = y0_ref[:, at] + keeper[k] * carried[:, at]
        y_ref[:, at] = y
        gated = y * gate[k]
        fed = gated * tap_ref[0:1, 384 + 128 * k : 512 + 128 * k]
        squares = squares + jnp.sum(gated * gated, axis=1, keepdims=True)
        inner = inner + jnp.sum(fed * dn_ref[:, at], axis=1, keepdims=True)
    lane = lanes(T)
    both = jnp.where(lane == 0, squares, jnp.where(lane == 1, inner, 0.0)).T
    stat_ref[...] = both[0:8]


def gated_kernel(
    s0_ref, s1_ref, s2_ref, s3_ref, y_ref, dn_ref, c_ref, aux_ref, tap_ref,
    dy_ref, dgate_ref, nout_ref, send_ref, rows_ref,
):
    total = s0_ref[...] + s1_ref[...] + s2_ref[...] + s3_ref[...]
    total = jnp.concatenate([total, jnp.zeros((120, T), f32)], axis=0).T
    rms = lax.rsqrt(total[:, 0:1] / DI + norm_eps)
    coef = rms * rms * rms * total[:, 1:2] / DI
    aux = aux_ref[...]
    keeper = spread(aux, 10)
    raw = gate_pair(*[c_ref[:, 128 * k : 128 * (k + 1)] for k in range(3)])
    x = x_pair(*[silu(c_ref[:, 128 * k : 128 * (k + 1)]) for k in range(3)])
    kept = []
    rows_ref[...] = jnp.zeros_like(rows_ref)
    for k in range(2):
        at = slice(128 * k, 128 * (k + 1))
        gain = tap_ref[0:1, 384 + 128 * k : 512 + 128 * k]
        s = sig(raw[k])
        gate = raw[k] * s
        y = y_ref[:, at]
        gated = y * gate
        dn = dn_ref[:, at]
        scaled = gated * rms
        nout_ref[:, at] = (scaled * gain).astype(bf16)
        d_gated = rms * gain * dn - gated * coef
        dy = d_gated * gate
        dy_ref[:, at] = dy
        dgate_ref[:, at] = d_gated * y * s * (1.0 + raw[k] * (1.0 - s))
        kept.append((dy * keeper[k]).astype(bf16))
        rows_ref[0:1, at] = jnp.sum(dn * scaled, axis=0, keepdims=True)
        rows_ref[1:2, at] = jnp.sum(dy * x[k], axis=0, keepdims=True)
    c_mat = silu(c_ref[:, 512:640]).astype(bf16)
    send_ref[...] = dot(jnp.concatenate(kept, axis=1), c_mat, 0, 0)[0:192].astype(bf16)


def halves(ref, core):
    keep = ref[pl.ds(pl.multiple_of(core * 256, 256), 256), :]
    give = ref[pl.ds(pl.multiple_of(256 - core * 256, 256), 256), :]
    return keep.astype(bf16), give.astype(bf16)


def out_kernel(at_ref, nout_ref, w_ref, keep_ref, give_ref, norm_ref):
    norm_ref[...] = dot(nout_ref[...], w_ref[:, 384:640], 1, 1)
    keep_ref[...], give_ref[...] = halves(norm_ref, at_ref[2])


def clear_edges(pad_ref):
    pad_ref[0:HALO] = jnp.zeros((HALO, 128), f32)
    pad_ref[HALO + T :] = jnp.zeros((HALO, 128), f32)


def conv_back(d_conv, taps, v_ref, at, valid, pad_ref):
    sums = [None, None, None, None, jnp.sum(d_conv, axis=0, keepdims=True)]
    sums[3] = jnp.sum(d_conv * v_ref[HALO:, at], axis=0, keepdims=True)
    pad_ref[HALO : HALO + T] = taps[3:4] * d_conv
    acc = pad_ref[0 : HALO + T]
    for lag in (1, 2, 3):
        masked = d_conv * valid[lag - 1]
        sums[3 - lag] = jnp.sum(
            masked * v_ref[pl.ds(HALO - lag, T), at], axis=0, keepdims=True
        )
        pad_ref[HALO : HALO + T] = taps[3 - lag : 4 - lag] * masked
        acc = acc + pad_ref[pl.ds(lag, HALO + T)]
    return acc, sums


def own_back_kernel(
    dy_ref, y_ref, y0_ref, c_ref, aux_ref, m_ref, mg_ref, state_ref,
    v_ref, ctap_ref, st_ref,
    dx_ref, db_ref, dcum_ref, xs_ref, b_ref, slope_ref, dvc_ref, crow_ref,
    pad_ref,
):
    aux = aux_ref[...]
    aux_t = aux.T
    act = []
    for k in range(5):
        at = slice(128 * k, 128 * (k + 1))
        v = c_ref[:, at]
        s = sig(v)
        act.append(v * s)
        slope = s * (1.0 + v * (1.0 - s))
        if k < 4:
            slope_ref[:, at] = slope
    x = x_pair(*act[:3])
    xs_ref[:, 0:128] = x[0]
    xs_ref[:, 128:256] = x[1]
    b_ref[...] = act[3].astype(bf16)
    b_low, c_low = act[3].astype(bf16), act[4].astype(bf16)
    dy = pair_of(dy_ref)
    lo = lanes(T) < 64
    dy_h = (
        jnp.where(lo, dy[0], 0.0).astype(bf16),
        jnp.where(lo, 0.0, dy[0]).astype(bf16),
        dy[1].astype(bf16),
    )
    x_low = x[0].astype(bf16), x[1].astype(bf16)
    lane = lanes(T)
    dx = [jnp.zeros((T, 128), f32), jnp.zeros((T, 128), f32)]
    spread_sum = jnp.zeros((T, T), f32)
    rows = jnp.zeros((T, 128), f32)
    cols = jnp.zeros((128, T), f32)
    sub = lax.broadcasted_iota(jnp.int32, (128, T), 0)
    for h in range(3):
        pairs = dot(dy_h[h], x_low[h // 2], 1, 1) * aux_t[3 + h : 4 + h, :]
        mixing = mg_ref[h]
        spread_sum = spread_sum + pairs * m_ref[h].astype(f32)
        weights = pairs * mixing.astype(f32)
        rows = jnp.where(lane == h, jnp.sum(weights, axis=1, keepdims=True), rows)
        cols = jnp.where(sub == h, jnp.sum(weights, axis=0, keepdims=True), cols)
        dx[h // 2] = dx[h // 2] + dot(mixing, dy_h[h], 0, 0)
    low = spread_sum.astype(bf16)
    keeper = spread(aux, 10)
    kept = jnp.concatenate([dy[0] * keeper[0], dy[1] * keeper[1]], axis=1).astype(bf16)
    d_c = dot(low, b_low) + dot(kept, state_ref[...].astype(bf16))
    valid = valid_masks(column_of(st_ref))
    clear_edges(pad_ref)
    dv, sums = conv_back(d_c * slope, ctap_ref[0:5, 128:256], v_ref, slice(512, 640), valid, pad_ref)
    dvc_ref[...] = dv.astype(bf16)
    crow_ref[...] = jnp.concatenate([*sums, jnp.zeros((3, 128), f32)], axis=0)
    db_ref[...] = dot(low, c_low, 0, 0)
    dx_ref[:, 0:128] = dx[0]
    dx_ref[:, 128:256] = dx[1]
    carried = [
        dy[k] * (y_ref[:, 128 * k : 128 * (k + 1)] - y0_ref[:, 128 * k : 128 * (k + 1)])
        for k in range(2)
    ]
    dcum_ref[...] = rows - cols.T + head_sums(carried)


def back_kernel(
    at_ref, a0_ref, a1_ref, a2_ref, a3_ref, own_ref, passed_ref, tails_ref, mine_ref,
    state_ref, dx_ref, db_ref, dcum_ref, xs_ref, b_ref, slope_ref,
    dvc_ref, crow_ref, aux_ref, v_ref, tap_ref, ctap_ref, hp_ref, st_ref, dy_ref, dgate_ref,
    w_ref, wide_ref, rows_ref, hid_ref, halo_ref,
    dv_ref, dstep_ref, keep_ref, give_ref, edge_ref, chan_ref, conv_ref, gain_ref,
    pad_ref, norm_ref,
):
    here = jnp.right_shift(at_ref[0], 2)
    states = in_place(here, (a0_ref, a1_ref, a2_ref, a3_ref), slice(0, 192))
    tails = [tails_ref[16 * p : 16 * p + 16, :] for p in range(4)]
    _, entering, _, _ = fold(here, states, tails, True)
    adj = passed_ref[...] * entering + own_ref[...]
    aux = aux_ref[...]
    lane = lanes(T)
    x = pair_of(xs_ref)
    b_low = b_ref[...]
    delta, ending = spread(aux, 3), spread(aux, 13)
    adj_low = jnp.concatenate([adj, jnp.zeros((64, 128), f32)], axis=0).astype(bf16)
    through_b = dot(b_low, adj_low, 1, 1)
    skip = skip_pair(hp_ref)
    dy = pair_of(dy_ref)
    ended, extra, full, d_x = [], [], [], []
    for k in range(2):
        at = slice(128 * k, 128 * (k + 1))
        late = ending[k] * through_b[:, at]
        total = dx_ref[:, at] + late
        d_x.append(delta[k] * total + skip[k] * dy[k])
        full.append(x[k] * total)
        extra.append(x[k] * late)
        ended.append(x[k] * delta[k] * ending[k])
    d_b = db_ref[...] + dot(jnp.concatenate(ended, axis=1).astype(bf16), adj_low)
    d_delta = head_sums(full)
    tail = head_sums(extra) * rolled(aux, -3)
    tail = jnp.where(lane < 3, tail, 0.0)
    d_cum = dcum_ref[...] - tail
    ri = lax.broadcasted_iota(jnp.int32, (T, T), 0)
    ci = lax.broadcasted_iota(jnp.int32, (T, T), 1)
    upper = jnp.where(ci >= ri, 1.0, 0.0).astype(bf16)
    d_log = joined(dot(upper, three_parts(d_cum).astype(bf16)))
    own = decay_rows(mine_ref[192:SROWS, :].astype(f32))
    met = own * adj * state_ref[0:192]
    lane1 = lanes(1)
    meets = jnp.zeros((1, 128), f32)
    for h in range(3):
        meets = jnp.where(lane1 == h, jnp.sum(met[64 * h : 64 * h + 64]), meets)
    d_log = d_log + jnp.sum(tail, axis=0, keepdims=True) + meets
    d_log = jnp.where(lane < 3, d_log, 0.0)
    rate = jnp.exp(head_row(hp_ref, 1))
    d_raw = (d_delta - rate * d_log) * rolled(aux, -6)
    d_raw = jnp.where(lane < 3, d_raw, 0.0)
    delta_cols = jnp.where(lane < 3, rolled(aux, -3), 0.0)
    step_low = half(d_raw).astype(bf16)
    dstep_ref[...] = step_low

    d_gate = pair_of(dgate_ref)
    x_tiles = head_tiles((jnp.zeros_like(d_x[0]),) * 2, d_x)
    gate_tiles = head_tiles(d_gate, (jnp.zeros_like(d_x[0]),) * 2)
    lo = lane < 64
    valid = valid_masks(column_of(st_ref))
    clear_edges(pad_ref)
    tap_rows = []
    for k in range(4):
        at = slice(128 * k, 128 * (k + 1))
        slope = slope_ref[:, at]
        if k < 3:
            d_conv = jnp.where(lo, gate_tiles[k], x_tiles[k] * slope)
            taps = tap_ref[0:5, at]
        else:
            d_conv = d_b * slope
            taps = ctap_ref[0:5, 0:128]
        dv, sums = conv_back(d_conv, taps, v_ref, at, valid, pad_ref)
        dv_ref[:, at] = dv.astype(bf16)
        tap_rows.append(sums)
    dv_ref[:, 512:640] = dvc_ref[...]
    tap_rows.append([crow_ref[j : j + 1, :] for j in range(5)])

    chan_ref_rows = []
    for j in range(5):
        pair = x_pair(*[tap_rows[k][j] for k in range(3)])
        chan_ref_rows.append(jnp.concatenate(pair, axis=1))
    chan_ref_rows.append(rows_ref[0:1, :])
    h0 = jnp.sum(d_raw, axis=0, keepdims=True)
    h1 = jnp.sum(d_log * (-rate) * delta_cols, axis=0, keepdims=True)
    h2 = head_sums((rows_ref[1:2, 0:128], rows_ref[1:2, 128:256]))
    zero = jnp.zeros((1, 128), f32)
    for r in (h0, h1, h2):
        chan_ref_rows.append(jnp.concatenate([r, zero], axis=1))
    for j, r in enumerate(chan_ref_rows):
        chan_ref[j : j + 1, :] = r
    chan_ref[9:16, :] = jnp.zeros((7, 256), f32)
    for j in range(5):
        conv_ref[j : j + 1, :] = jnp.concatenate([tap_rows[3][j], tap_rows[4][j]], axis=1)
    conv_ref[5:8, :] = jnp.zeros((3, 256), f32)

    d_norm = dot(dv_ref[:, 0:384], w_ref[:, 0:384], 1, 1)
    d_norm = d_norm + dot(dv_ref[:, 384:640], wide_ref[...], 1, 1)
    main = d_norm[HALO:] + dot(step_low, w_ref[:, 512:640], 1, 1)
    norm_ref[...] = main
    keep_ref[...], give_ref[...] = halves(norm_ref, at_ref[2])
    edge_ref[...] = d_norm[0:HALO].astype(bf16)
    total = jnp.zeros((1, D), f32)
    for src, val in ((halo_ref, d_norm[0:HALO]), (hid_ref, main)):
        h = src[...].astype(f32)
        inv = lax.rsqrt(jnp.mean(h * h, axis=1, keepdims=True) + norm_eps)
        total = total + jnp.sum(val * (h * inv), axis=0, keepdims=True)
    gain_ref[0:1] = total
    gain_ref[1:8] = jnp.zeros((7, D), f32)


def picked(rows, head):
    a = lax.broadcasted_iota(jnp.int32, (rows, D), 0)
    d = lax.broadcasted_iota(jnp.int32, (rows, D), 1)
    return jnp.where(d - slab_rows(a) == 6 * head, 1.0, 0.0).astype(bf16)


def grad_kernel(
    at_ref, normed_ref, dv_ref, dstep_ref, nout_ref, cot_ref, conv_ref, gain_ref, chan_ref,
    edge_ref, out_ref, keep_ref, give_ref, slab_ref,
):
    give_ref[384:400, :] = edge_ref[:, 0:384]
    give_ref[400:416, :] = edge_ref[:, 384:768]
    normed = normed_ref[...]
    slab_ref[:, 0:256] = dot(normed, dv_ref[:, 384:640], 0, 0).astype(bf16)
    grads = jnp.concatenate([jnp.zeros((MISC + 5, 256), f32), conv_ref[0:5, :]], axis=0)
    grads = jnp.concatenate([grads, jnp.zeros((128 - MISC - 10, 256), f32)], axis=0)
    sub = lax.broadcasted_iota(jnp.int32, (128, D), 0)
    column = jnp.where(sub == MISC + 3, gain_ref[0:1], 0.0).T
    slab_ref[:, 256:384] = (dot(selector(), grads.astype(bf16), 1, 1) + column).astype(bf16)
    slab = slab_ref[...]
    for x in range(4):
        rows = slice(96 * x, 96 * x + 96)
        keep_ref[rows, :] = dot(picked(96, 2 * x + at_ref[2]), slab).astype(bf16)
        give_ref[rows, :] = dot(picked(96, 2 * x + 1 - at_ref[2]), slab).astype(bf16)
    out_ref[:, 0:384] = dot(normed, dv_ref[:, 0:384], 0, 0).astype(bf16)
    outs = dot(cot_ref[...], nout_ref[...], 0, 0)
    out_ref[:, 384:512] = outs[:, 0:128].astype(bf16)
    tile = outs[:, 128:256] + dot(normed_ref[HALO:, :], dstep_ref[...], 0, 0)
    turned = jnp.concatenate([chan_ref[...], jnp.zeros((112, 256), f32)], axis=0).T
    shared = jnp.zeros((48, 128), f32)
    for g in range(4):
        piece = turned[48 * g : 48 * g + 48]
        piece = jnp.where(lanes(48) < (9 if g == 0 else 6), piece, 0.0)
        shared = shared + rolled(piece, CHAN[g])
    out_ref[:, 512:640] = (tile + jnp.concatenate([shared] * N_SEQ, axis=0)).astype(bf16)


def merge_kernel(a_ref, b_ref, c_ref, d_ref, pack_ref, out_ref):
    total = a_ref[128:176].astype(f32) + b_ref[128:176].astype(f32)
    total = total + c_ref[128:176].astype(f32) + d_ref[128:176].astype(f32)
    total = jnp.concatenate([total[:, 0:384], total[:, 384:768]], axis=0)
    misc = total[:, 256:384]
    lane = lanes(96)
    d = lax.broadcasted_iota(jnp.int32, (D, 96), 0)
    a = lax.broadcasted_iota(jnp.int32, (D, 96), 1)
    gap = d - slab_rows(a)
    places, laid = [], []
    for j in range(8):
        tile = rolled(total[:, 128 * (j // 4) : 128 * (j // 4) + 128], SLAB - 32 * (j % 4))
        one = misc if j == 0 else rolled(misc, -1 - j)
        laid.append(
            jnp.where(lane >= SLAB, tile, jnp.where((lane == MISC + 3) & (j < 6), one, 0.0))
        )
        places.append(jnp.where(gap == 6 * j, 1.0, 0.0))
    added = dot(
        jnp.concatenate(places, axis=1).astype(bf16),
        jnp.concatenate(laid, axis=0).astype(bf16),
    )
    out_ref[:, 0:512] = pack_ref[:, 0:512]
    out_ref[:, 512:640] = (pack_ref[:, 512:640].astype(f32) + added).astype(bf16)


def pair_kernel(
    at_ref, keep_ref, got_ref, edge_ref, slab_keep_ref, slab_ref, out_keep_ref, out_got_ref,
    own_ref, s1, s2, s3, sum_ref, both_ref,
):
    both_ref[...] = slab_keep_ref[...].astype(f32) + slab_ref[0:384].astype(f32)
    sum_ref[0:256] = keep_ref[...].astype(f32) + got_ref[...].astype(f32)
    sibling = jnp.concatenate([slab_ref[384:400, :], slab_ref[400:416, :]], axis=1)
    edge = edge_ref[...].astype(f32) + sibling.astype(f32)
    sum_ref[256 - HALO : 256] += jnp.where(at_ref[2] == 1, edge, 0.0)
    sum_ref[256:512] = out_keep_ref[...].astype(f32) + out_got_ref[...].astype(f32)
    for by, ref in enumerate((own_ref, s1, s2, s3)):
        x = lax.rem(at_ref[1] + by, 4)
        start = pl.multiple_of(x * 64, 64)
        for k in range(2):
            rows = pl.ds(pl.multiple_of(x * 96 + 48 * k, 48), 48)
            ref[128:176, 384 * k : 384 * k + 384] = both_ref[rows, :].astype(bf16)
            ref[64 * k : 64 * k + 64] = sum_ref[pl.ds(256 * k + start, 64), :].astype(bf16)


def four_kernel(at_ref, a_ref, b_ref, c_ref, d_ref, hid_ref, out_ref):
    total = a_ref[0:128].astype(f32) + b_ref[0:128].astype(f32)
    total = total + c_ref[0:128].astype(f32) + d_ref[0:128].astype(f32)
    start = pl.multiple_of((4 * at_ref[2] + at_ref[1]) * 64, 64)
    out_ref[:, 0:D] = total[0:64].astype(bf16)
    out_ref[:, D:] = (total[64:128] + hid_ref[pl.ds(start, 64), :].astype(f32)).astype(bf16)


def input_kernel(*refs):
    at_ref, refs = refs[0], refs[1:]
    hid_ref, cot_ref, row_ref, out_ref, block_ref = refs[8:]
    for side in range(2):
        core = at_ref[2] if side == 0 else 1 - at_ref[2]
        for by in range(4):
            block = core * 4 + lax.rem(at_ref[1] + 4 - by, 4)
            rows = pl.ds(pl.multiple_of(block * 64, 64), 64)
            piece = refs[4 * side + by]
            h = hid_ref[rows, :].astype(f32)
            inv = lax.rsqrt(jnp.mean(h * h, axis=1, keepdims=True) + norm_eps)
            d_scaled = piece[:, 0:D].astype(f32) * row_ref[0:1, :]
            inner = jnp.sum(d_scaled * h, axis=1, keepdims=True)
            out_ref[rows, :] = (
                cot_ref[rows, :].astype(f32)
                + inv * d_scaled
                - h * (inv * inv * inv * inner / D)
            )
            block_ref[rows, :] = piece[:, D:]


def adam(weight, grad, first, second, rate):
    first_new = beta_one * first + (1.0 - beta_one) * grad
    second_new = beta_two * second + (1.0 - beta_two) * grad * grad
    first_hat = first_new / (1.0 - beta_one**STEP)
    second_hat = second_new / (1.0 - beta_two**STEP)
    weight_new = weight - rate * (
        first_hat / (jnp.sqrt(second_hat) + adam_eps) + decay_rate * weight
    )
    return first_new, second_new, weight_new


RATE_D = 1.4 * D ** (-0.5)
RATE_I = 1.4 * DI ** (-0.5)


def put(refs, at, values):
    for ref, value in zip(refs, values):
        ref[at] = value


def update_kernel(*refs):
    grad_ref, refs = refs[0], refs[1:]
    proj, step, out, chan, head, shared, gain, conv = (
        refs[3 * k : 3 * k + 3] for k in range(8)
    )
    outs = refs[24:]
    proj_o, step_o, out_o, chan_o, head_o, shared_o, gain_o, conv_o = (
        outs[3 * k : 3 * k + 3] for k in range(8)
    )
    wide_ref, conv_ref = outs[24:]
    total = grad_ref[0].astype(f32)
    for q in range(1, N_SEQ):
        total = total + grad_ref[q].astype(f32)
    misc = total[:, 512:640]
    for h in range(3):
        w, m, v = (r[h] for r in proj)
        put(proj_o, h, adam(w, total[:, 128 * h : 128 * (h + 1)], m, v, RATE_D))
        tile = total[:, 384 + 128 * (h // 2) : 512 + 128 * (h // 2)]
        tile = half(tile) if h == 1 else tile
        w, m, v = (r[h] for r in out)
        put(out_o, h, adam(w, tile[:, 0:64], m, v, RATE_I))
    turned = jnp.concatenate([misc, jnp.zeros((80, 128), f32)], axis=0).T
    at = (slice(None), slice(None))
    w, m, v = (r[at] for r in step)
    put(step_o, at, adam(w, turned[MISC : MISC + 3, 0:48], m, v, RATE_D))
    p = [turned[CHAN[g] : CHAN[g] + 9] for g in range(4)]
    lane = lanes(9)
    wrapped = rolled(p[2], 96)
    pair = (
        p[0] + rolled(p[1], 48) + jnp.where(lane >= 96, wrapped, 0.0),
        jnp.where(lane < 16, wrapped, 0.0) + rolled(p[3], 16),
    )
    for h in range(3):
        piece = half(pair[0]) if h == 1 else pair[h // 2]
        spot = (slice(None), h, slice(None))
        w, m, v = (r[spot] for r in chan)
        put(chan_o, spot, adam(w, piece[0:6, 0:64], m, v, 0.5))
    w, m, v = (r[at] for r in head)
    put(head_o, at, adam(w, p[0][6:9, 0:3], m, v, 1.0))
    lane = lanes(6)
    for t in range(2):
        tile = jnp.zeros((6, 128), f32)
        for i in range(4):
            j = 4 * t + i
            own = jnp.where(lane >= SLAB, misc[6 * j : 6 * j + 6], 0.0)
            tile = tile + rolled(own, 32 * i - SLAB)
        wide_ref[:, 128 * t : 128 * t + 128] = tile
    w, m, v = (r[at] for r in shared)
    put(shared_o, at, adam(w, wide_ref[...], m, v, RATE_D))
    column = turned[MISC + 3 : MISC + 4]
    w, m, v = (r[at] for r in gain)
    put(gain_o, at, adam(w, column[:, 0:6], m, v, 0.5))
    lane = lanes(2)
    taps = jnp.zeros((2, 128), f32)
    for t in range(5):
        taps = jnp.where(
            lane == t, misc[6 + 6 * t : 8 + 6 * t, MISC + 3 : MISC + 4], taps
        )
    conv_ref[...] = taps
    w, m, v = (r[at] for r in conv)
    put(conv_o, at, adam(w, conv_ref[:, 0:5], m, v, 0.5))


def exchange(blocks, axis):
    return lax.all_to_all(blocks, axis, 0, 0, tiled=True)


def around(a, axis, by):
    peers = lax.axis_size(axis)
    return lax.ppermute(a, axis, [(i, (i + by) % peers) for i in range(peers)])


def to_next(a):
    return lax.ppermute(a, SEQ, [(i, i + 1) for i in range(N_SEQ - 1)])


def to_previous(a):
    return lax.ppermute(a, SEQ, [(i + 1, i) for i in range(N_SEQ - 1)])


def body(
    hidden_in, cotangent, doc_starts, proj_weight, step_weight, out_weight, shared_weight,
    pre_gain, channel_params, head_params, shared_conv, proj_first, proj_second, step_first,
    step_second, out_first, out_second, shared_first, shared_second, gain_first, gain_second,
    channel_first, channel_second, head_first, head_second, conv_first, conv_second,
):
    where = jnp.stack(
        [lax.axis_index(SEQ), lax.axis_index("head_0"), lax.axis_index("head_1")]
    ).astype(jnp.int32)
    halo = to_next(hidden_in[T - HALO :])
    matrices = [jnp.transpose(a, (1, 0, 2)) for a in (proj_weight, proj_first, proj_second)]
    steps = [a.T for a in (step_weight, step_first, step_second)]
    out_weights = [jnp.transpose(a, (0, 2, 1)) for a in (out_weight, out_first, out_second)]
    gains_in = [a.reshape(1, 6) for a in (pre_gain, gain_first, gain_second)]

    (pack,) = call(
        pack_kernel, [((N_SEQ, 48, NW), bf16)],
        matrices[0], out_weights[0], steps[0], shared_weight, gains_in[0], shared_conv,
        scratch=[pltpu.VMEM((128, 128), f32), pltpu.VMEM((48, 128), f32)], name="pack",
    )
    weights = exchange(pack, SEQ).reshape(D, NW)
    (slab,) = call(slab_kernel, [((96, 384), bf16)], weights, name="slab")
    near = [slab] + [around(slab, "head_0", by) for by in (1, 2, 3)]
    slabs = near + [around(a, "head_1", 1) for a in near]

    marks = doc_starts.astype(f32).reshape(1, T)
    fixed = jnp.broadcast_to(
        (jnp.arange(6) == 3).astype(f32)[:, None, None], channel_params.shape
    )
    taps = jnp.concatenate([fixed, channel_params], axis=2).reshape(6, 384)
    gains = jnp.pad(channel_params[5].reshape(1, 192), ((0, 5), (0, 64)))
    taps = jnp.pad(jnp.concatenate([taps, gains], axis=1), ((0, 2), (0, 0)))

    normed, values, conv, aux, sent, row, wide, conv_taps = call(
        first_kernel,
        [
            ((HALO + T, D), bf16), ((HALO + T, NV), f32), ((T, NV), f32), ((T, 128), f32),
            ((SROWS, 128), bf16), ((8, D), f32), ((D, 256), bf16), ((8, 256), f32),
        ],
        where, *slabs, hidden_in, halo, marks, weights, taps, head_params, smem=(0, 14),
        scratch=[pltpu.VMEM((D, 384), bf16)], name="first",
    )
    states = [sent] + [around(sent, "seq_1", by) for by in (1, 2, 3)]
    group, group_in, group_passed, group_tails = call(
        group_kernel,
        [((SROWS, 128), bf16), ((192, 128), f32), ((192, 128), f32), ((64, 128), f32)],
        where, *states, smem=(0,), name="group",
    )
    groups = [group] + [around(group, "seq_0", by) for by in (1, 2, 3)]
    y_own, d_normed, decays, mixing = call(
        own_kernel,
        [((T, 256), f32), ((T, 256), f32), ((3, T, T), bf16), ((3, T, T), bf16)],
        conv, aux, cotangent, weights, head_params, smem=(4,), name="own",
    )
    y_full, state, stat, all_tails = call(
        enter_kernel,
        [((T, 256), f32), ((256, 128), f32), ((8, T), f32), ((64, 128), f32)],
        where, *groups, group_in, group_passed, y_own, d_normed, conv, aux, taps, smem=(0,), name="enter",
    )
    stat = stat + around(stat, "head_1", 1)
    stats = [stat] + [around(stat, "head_0", by) for by in (1, 2, 3)]
    d_y, d_gate, normed_out, sent_adj, rows = call(
        gated_kernel,
        [
            ((T, 256), f32), ((T, 256), f32), ((T, 256), bf16),
            ((192, 128), bf16), ((8, 256), f32),
        ],
        *stats, y_full, d_normed, conv, aux, taps, name="gated",
    )
    adjoints = [sent_adj] + [around(sent_adj, "seq_1", by) for by in (1, 2, 3)]
    half_rows = ((T // 2, D), bf16)
    out_keep, out_give = call(
        out_kernel, [half_rows] * 2, where, normed_out, weights, smem=(0,),
        scratch=[pltpu.VMEM((T, D), f32)], name="out",
    )
    out_taken = around(out_give, "head_1", 1)
    group, adj_in, adj_passed = call(
        group_back_kernel,
        [((192, 128), bf16), ((192, 128), f32), ((192, 128), f32)],
        where, *adjoints, group_tails, out_keep, smem=(0,), anywhere=(6,), name="group_back",
    )
    groups = [group] + [around(group, "seq_0", by) for by in (1, 2, 3)]
    piece = ((T // N_HEAD, D), bf16)
    d_x, d_b, d_cum, x_act, b_act, slopes, d_value_c, c_rows = call(
        own_back_kernel,
        [
            ((T, 256), f32), ((T, 128), f32), ((T, 128), f32), ((T, 256), f32),
            ((T, 128), bf16), ((T, 512), f32), ((HALO + T, 128), bf16), ((8, 128), f32),
        ],
        d_y, y_full, y_own, conv, aux, decays, mixing, state, values, conv_taps, marks,
        scratch=[pltpu.VMEM((T + 2 * HALO, 128), f32)], name="own_back",
    )
    d_values, d_step, keep, give, edge, chan, d_conv, d_gain = call(
        back_kernel,
        [
            ((HALO + T, NV), bf16), ((T, 128), bf16), half_rows, half_rows,
            ((HALO, D), bf16), ((16, 256), f32), ((8, 256), f32), ((8, D), f32),
        ],
        where, *groups, adj_in, adj_passed, all_tails, sent, state, d_x, d_b, d_cum, x_act, b_act, slopes, d_value_c,
        c_rows, aux, values, taps, conv_taps, head_params, marks, d_y, d_gate, weights, wide,
        rows, hidden_in, halo,
        smem=(0, 22),
        scratch=[pltpu.VMEM((T + 2 * HALO, 128), f32), pltpu.VMEM((T, D), f32)],
        name="back",
    )
    taken = around(give, "head_1", 1)
    edge = to_previous(edge)
    grads, slab_keep, slab_give = call(
        grad_kernel, [((D, NW), bf16), ((384, 384), bf16), ((416, 384), bf16)],
        where, normed, d_values, d_step, normed_out, cotangent, d_conv, d_gain, chan,
        edge, smem=(0,),
        scratch=[pltpu.VMEM((D, 384), bf16)], name="grad",
    )
    slab_taken = around(slab_give, "head_1", 1)
    pieces = call(
        pair_kernel, [((176, D), bf16)] * 4, where, keep, taken, edge, slab_keep, slab_taken,
        out_keep, out_taken, smem=(0,), scratch=[pltpu.VMEM((T, D), f32), pltpu.VMEM((384, 384), f32)], name="pair",
    )
    parts = [pieces[0]] + [around(pieces[by], "head_0", by) for by in (1, 2, 3)]
    (grads,) = call(merge_kernel, [((D, NW), bf16)], *parts, grads, name="merge")
    grads = exchange(grads.reshape(N_SEQ, 48, NW), SEQ)
    (own,) = call(
        four_kernel, [((T // N_HEAD, 2 * D), bf16)], where, *parts, hidden_in,
        smem=(0,), name="four",
    )
    near = [own] + [around(own, "head_0", by) for by in (1, 2, 3)]
    far = [around(a, "head_1", 1) for a in near]
    input_grad, block_out = call(
        input_kernel, [((T, D), f32), ((T, D), bf16)], where, *near, *far, hidden_in, cotangent, row,
        smem=(0,), name="input",
    )

    proj, step, out = (3, 48, 128), (3, 48), (3, 48, 64)
    shapes = [proj] * 3 + [step] * 3 + [out] * 3 + [(6, 3, 64)] * 3 + [(3, 3)] * 3
    shapes += [(6, 256)] * 3 + [(1, 6)] * 3 + [(2, 5)] * 3
    updated = call(
        update_kernel, [(s, f32) for s in shapes],
        grads, *matrices, *steps, *out_weights, channel_params, channel_first,
        channel_second, head_params, head_first, head_second, shared_weight, shared_first,
        shared_second, *gains_in, shared_conv, conv_first, conv_second,
        scratch=[pltpu.VMEM((6, 256), f32), pltpu.VMEM((2, 128), f32)],
        params=WIDE, name="update",
    )
    return (
        block_out, input_grad,
        *(jnp.transpose(a, (1, 0, 2)) for a in updated[0:3]),
        *(a.T for a in updated[3:6]),
        *(jnp.transpose(a, (0, 2, 1)) for a in updated[6:9]),
        *updated[15:18],
        *(g.reshape(6) for g in updated[18:21]),
        *updated[9:15],
        *updated[21:24],
    )


def solution(mesh):
    finer = Mesh(mesh.devices.reshape(4, 4, 4, 2), SEQ_HEAD)
    matrix = P(SEQ, HEAD, None)
    step = P(SEQ, HEAD)
    out = P(HEAD, None, SEQ)
    both = P(SEQ_HEAD, None)
    gain = P(SEQ_HEAD)
    channel = P(None, HEAD, None)
    head = P(None, HEAD)
    tokens = P(SEQ, None)
    return jax.shard_map(
        body,
        mesh=finer,
        in_specs=(
            tokens, tokens, P(SEQ), matrix, step, out, both, gain, channel, head, both,
            matrix, matrix, step, step, out, out, both, both, gain, gain, channel, channel,
            head, head, both, both,
        ),
        out_specs=(
            (tokens, tokens)
            + (matrix,) * 3 + (step,) * 3 + (out,) * 3 + (both,) * 3 + (gain,) * 3
            + (channel,) * 3 + (head,) * 3 + (both,) * 3
        ),
        check_vma=False,
    )
```
